32 devices in a mesh: dp: 8 (over z, x), tensor: 4 (over y, core).
Axes of the slice: x: 2, y: 2, z: 4, core: 2. Of those that a mesh axis runs over, the one named last changes fastest.
Arguments:
- query_input: bfloat16 [12288, 768], P(('dp', 'tensor')), may hold values from -6 to 6
- key_input: bfloat16 [12288, 768], P(('dp', 'tensor')), may hold values from -6 to 6
- query_length: int32 [48], P('dp'), may hold values from 128 to 256, as said below
- key_length: int32 [48], P('dp'), may hold values from 128 to 256, as said below
- pair_count: int32 [8], P('dp'), may hold values from 1 to 6, as said below
- query_qkv: bfloat16 [2, 768, 3, 768], P(None, None, None, 'tensor'), may hold values from -0.21875 to 0.21875
- query_qv_bias: float32 [2, 2, 768], P(None, None, 'tensor'), may hold values from -1.8 to 1.8
- query_out: bfloat16 [2, 768, 768], P(None, 'tensor'), may hold values from -1.5 to 1.5
- query_in: bfloat16 [2, 768, 3072], P(None, None, 'tensor'), may hold values from -0.21875 to 0.21875
- query_in_bias: float32 [2, 3072], P(None, 'tensor'), may hold values from -1.8 to 1.8
- query_down: bfloat16 [2, 3072, 768], P(None, 'tensor'), may hold values from -0.109375 to 0.109375
- query_gain: float32 [2, 2, 768], replicated, may hold values from 0.5 to 1.5
- query_shift: float32 [2, 4, 768], replicated, may hold values from -0.6 to 0.6
- key_qkv: bfloat16 [2, 768, 3, 768], P(None, None, None, 'tensor'), may hold values from -0.21875 to 0.21875
- key_qv_bias: float32 [2, 2, 768], P(None, None, 'tensor'), may hold values from -1.8 to 1.8
- key_out: bfloat16 [2, 768, 768], P(None, 'tensor'), may hold values from -1.5 to 1.5
- key_in: bfloat16 [2, 768, 3072], P(None, None, 'tensor'), may hold values from -0.21875 to 0.21875
- key_in_bias: float32 [2, 3072], P(None, 'tensor'), may hold values from -1.8 to 1.8
- key_down: bfloat16 [2, 3072, 768], P(None, 'tensor'), may hold values from -0.109375 to 0.109375
- key_gain: float32 [2, 2, 768], replicated, may hold values from 0.5 to 1.5
- key_shift: float32 [2, 4, 768], replicated, may hold values from -0.6 to 0.6
Outputs:
- per_pair: float32 [48], P('dp')
- query_grad: float32 [12288, 768], P(('dp', 'tensor'))
- grad_qkv: float32 [2, 768, 3, 768], P(None, 'dp', None, 'tensor')
- grad_out: float32 [2, 768, 768], P(None, 'tensor', 'dp')
- grad_in: float32 [2, 768, 3072], P(None, 'dp', 'tensor')
- grad_down: float32 [2, 3072, 768], P(None, 'tensor', 'dp')
- grad_qv_bias: float32 [2, 2, 768], replicated
- grad_in_bias: float32 [2, 3072], replicated
- grad_gain: float32 [2, 2, 768], replicated
- grad_shift: float32 [2, 4, 768], replicated
The draws below stay inside these ranges and needn't reach their ends.
Inputs may be any that keep to these rules, and one draw needn't show every extreme that they name: `query_length`: unpadded tokens of each query crop; some crop of every draw has all 256. `key_length`: unpadded tokens of each key crop; some crop of every draw has all 256. `pair_count`: live pairs of an index of dp; some index has all 6 live.
All inputs are finite; a program needn't handle non-finite values.
Results may differ from the reference program's by a relative error of at most 0.019.
Values may be sent and summed in bfloat16 or wider, within the bound.
A program may use at most 192 MiB of HBM per device.

```python
import math
import jax
import jax.numpy as jnp
from jax import lax

D = 768
HEADS = 12
FF = 3072
SEQ = 256
LAYERS = 2
SLOTS = 6
PAIRS = 48
GROUPS = 8


def crop_lengths(key, salt):
    stream = jax.random.fold_in(key, salt)
    drawn = jax.random.randint(stream, (PAIRS,), SEQ // 2, SEQ + 1)
    full_slot = jax.random.randint(jax.random.fold_in(stream, 5), (), 0, PAIRS)
    return jnp.where(jnp.arange(PAIRS) == full_slot, SEQ, drawn).astype(jnp.int32)


def draw_query_length(key, part):
    return crop_lengths(key, 11)


def draw_key_length(key, part):
    return crop_lengths(key, 13)


def draw_pair_count(key, part):
    stream = jax.random.fold_in(key, 17)
    drawn = jax.random.randint(stream, (GROUPS,), 1, SLOTS + 1)
    full_group = jax.random.randint(jax.random.fold_in(stream, 5), (), 0, GROUPS)
    return jnp.where(jnp.arange(GROUPS) == full_group, SLOTS, drawn).astype(jnp.int32)


def block_levels(rng, shape, pieces, least, top_value):
    def one(axis_at, blocks):
        draws = jax.random.uniform(jax.random.fold_in(jax.random.fold_in(rng, 6), axis_at), (blocks,), jnp.float32, least / len(pieces), top_value / len(pieces))
        return jnp.repeat(jnp.exp(draws), shape[axis_at] // blocks).reshape((-1,) + (1,) * (len(shape) - axis_at - 1))

    level = one(*pieces[0])
    for cut in pieces[1:]:
        level = level * one(*cut)
    return level


def normal_values(stream_key, dims, deviation, limit, shards=(), kind=jnp.bfloat16):
    values = jax.random.normal(stream_key, dims, jnp.float32) * deviation
    if len(shards) > 0:
        values = block_levels(stream_key, dims, shards, -0.22, 0.18) * values
    return jnp.clip(values, min=-limit, max=limit).astype(kind)


def setup_inputs(seed: int = 0) -> dict:
    key_of = jax.random.split(jax.random.key(seed), 22)
    query_input = normal_values(key_of[0], (PAIRS * SEQ, D), 1.0, 6.0, ((0, 32),))
    key_input = normal_values(key_of[1], (PAIRS * SEQ, D), 1.0, 6.0, ((0, 32),))
    query_length = draw_query_length(jax.random.fold_in(key_of[21], 71), 0)
    key_length = draw_key_length(jax.random.fold_in(key_of[21], 71), 0)
    pair_count = draw_pair_count(jax.random.fold_in(key_of[21], 71), 0)
    query_qkv = normal_values(key_of[5], (LAYERS, D, 3, D), D ** -0.5, 0.21875, ((3, 4),))
    query_qv_bias = normal_values(key_of[6], (LAYERS, 2, D), 0.3, 1.8, ((2, 4),), jnp.float32)
    query_out = normal_values(key_of[7], (LAYERS, D, D), (D // 48) ** -0.5, 1.5, ((1, 4),))
    query_in = normal_values(key_of[8], (LAYERS, D, FF), D ** -0.5, 0.21875, ((2, 4),))
    query_in_bias = normal_values(key_of[9], (LAYERS, FF), 0.3, 1.8, ((1, 4),), jnp.float32)
    query_down = normal_values(key_of[10], (LAYERS, FF, D), FF ** -0.5, 0.109375, ((1, 4),))
    query_gain = jnp.clip(1.0 + 0.1 * jax.random.normal(key_of[11], (LAYERS, 2, D), jnp.float32), 0.5, 1.5)
    query_shift = normal_values(key_of[12], (LAYERS, 4, D), 0.1, 0.6, (), jnp.float32)
    key_qkv = normal_values(key_of[13], (LAYERS, D, 3, D), D ** -0.5, 0.21875, ((3, 4),))
    key_qv_bias = normal_values(key_of[14], (LAYERS, 2, D), 0.3, 1.8, ((2, 4),), jnp.float32)
    key_out = normal_values(key_of[15], (LAYERS, D, D), (D // 48) ** -0.5, 1.5, ((1, 4),))
    key_in = normal_values(key_of[16], (LAYERS, D, FF), D ** -0.5, 0.21875, ((2, 4),))
    key_in_bias = normal_values(key_of[17], (LAYERS, FF), 0.3, 1.8, ((1, 4),), jnp.float32)
    key_down = normal_values(key_of[18], (LAYERS, FF, D), FF ** -0.5, 0.109375, ((1, 4),))
    key_gain = jnp.clip(1.0 + 0.1 * jax.random.normal(key_of[19], (LAYERS, 2, D), jnp.float32), 0.5, 1.5)
    key_shift = normal_values(key_of[20], (LAYERS, 4, D), 0.1, 0.6, (), jnp.float32)
    return {"query_input": query_input, "key_input": key_input, "query_length": query_length, "key_length": key_length, "pair_count": pair_count, "query_qkv": query_qkv, "query_qv_bias": query_qv_bias, "query_out": query_out, "query_in": query_in, "query_in_bias": query_in_bias, "query_down": query_down, "query_gain": query_gain, "query_shift": query_shift, "key_qkv": key_qkv, "key_qv_bias": key_qv_bias, "key_out": key_out, "key_in": key_in, "key_in_bias": key_in_bias, "key_down": key_down, "key_gain": key_gain, "key_shift": key_shift}


@jax.custom_vjp
def low(v):
    return lax.optimization_barrier(v.astype(jnp.bfloat16)).astype(jnp.float32)

@jax.custom_vjp
def low_back(v):
    return v

def low_keep(v):
    return (low(v), None)

def low_pass(kept, grad):
    return (grad,)

def back_keep(v):
    return (v, None)

def back_low(kept, grad):
    return (low(grad),)
low.defvjp(low_keep, low_pass)
low_back.defvjp(back_keep, back_low)
norm_eps = 1e-06
temper = 0.05

def matmul_high(left, right):
    return jnp.dot(left, right, precision=lax.Precision.HIGHEST, preferred_element_type=jnp.float32)

def layer_norm(values, gain, shift):
    center = values - lax.optimization_barrier(jnp.mean(values, axis=-1, keepdims=True))
    spread = lax.optimization_barrier(jnp.mean(center * center, axis=-1, keepdims=True))
    return center * lax.rsqrt(spread + norm_eps) * gain + shift

def encode(params, inputs, lengths):
    qkv_w, qv_bias, out_w, in_w, in_bias, down_w, gains, shifts = params
    group = inputs.shape[0]
    head_dim = D // HEADS
    scale = head_dim ** (-0.5)
    position = jnp.arange(SEQ, dtype=jnp.int32)
    visible = position[None, :] < lengths[:, None]
    state = inputs.reshape(group * SEQ, D)
    for layer in range(LAYERS):
        hidden = low(state)
        bias = jnp.stack([qv_bias[layer, 0], jnp.zeros_like(qv_bias[layer, 0]), qv_bias[layer, 1]])
        projected = matmul_high(hidden, qkv_w[layer].reshape(D, 3 * D)).reshape(group * SEQ, 3, D) + bias
        projected = low(low_back(projected)).reshape(group, SEQ, 3, HEADS, head_dim)
        queries = projected[:, :, 0]
        keys_part = projected[:, :, 1]
        values = projected[:, :, 2]
        scores = jnp.einsum('gqhe,gkhe->ghqk', queries, keys_part, precision=lax.Precision.HIGHEST) * scale
        scores = low_back(scores)
        scores = jnp.where(visible[:, None, None, :], scores, -1e+30)
        probs = low(jax.nn.softmax(scores, axis=-1))
        mixed = jnp.einsum('ghqk,gkhe->gqhe', probs, values, precision=lax.Precision.HIGHEST).reshape(group * SEQ, D)
        mixed = low(low_back(mixed))
        attended = low_back(matmul_high(mixed, out_w[layer]))
        resid = state + attended + shifts[layer, 0]
        normed = layer_norm(resid, gains[layer, 0], shifts[layer, 1])
        inner = low_back(matmul_high(low(normed), in_w[layer]) + in_bias[layer])
        active = low(jax.nn.gelu(inner, approximate=False))
        reduced = low_back(matmul_high(active, down_w[layer]))
        state = layer_norm(normed + reduced + shifts[layer, 2], gains[layer, 1], shifts[layer, 3])
    pool_weight = visible.astype(jnp.float32) / lengths[:, None].astype(jnp.float32)
    pooled = jnp.einsum('gs,gsd->gd', pool_weight, state.reshape(group, SEQ, D), precision=lax.Precision.HIGHEST)
    return pooled * lax.rsqrt(lax.optimization_barrier(jnp.sum(pooled * pooled, axis=1, keepdims=True)) + norm_eps)

def pool_all(params, inputs, lengths):
    group = math.gcd(PAIRS, 16)
    blocks = PAIRS // group
    packed = inputs.reshape(blocks, group, SEQ, D)
    packed_len = lengths.reshape(blocks, group)
    runner = jax.checkpoint(lambda pack: encode(params, pack[0], pack[1]))
    return lax.map(runner, (packed, packed_len)).reshape(PAIRS, D)

def reference(query_input, key_input, query_length, key_length, pair_count, query_qkv, query_qv_bias, query_out, query_in, query_in_bias, query_down, query_gain, query_shift, key_qkv, key_qv_bias, key_out, key_in, key_in_bias, key_down, key_gain, key_shift):
    query_params = tuple((a.astype(jnp.float32) for a in (query_qkv, query_qv_bias, query_out, query_in, query_in_bias, query_down, query_gain, query_shift)))
    key_params = tuple((a.astype(jnp.float32) for a in (key_qkv, key_qv_bias, key_out, key_in, key_in_bias, key_down, key_gain, key_shift)))
    unit_key = pool_all(key_params, key_input.astype(jnp.float32).reshape(PAIRS, SEQ, D), key_length)
    slot = jnp.arange(PAIRS, dtype=jnp.int32)
    live_slot = slot % SLOTS < pair_count[slot // SLOTS]
    live_float = live_slot.astype(jnp.float32)

    def objective(params, inputs):
        unit_query = pool_all(params, inputs.reshape(PAIRS, SEQ, D), query_length)
        logits = matmul_high(unit_query, unit_key.T) / temper
        logits = jnp.where(live_slot[None, :], logits, -1e+30)
        highest = lax.optimization_barrier(jnp.max(logits, axis=1, keepdims=True))
        log_total = highest[:, 0] + jnp.log(lax.optimization_barrier(jnp.sum(jnp.exp(logits - highest), axis=1)))
        own_logit = lax.optimization_barrier(jnp.sum(unit_query * unit_key, axis=1)) / temper
        per_pair = (log_total - own_logit) * live_float
        return (SEQ * jnp.sum(per_pair), per_pair)
    scaled, backward, per_pair = jax.vjp(objective, query_params, query_input.astype(jnp.float32), has_aux=True)
    grad_params, grad_input = backward(jnp.ones_like(scaled))
    return (per_pair, grad_input.reshape(PAIRS * SEQ, D), grad_params[0], grad_params[2], grad_params[3], grad_params[5], grad_params[1], grad_params[4], grad_params[6], grad_params[7])
```

```python
import functools
import math

import jax
import jax.numpy as jnp
from jax import lax
from jax.experimental import pallas as pl
from jax.experimental.pallas import tpu as pltpu
from jax.sharding import PartitionSpec as P

D = 768
HEAD = 64
SEQ = 256
LAYERS = 2
BLOB = 768
EPS = 1e-06
TEMPER = 0.05
FILL = -1e30
BF = jnp.bfloat16
F32 = jnp.float32
MESH = pl.DeviceIdType.MESH
SCALE = HEAD ** (-0.5)
MIB = 2**20


def mm(a, b):
    return jnp.dot(a, b, preferred_element_type=F32)


def mm_nt(a, b):
    return lax.dot_general(a, b, (((1,), (1,)), ((), ())), preferred_element_type=F32)


def mm_tn(a, b):
    return lax.dot_general(a, b, (((0,), (0,)), ((), ())), preferred_element_type=F32)


def norm(v, gain, shift):
    center = v - jnp.mean(v, axis=-1, keepdims=True)
    rate = lax.rsqrt(jnp.mean(center * center, axis=-1, keepdims=True) + EPS)
    xhat = center * rate
    return xhat, rate, xhat * gain + shift


def norm_back(g, xhat, rate, gain):
    gx = g * gain
    return rate * (
        gx
        - jnp.mean(gx, axis=-1, keepdims=True)
        - xhat * jnp.mean(gx * xhat, axis=-1, keepdims=True)
    )


def rows(v):
    return jnp.sum(v, axis=0, keepdims=True)


def assemble(dst, pieces, q):
    n = pieces[0].shape[0]
    for k in range(3):
        dst[pl.ds(pl.multiple_of((q ^ k) * n, 16), n), :] = pieces[k][...]
    last = pl.multiple_of((q ^ 3) * n, 16)
    dst[pl.ds(last, n // 2), :] = pieces[3][...]
    dst[pl.ds(pl.multiple_of(last + n // 2, 16), n // 2), :] = pieces[4][...]


def attn_forward(first, save, meta, *refs):
    refs = list(refs)
    if first:
        x_in = refs.pop(0)
    else:
        base, mine, theirs, gain_prev, shift_prev = [refs.pop(0) for _ in range(5)]
    own = refs.pop(0)
    pieces = [refs.pop(0) for _ in range(5)]
    bias, shift = [refs.pop(0) for _ in range(2)]
    base_out, part_out = [refs.pop(0) for _ in range(2)]
    if save:
        hidden_out, proj_out, probs_out, mixed_out = [refs.pop(0) for _ in range(4)]
        if not first:
            xhat_out, rate_out = [refs.pop(0) for _ in range(2)]
    far = refs.pop(0)
    crop = pl.program_id(0)

    @pl.when(crop == 0)
    def _():
        assemble(far, pieces, meta[0])

    if first:
        low = x_in[...]
        x = low.astype(F32)
    else:
        v = base[...] + (mine[...].astype(F32) + theirs[...].astype(F32))
        xhat, rate, x = norm(v, gain_prev[1:2, :], shift_prev[3:4, :])
        low = x.astype(BF)
        if save:
            xhat_out[...] = xhat
            rate_out[...] = rate
    width = bias.shape[1] // 3
    heads = width // HEAD
    visible = lax.broadcasted_iota(jnp.int32, (1, SEQ), 1) < meta[1 + crop]
    total = None
    for s, w in enumerate((own, far)):
        proj = (mm_nt(low, w[: 3 * width, :]) + bias[s : s + 1, :]).astype(BF)
        mixed = []
        for h in range(heads):
            queries = proj[:, h * HEAD : (h + 1) * HEAD]
            keys = proj[:, width + h * HEAD : width + (h + 1) * HEAD]
            values = proj[:, 2 * width + h * HEAD : 2 * width + (h + 1) * HEAD]
            scores = jnp.where(visible, mm_nt(queries, keys) * SCALE, FILL)
            e = jnp.exp(scores - jnp.max(scores, axis=1, keepdims=True))
            probs = (e * (1.0 / jnp.sum(e, axis=1, keepdims=True))).astype(BF)
            if save:
                probs_out[s, 0, h] = probs
            mixed.append(mm(probs, values).astype(BF))
        mixed = jnp.concatenate(mixed, axis=1)
        if save:
            proj_out[s] = proj
            mixed_out[s] = mixed
        term = mm(mixed, w[3 * width : 4 * width, :])
        total = term if total is None else total + term
    if save:
        hidden_out[...] = low
    base_out[...] = x + shift[0:1, :]
    part_out[...] = total.astype(BF)


def ffn_forward(save, meta, *refs):
    refs = list(refs)
    base, mine, theirs, own_in, own_down = [refs.pop(0) for _ in range(5)]
    pieces_in = [refs.pop(0) for _ in range(5)]
    pieces_down = [refs.pop(0) for _ in range(5)]
    bias, gain, shift = [refs.pop(0) for _ in range(3)]
    base_out, part_out = [refs.pop(0) for _ in range(2)]
    if save:
        xhat_out, rate_out, normed_out, active_out, slope_out = [refs.pop(0) for _ in range(5)]
    far_in, far_down = refs

    @pl.when(pl.program_id(0) == 0)
    def _():
        assemble(far_in, pieces_in, meta[0])
        assemble(far_down, pieces_down, meta[0])

    v = base[...] + (mine[...].astype(F32) + theirs[...].astype(F32))
    xhat, rate, normed = norm(v, gain[0:1, :], shift[1:2, :])
    low = normed.astype(BF)
    if save:
        xhat_out[...] = xhat
        rate_out[...] = rate
        normed_out[...] = low
    total = None
    for s, (w_in, w_down) in enumerate(((own_in, own_down), (far_in, far_down))):
        u = mm(low, w_in[...]) + bias[s : s + 1, :]
        share = 0.5 + 0.5 * lax.erf(u * (0.5**0.5))
        active = (u * share).astype(BF)
        if save:
            active_out[s] = active
            slope_out[s] = (share + u * (jnp.exp(-0.5 * u * u) * ((2 * math.pi) ** -0.5))).astype(BF)
        term = mm(active, w_down[...])
        total = term if total is None else total + term
    base_out[...] = normed + shift[2:3, :]
    part_out[...] = total.astype(BF)


def pool_forward(save, meta, base, mine, theirs, gain, shift, sums_out, *saved):
    crop = pl.program_id(0)
    v = base[...] + (mine[...].astype(F32) + theirs[...].astype(F32))
    xhat, rate, x = norm(v, gain[1:2, :], shift[3:4, :])
    if save:
        saved[0][...] = xhat
        saved[1][...] = rate
    visible = lax.broadcasted_iota(jnp.int32, (SEQ, 1), 0) < meta[1 + crop]
    sums_out[0] = rows(jnp.where(visible, x, 0.0))


def flips(dp_size, with_core):
    d = lax.axis_index("dp")
    t = lax.axis_index("tensor")
    found = [(d, t ^ 2)]
    for b in range(dp_size.bit_length() - 1):
        found.append((d ^ (1 << b), t))
    if with_core:
        found.append((d, t ^ 1))
    return found


def greet(partners):
    barrier = pltpu.get_barrier_semaphore()
    for p in partners:
        pl.semaphore_signal(barrier, inc=1, device_id=p, device_id_type=MESH)
    pl.semaphore_wait(barrier, len(partners))


def contrast(dp_size, nc, count, inv_q, inv_k, sums_q, sums_k, pair_out, grad_out, held, send, recv):
    wide = D + 128
    d = lax.axis_index("dp")
    half = lax.axis_index("tensor") // 2
    me = d * 2 + half
    partners = flips(dp_size, False)
    greet(partners)

    def unit(s, inv):
        pooled = s * inv
        r = lax.rsqrt(jnp.sum(pooled * pooled, axis=1, keepdims=True) + EPS)
        return pooled * r, r

    unit_q, rate_q = unit(sums_q[...], inv_q[...])
    unit_k, _ = unit(sums_k[...], inv_k[...])
    held[me] = jnp.zeros((8, wide), F32)
    held[me, 0:nc, 0:D] = unit_k
    held[me, nc : 2 * nc, 0:D] = unit_q
    slot = half * nc + lax.broadcasted_iota(jnp.int32, (nc, 128), 0)
    lane = lax.broadcasted_iota(jnp.int32, (nc, 128), 1)
    held[me, 0:nc, D:wide] = jnp.where((slot < count[0]) & (lane == 0), 1.0, 0.0)
    for s, p in enumerate(partners):
        block = pl.ds(((me >> s) << s), 1 << s)
        copy = pltpu.make_async_remote_copy(
            src_ref=held.at[block],
            dst_ref=held.at[block],
            send_sem=send.at[s],
            recv_sem=recv.at[s],
            device_id=p,
            device_id_type=MESH,
        )
        copy.start()
        copy.wait()
    chips = held.shape[0]
    every = held[...].reshape(chips * 8, wide)
    keys = every[:, 0:D]
    here = held[pl.ds(2 * d, 2)].reshape(16, wide)[:, 0:D]

    def exact(a, b, dims):
        return lax.dot_general(
            a, b, (dims, ((), ())), precision=lax.Precision.HIGHEST, preferred_element_type=F32
        )

    one = jnp.where(lax.broadcasted_iota(jnp.int32, (16, 128), 1) == 0, 1.0, 0.0)
    live = exact(one, every[:, D:wide], ((1,), (1,))) > 0.5
    logits = exact(here, keys, ((1,), (1,))) / TEMPER
    masked = jnp.where(live, logits, FILL)
    highest = jnp.max(masked, axis=1, keepdims=True)
    e = jnp.exp(masked - highest)
    total = jnp.sum(e, axis=1, keepdims=True)
    row = lax.broadcasted_iota(jnp.int32, (16, 1), 0)
    chip = row // 8
    place = row % 8 - nc
    column = lax.broadcasted_iota(jnp.int32, (16, chips * 8), 1)
    own = column == (2 * d + chip) * 8 + place
    mine = (place >= 0) & (place < nc) & (chip * nc + place < count[0])
    own_logit = jnp.sum(jnp.where(own, logits, 0.0), axis=1, keepdims=True)
    pair_out[...] = jnp.broadcast_to(
        jnp.where(mine, highest + jnp.log(total) - own_logit, 0.0), (16, 128)
    )
    weighting = jnp.where(mine, e / total - own.astype(F32), 0.0) * (SEQ / TEMPER)
    g_unit = exact(weighting, keys, ((1,), (0,)))
    mine_first = half == 0
    g_unit = jnp.where(mine_first, g_unit[nc : 2 * nc], g_unit[8 + nc : 8 + 2 * nc])
    g_pooled = rate_q * (g_unit - unit_q * jnp.sum(unit_q * g_unit, axis=1, keepdims=True))
    grad_out[...] = g_pooled * inv_q[...]


def total_over(dp_size, v_ref, out_ref, held, got, send, recv):
    partners = flips(dp_size, True)
    greet(partners)
    held[0] = v_ref[...]
    for s, p in enumerate(partners):
        copy = pltpu.make_async_remote_copy(
            src_ref=held.at[s],
            dst_ref=got.at[s],
            send_sem=send.at[s],
            recv_sem=recv.at[s],
            device_id=p,
            device_id_type=MESH,
        )
        copy.start()
        copy.wait()
        held[s + 1] = held[s] + got[s]
    out_ref[...] = held[len(partners)]


def ffn_backward(top, meta, *refs):
    refs = list(refs)
    if top:
        g_sum = refs.pop(0)
    else:
        base, theirs = [refs.pop(0) for _ in range(2)]
    xhat, rate, slope, own_in, own_down = [refs.pop(0) for _ in range(5)]
    pieces_in = [refs.pop(0) for _ in range(5)]
    pieces_down = [refs.pop(0) for _ in range(5)]
    gain = refs.pop(0)
    base_out, part_out, low_out, inner_out, vec_out, bias_out = [refs.pop(0) for _ in range(6)]
    far_in, far_down = refs
    crop = pl.program_id(0)

    @pl.when(crop == 0)
    def _():
        assemble(far_in, pieces_in, meta[0])
        assemble(far_down, pieces_down, meta[0])
        vec_out[...] = jnp.zeros_like(vec_out)
        bias_out[...] = jnp.zeros_like(bias_out)

    if top:
        visible = lax.broadcasted_iota(jnp.int32, (SEQ, 1), 0) < meta[1 + crop]
        g = jnp.where(visible, g_sum[0], 0.0)
    else:
        g = base[...] + theirs[...].astype(F32)
    xh = xhat[...]
    gc = norm_back(g, xh, rate[...], gain[1:2, :])
    vec_out[0:1, :] += rows(g * xh)
    vec_out[1:2, :] += rows(g)
    vec_out[2:3, :] += rows(gc)
    low = gc.astype(BF)
    low_out[...] = low
    total = gc
    part = None
    for s, (w_in, w_down) in enumerate(((own_in, own_down), (far_in, far_down))):
        inner = (mm_nt(low, w_down[...]) * slope[s].astype(F32)).astype(BF)
        inner_out[s] = inner
        bias_out[s : s + 1, :] += rows(inner.astype(F32))
        term = mm_nt(inner, w_in[...])
        part = term if part is None else part + term
    base_out[...] = total + part
    part_out[...] = part.astype(BF)


def attn_backward(meta, *refs):
    refs = list(refs)
    base, theirs, xhat, rate, proj, probs, own = [refs.pop(0) for _ in range(7)]
    pieces = [refs.pop(0) for _ in range(5)]
    gain = refs.pop(0)
    base_out, part_out, low_out, proj_out, vec_out, bias_out = [refs.pop(0) for _ in range(6)]
    far = refs.pop(0)
    crop = pl.program_id(0)

    @pl.when(crop == 0)
    def _():
        assemble(far, pieces, meta[0])
        vec_out[...] = jnp.zeros_like(vec_out)
        bias_out[...] = jnp.zeros_like(bias_out)

    g = base[...] + theirs[...].astype(F32)
    xh = xhat[...]
    gr = norm_back(g, xh, rate[...], gain[0:1, :])
    vec_out[0:1, :] += rows(g * xh)
    vec_out[1:2, :] += rows(g)
    vec_out[2:3, :] += rows(gr)
    low = gr.astype(BF)
    low_out[...] = low
    width = proj.shape[2] // 3
    heads = width // HEAD
    part = None
    for s, w in enumerate((own, far)):
        g_mixed = mm_nt(low, w[3 * width : 4 * width, :]).astype(BF)
        pr = proj[s]
        parts = [[], [], []]
        for h in range(heads):
            queries = pr[:, h * HEAD : (h + 1) * HEAD]
            keys = pr[:, width + h * HEAD : width + (h + 1) * HEAD]
            values = pr[:, 2 * width + h * HEAD : 2 * width + (h + 1) * HEAD]
            gm = g_mixed[:, h * HEAD : (h + 1) * HEAD]
            p_low = probs[s, 0, h]
            p = p_low.astype(F32)
            gp = mm_nt(gm, values)
            gs = (p * (gp - jnp.sum(p * gp, axis=1, keepdims=True))).astype(BF)
            parts[0].append((mm(gs, keys) * SCALE).astype(BF))
            parts[1].append((mm_tn(gs, queries) * SCALE).astype(BF))
            parts[2].append(mm_tn(p_low, gm).astype(BF))
        g_proj = jnp.concatenate(parts[0] + parts[1] + parts[2], axis=1)
        proj_out[s] = g_proj
        bias_out[s : s + 1, :] += rows(g_proj.astype(F32))
        term = mm(g_proj, w[: 3 * width, :])
        part = term if part is None else part + term
    base_out[...] = gr + part
    part_out[...] = part.astype(BF)


def ffn_weights(low, active, normed, inner, in_out, down_out):
    down_out[0] = mm_tn(low[...], active[0])
    in_out[0] = mm_tn(normed[...], inner[0])


def attn_weights(low, mixed, hidden, g_proj, out):
    width = mixed.shape[2]
    out[0, :, 0 : 3 * width] = mm_tn(hidden[...], g_proj[0])
    out[0, :, 3 * width : 4 * width] = mm_tn(low[...], mixed[0])


SMEM = pl.BlockSpec(memory_space=pltpu.SMEM)


def row_block(width):
    return pl.BlockSpec((SEQ, width), lambda i: (i, 0))


def shard_block(width):
    return pl.BlockSpec((2, SEQ, width), lambda i: (0, i, 0))


def whole_block(shape):
    return pl.BlockSpec(shape, lambda i: (0,) * len(shape))


def call(body, grid, ins, outs, scratch, flops, name):
    arrays = [a for a, _ in ins]
    size = sum(a.size * a.dtype.itemsize for a in arrays)
    size += sum(math.prod(s) * jnp.dtype(t).itemsize for s, t, _ in outs)
    return pl.pallas_call(
        body,
        grid=grid,
        in_specs=[s for _, s in ins],
        out_specs=[s for _, _, s in outs],
        out_shape=[jax.ShapeDtypeStruct(s, t) for s, t, _ in outs],
        scratch_shapes=scratch,
        compiler_params=pltpu.CompilerParams(vmem_limit_bytes=52 * MIB),
        cost_estimate=pl.CostEstimate(flops=int(flops), bytes_accessed=int(size), transcendentals=0),
        name=name,
    )(*arrays)


def on_device(mesh_shape, *args):
    (
        query_input,
        key_input,
        query_length,
        key_length,
        pair_count,
    ) = args[:5]
    encoders = (args[5:13], args[13:21])
    dp_size = mesh_shape["dp"]
    dp_bits = dp_size.bit_length() - 1
    d_pos = lax.axis_index("dp")
    t_pos = lax.axis_index("tensor")
    quarter = d_pos & 3
    core = t_pos & 1
    half = t_pos // 2
    share = query_input.shape[0]
    total_rows = 2 * share
    nc = total_rows // SEQ
    width = args[5].shape[3]

    def far_perm(x):
        return lax.ppermute(x, "tensor", [(i, i ^ 2) for i in range(4)])

    def core_perm(x):
        return lax.ppermute(x, "tensor", [(i, i ^ 1) for i in range(4)])

    def dp_perm(x, bit):
        return lax.ppermute(x, "dp", [(i, i ^ (1 << bit)) for i in range(dp_size)])

    def fetch(blob):
        n = blob.shape[0] // 4
        r0 = far_perm(lax.dynamic_slice(blob, (quarter * n, 0), (n, blob.shape[1])))
        r1 = dp_perm(r0, 0)
        r2 = dp_perm(r0, 1)
        r3 = dp_perm(r2[: n // 2], 0)
        r4 = dp_perm(r1[n // 2 :], 1)
        return (r0, r1, r2, r3, r4)

    def chip_rows(x):
        other = core_perm(x)
        return jnp.where(core == 0, jnp.concatenate([x, other]), jnp.concatenate([other, x]))

    small = jnp.stack(
        [jnp.concatenate([w[1].reshape(-1), w[4].reshape(-1)]) for w in encoders]
    )
    small_far = far_perm(small)
    own = [[None] * LAYERS for _ in range(2)]
    far = [[None] * LAYERS for _ in range(2)]
    qkv_bias = [[None] * LAYERS for _ in range(2)]
    in_bias = [[None] * LAYERS for _ in range(2)]
    for layer in range(LAYERS):
        for e, w in enumerate(encoders):
            attn = jnp.concatenate(
                [w[0][layer].transpose(1, 2, 0).reshape(3 * width, D), w[2][layer]], axis=0
            )
            own[e][layer] = (attn, w[3][layer], w[5][layer])
            far[e][layer] = tuple(fetch(b) for b in own[e][layer])
            pair = []
            inner_rows = []
            for v in (small, small_far):
                qv = v[e, : LAYERS * 2 * width].reshape(LAYERS, 2, width)[layer]
                pair.append(jnp.concatenate([qv[0], jnp.zeros((width,), F32), qv[1]]))
                inner_rows.append(v[e, LAYERS * 2 * width :].reshape(LAYERS, -1)[layer])
            qkv_bias[e][layer] = jnp.stack(pair)
            in_bias[e][layer] = jnp.stack(inner_rows)

    lengths = [
        lax.dynamic_slice(v, (half * nc,), (nc,)) for v in (query_length, key_length)
    ]
    metas = [jnp.concatenate([quarter[None], v]).astype(jnp.int32) for v in lengths]
    grid = (nc,)
    wspec = whole_block((BLOB, D))
    pspecs = [whole_block((BLOB // 4, D))] * 3 + [whole_block((BLOB // 8, D))] * 2
    gspec = whole_block((2, D))
    sspec = whole_block((4, D))
    flat = row_block(D)
    blob_scratch = pltpu.VMEM((BLOB, D), BF)
    big = (total_rows, D)
    unit_flops = 2 * total_rows * D

    def weight_ins(e, layer, which):
        return [(own[e][layer][which], wspec)]

    def piece_ins(e, layer, which):
        return list(zip(far[e][layer][which], pspecs))

    state = [None, None]
    kept = [dict() for _ in range(LAYERS)]
    x_in = [chip_rows(query_input), chip_rows(key_input)]
    for layer in range(LAYERS):
        for e in range(2):
            save = e == 0
            gains, shifts = encoders[e][6], encoders[e][7]
            ins = [(metas[e], SMEM)]
            if layer == 0:
                ins += [(x_in[e], flat)]
            else:
                ins += [(a, flat) for a in state[e]]
                ins += [(gains[layer - 1], gspec), (shifts[layer - 1], sspec)]
            ins += weight_ins(e, layer, 0) + piece_ins(e, layer, 0)
            ins += [(qkv_bias[e][layer], whole_block((2, 3 * width))), (shifts[layer], sspec)]
            outs = [(big, F32, flat), (big, BF, flat)]
            if save:
                heads = width // HEAD
                outs += [
                    (big, BF, flat),
                    ((2, total_rows, 3 * width), BF, shard_block(3 * width)),
                    (
                        (2, nc, heads, SEQ, SEQ),
                        BF,
                        pl.BlockSpec((2, 1, heads, SEQ, SEQ), lambda i: (0, i, 0, 0, 0)),
                    ),
                    ((2, total_rows, width), BF, shard_block(width)),
                ]
                if layer > 0:
                    outs += [(big, F32, flat), ((total_rows, 1), F32, row_block(1))]
            got = call(
                functools.partial(attn_forward, layer == 0, save),
                grid,
                ins,
                outs,
                [blob_scratch],
                unit_flops * 10 * width,
                f"attn_forward_{e}_{layer}",
            )
            base, part = got[:2]
            if save:
                kept[layer].update(zip(("hidden", "proj", "probs", "mixed"), got[2:6]))
                if layer > 0:
                    kept[layer - 1].update(zip(("xhat2", "rate2"), got[6:8]))
            other = core_perm(part)
            ins = [(metas[e], SMEM), (base, flat), (part, flat), (other, flat)]
            ins += weight_ins(e, layer, 1) + weight_ins(e, layer, 2)
            ins += piece_ins(e, layer, 1) + piece_ins(e, layer, 2)
            ins += [(in_bias[e][layer], whole_block((2, BLOB))), (gains[layer], gspec), (shifts[layer], sspec)]
            outs = [(big, F32, flat), (big, BF, flat)]
            if save:
                outs += [
                    (big, F32, flat),
                    ((total_rows, 1), F32, row_block(1)),
                    (big, BF, flat),
                    ((2, total_rows, BLOB), BF, shard_block(BLOB)),
                    ((2, total_rows, BLOB), BF, shard_block(BLOB)),
                ]
            got = call(
                functools.partial(ffn_forward, save),
                grid,
                ins,
                outs,
                [blob_scratch, blob_scratch],
                unit_flops * 4 * BLOB,
                f"ffn_forward_{e}_{layer}",
            )
            if save:
                kept[layer].update(
                    zip(("xhat1", "rate1", "normed", "active", "slope"), got[2:7])
                )
            state[e] = (got[0], got[1], core_perm(got[1]))
    sums = []
    for e in range(2):
        save = e == 0
        gains, shifts = encoders[e][6], encoders[e][7]
        outs = [((nc, 1, D), F32, pl.BlockSpec((1, 1, D), lambda i: (i, 0, 0)))]
        if save:
            outs += [(big, F32, flat), ((total_rows, 1), F32, row_block(1))]
        got = call(
            functools.partial(pool_forward, save),
            grid,
            [(metas[e], SMEM)]
            + [(a, flat) for a in state[e]]
            + [(gains[LAYERS - 1], gspec), (shifts[LAYERS - 1], sspec)],
            outs,
            [],
            unit_flops,
            f"pool_forward_{e}",
        )
        sums.append(got[0].reshape(nc, D))
        if save:
            kept[LAYERS - 1].update(zip(("xhat2", "rate2"), got[1:3]))

    inverse = [(1.0 / v.astype(F32))[:, None] for v in lengths]
    vmem = pl.BlockSpec(memory_space=pltpu.VMEM)
    hops = dp_bits + 1
    pair_rows, g_sum = pl.pallas_call(
        functools.partial(contrast, dp_size, nc),
        in_specs=[SMEM] + [vmem] * 4,
        out_specs=[vmem] * 2,
        out_shape=[
            jax.ShapeDtypeStruct((16, 128), F32),
            jax.ShapeDtypeStruct((nc, D), F32),
        ],
        scratch_shapes=[
            pltpu.VMEM((2 * dp_size, 8, D + 128), F32),
            pltpu.SemaphoreType.DMA((hops,)),
            pltpu.SemaphoreType.DMA((hops,)),
        ],
        compiler_params=pltpu.CompilerParams(
            collective_id=0, has_side_effects=True, vmem_limit_bytes=40 * MIB
        ),
        name="contrast",
    )(pair_count, inverse[0], inverse[1], sums[0], sums[1])
    per_pair = jnp.concatenate([pair_rows[nc : 2 * nc, 0], pair_rows[8 + nc : 8 + 2 * nc, 0]])

    def scatter(full, order):
        cur = full.reshape((2,) + (2,) * dp_bits + (D // dp_size, BLOB))
        axes = ["y"] + list(reversed(range(dp_bits)))
        for name in order:
            at = axes.index(name)
            bit = jnp.int32(0) if name == "y" else (d_pos >> name) & 1
            keep = lax.dynamic_index_in_dim(cur, bit, at, keepdims=False)
            send = lax.dynamic_index_in_dim(cur, 1 - bit, at, keepdims=False)
            got = far_perm(send) if name == "y" else dp_perm(send, name)
            cur = keep + got
            axes.pop(at)
        return cur

    rest = list(range(2, dp_bits))
    order_in = ["y", 0, 1] + rest
    order_down = [0, "y", 1] + rest
    order_attn = [1, "y", 0] + rest

    vec_spec = whole_block((8, D))
    grad_in = [None] * LAYERS
    grad_down = [None] * LAYERS
    grad_attn = [None] * LAYERS
    vectors = [None] * LAYERS
    g_state = None
    for layer in reversed(range(LAYERS)):
        w = encoders[0]
        gains = w[6]
        k = kept[layer]
        top = layer == LAYERS - 1
        ins = [(metas[0], SMEM)]
        if top:
            ins += [(g_sum.reshape(nc, 1, D), pl.BlockSpec((1, 1, D), lambda i: (i, 0, 0)))]
        else:
            ins += [(a, flat) for a in g_state]
        ins += [(k["xhat2"], flat), (k["rate2"], row_block(1)), (k["slope"], shard_block(BLOB))]
        ins += weight_ins(0, layer, 1) + weight_ins(0, layer, 2)
        ins += piece_ins(0, layer, 1) + piece_ins(0, layer, 2)
        ins += [(gains[layer], gspec)]
        base, part, low, inner, vec_f, bias_f = call(
            functools.partial(ffn_backward, top),
            grid,
            ins,
            [
                (big, F32, flat),
                (big, BF, flat),
                (big, BF, flat),
                ((2, total_rows, BLOB), BF, shard_block(BLOB)),
                ((8, D), F32, vec_spec),
                ((8, BLOB), F32, whole_block((8, BLOB))),
            ],
            [blob_scratch, blob_scratch],
            unit_flops * 4 * BLOB,
            f"ffn_backward_{layer}",
        )
        other = core_perm(part)
        one_shard = pl.BlockSpec((1, total_rows, BLOB), lambda i: (i, 0, 0))
        full_out = pl.BlockSpec((1, D, BLOB), lambda i: (i, 0, 0))
        g_in, g_down = call(
            ffn_weights,
            (2,),
            [
                (low, whole_block(big)),
                (k["active"], one_shard),
                (k["normed"], whole_block(big)),
                (inner, one_shard),
            ],
            [((2, D, BLOB), F32, full_out), ((2, D, BLOB), F32, full_out)],
            [],
            unit_flops * 4 * BLOB,
            f"ffn_weights_{layer}",
        )
        grad_in[layer] = scatter(g_in, order_in)
        grad_down[layer] = scatter(g_down, order_down)
        ins = [(metas[0], SMEM), (base, flat), (other, flat)]
        ins += [(k["xhat1"], flat), (k["rate1"], row_block(1)), (k["proj"], shard_block(3 * width))]
        heads = width // HEAD
        ins += [(k["probs"], pl.BlockSpec((2, 1, heads, SEQ, SEQ), lambda i: (0, i, 0, 0, 0)))]
        ins += weight_ins(0, layer, 0) + piece_ins(0, layer, 0)
        ins += [(gains[layer], gspec)]
        base, part, low, g_proj, vec_a, bias_a = call(
            attn_backward,
            grid,
            ins,
            [
                (big, F32, flat),
                (big, BF, flat),
                (big, BF, flat),
                ((2, total_rows, 3 * width), BF, shard_block(3 * width)),
                ((8, D), F32, vec_spec),
                ((8, 3 * width), F32, whole_block((8, 3 * width))),
            ],
            [blob_scratch],
            unit_flops * 14 * width,
            f"attn_backward_{layer}",
        )
        if layer > 0:
            g_state = (base, core_perm(part))
        else:
            mine = lax.dynamic_slice(base, (core * share, 0), (share, D))
            away = lax.dynamic_slice(part, ((1 - core) * share, 0), (share, D))
            query_grad = mine + core_perm(away).astype(F32)
        (g_attn,) = call(
            attn_weights,
            (2,),
            [
                (low, whole_block(big)),
                (k["mixed"], pl.BlockSpec((1, total_rows, width), lambda i: (i, 0, 0))),
                (k["hidden"], whole_block(big)),
                (g_proj, pl.BlockSpec((1, total_rows, 3 * width), lambda i: (i, 0, 0))),
            ],
            [((2, D, BLOB), F32, full_out)],
            [],
            unit_flops * 8 * width,
            f"attn_weights_{layer}",
        )
        grad_attn[layer] = scatter(g_attn, order_attn)
        vectors[layer] = (vec_f, bias_f, vec_a, bias_a)

    first = jnp.where(core == 0, 1.0, 0.0)
    packed = []
    for vec_f, bias_f, vec_a, bias_a in vectors:
        norms = jnp.stack([vec_a[0], vec_f[0], vec_a[2], vec_a[1], vec_f[2], vec_f[1]]) * first
        inner_rows = jnp.zeros((4, BLOB), F32)
        inner_rows = lax.dynamic_update_slice(inner_rows, bias_f[0:1], (t_pos, 0))
        inner_rows = lax.dynamic_update_slice(inner_rows, bias_f[1:2], (t_pos ^ 2, 0))
        qv = jnp.zeros((4, 2, width), F32)
        for s, at in ((0, t_pos), (1, t_pos ^ 2)):
            both = jnp.stack([bias_a[s, :width], bias_a[s, 2 * width :]])
            qv = lax.dynamic_update_slice(qv, both[None], (at, 0, 0))
        packed.append(jnp.concatenate([norms, inner_rows, qv.transpose(1, 0, 2).reshape(2, 4 * width)]))
    packed = jnp.concatenate(packed)
    hops += 1
    summed = pl.pallas_call(
        functools.partial(total_over, dp_size),
        in_specs=[vmem],
        out_specs=vmem,
        out_shape=jax.ShapeDtypeStruct(packed.shape, F32),
        scratch_shapes=[
            pltpu.VMEM((hops + 1,) + packed.shape, F32),
            pltpu.VMEM((hops,) + packed.shape, F32),
            pltpu.SemaphoreType.DMA((hops,)),
            pltpu.SemaphoreType.DMA((hops,)),
        ],
        compiler_params=pltpu.CompilerParams(
            collective_id=1, has_side_effects=True, vmem_limit_bytes=16 * MIB
        ),
        name="total_over",
    )(packed)
    summed = summed.reshape(LAYERS, 12, D)
    grad_gain = summed[:, 0:2]
    grad_shift = summed[:, 2:6]
    grad_in_bias = summed[:, 6:10].reshape(LAYERS, 4 * BLOB)
    grad_qv_bias = summed[:, 10:12]

    attn = jnp.stack(grad_attn)
    return (
        per_pair,
        query_grad,
        attn[:, :, : 3 * width].reshape(LAYERS, D // dp_size, 3, width),
        attn[:, :, 3 * width :].transpose(0, 2, 1),
        jnp.stack(grad_in),
        jnp.stack(grad_down).transpose(0, 2, 1),
        grad_qv_bias,
        grad_in_bias,
        grad_gain,
        grad_shift,
    )


def solution(mesh):
    split = P(("dp", "tensor"), None)
    weights = (
        P(None, None, None, "tensor"),
        P(None, None, "tensor"),
        P(None, "tensor", None),
        P(None, None, "tensor"),
        P(None, "tensor"),
        P(None, "tensor", None),
        P(),
        P(),
    )
    return jax.shard_map(
        functools.partial(on_device, dict(mesh.shape)),
        mesh=mesh,
        in_specs=(split, split, P("dp"), P("dp"), P("dp")) + weights + weights,
        out_specs=(
            P("dp"),
            split,
            P(None, "dp", None, "tensor"),
            P(None, "tensor", "dp"),
            P(None, "dp", "tensor"),
            P(None, "tensor", "dp"),
            P(),
            P(),
            P(),
            P(),
        ),
        check_vma=False,
    )
```

```python
import functools
import math

import jax
import jax.numpy as jnp
from jax import lax
from jax.experimental import pallas as pl
from jax.experimental.pallas import tpu as pltpu
from jax.sharding import PartitionSpec as P

D = 768
HEAD = 64
SEQ = 256
LAYERS = 2
BLOB = 768
EPS = 1e-06
TEMPER = 0.05
FILL = -1e30
BF = jnp.bfloat16
F32 = jnp.float32
MESH = pl.DeviceIdType.MESH
SCALE = HEAD ** (-0.5)
MIB = 2**20


def mm(a, b):
    return jnp.dot(a, b, preferred_element_type=F32)


def mm_nt(a, b):
    return lax.dot_general(a, b, (((1,), (1,)), ((), ())), preferred_element_type=F32)


def mm_tn(a, b):
    return lax.dot_general(a, b, (((0,), (0,)), ((), ())), preferred_element_type=F32)


def norm(v, gain, shift):
    center = v - jnp.mean(v, axis=-1, keepdims=True)
    rate = lax.rsqrt(jnp.mean(center * center, axis=-1, keepdims=True) + EPS)
    xhat = center * rate
    return xhat, rate, xhat * gain + shift


def norm_back(g, xhat, rate, gain):
    gx = g * gain
    return rate * (
        gx
        - jnp.mean(gx, axis=-1, keepdims=True)
        - xhat * jnp.mean(gx * xhat, axis=-1, keepdims=True)
    )


def rows(v):
    return jnp.sum(v, axis=0, keepdims=True)


def groups():
    return [(layer, e, kind) for layer in range(LAYERS) for kind in range(2) for e in range(2)]


def forward(dp_size, nc, *refs):
    refs = list(refs)

    def take(n):
        return [refs.pop(0) for _ in range(n)]

    meta, count = take(2)
    x_in, blob_a, w_in, w_down, gains, shifts = [take(2) for _ in range(6)]
    bias, inv_q, inv_k = take(3)
    saves = dict(
        zip(("hidden", "proj", "probs", "mixed", "v1", "normed", "active", "slope", "v2"), take(9))
    )
    far_out, pair_out, grad_out = take(3)
    low, base, acc, send, recv, own_a, own_f, far = take(8)
    v_st, proj_st, probs_st, mixed_st, active_st, slope_st = take(6)
    far_bias, sums, held = take(3)
    y_send, y_recv, p_send, p_recv, x_send, x_recv, own_sem, save_sem, c_send, c_recv, b_sem = take(11)

    d = lax.axis_index("dp")
    t = lax.axis_index("tensor")
    core = t & 1
    half = t // 2
    q = d & 3
    share = x_in[0].shape[0]
    far_id, core_id, x_id, z_id = (d, t ^ 2), (d, t ^ 1), (d ^ 1, t), (d ^ 2, t)
    dp_bits = dp_size.bit_length() - 1
    bit_ids = [(d ^ (1 << k), t) for k in reversed(range(dp_bits))] + [far_id]
    greet(bit_ids + [core_id])

    def remote(src, dst, sems, at, device):
        return pltpu.make_async_remote_copy(
            src_ref=src,
            dst_ref=dst,
            send_sem=sems[0].at[at],
            recv_sem=sems[1].at[at],
            device_id=device,
            device_id_type=MESH,
        )

    mine = pl.ds(pl.multiple_of(core * share, 16), share)
    x_local = []
    x_remote = []
    for e in range(2):
        x_local.append(pltpu.make_async_copy(x_in[e], low.at[e, mine], own_sem.at[e, 2]))
        x_remote.append(remote(x_in[e], low.at[e, mine], (x_send, x_recv), e, core_id))

    def load_a(e, layer):
        return [pltpu.make_async_copy(blob_a[e].at[layer], own_a.at[e], own_sem.at[e, 0])]

    def load_f(e, layer):
        return [
            pltpu.make_async_copy(w_in[e].at[layer], own_f.at[e, 0], own_sem.at[e, 1]),
            pltpu.make_async_copy(w_down[e].at[layer], own_f.at[e, 1], own_sem.at[e, 3]),
        ]

    x_local[0].start()
    x_remote[0].start()
    for copy in load_a(0, 0):
        copy.start()
    b_copy = pltpu.make_async_remote_copy(
        src_ref=bias,
        dst_ref=far_bias,
        send_sem=b_sem.at[0],
        recv_sem=b_sem.at[1],
        device_id=far_id,
        device_id_type=MESH,
    )
    b_copy.start()
    x_local[1].start()
    x_remote[1].start()
    for copy in load_a(1, 0) + load_f(0, 0) + load_f(1, 0):
        copy.start()

    n = BLOB // 4
    third = n // 3
    order = groups()
    moves = []
    for g, (layer, e, kind) in enumerate(order):
        u = layer * 2 + e

        def at(quarter, start, size, which=None):
            row = pl.ds(pl.multiple_of(quarter * n + start, 16), size)
            if kind == 0:
                return far.at[u, 0, row]
            return far.at[u, pl.ds(1, 2), row] if which is None else far.at[u, 1 + which, row]

        def source(which, quarter, start, size):
            row = pl.ds(pl.multiple_of(quarter * n + start, 16), size)
            ref = blob_a[e] if kind == 0 else (w_in[e], w_down[e])[which]
            return ref.at[layer, row]

        sems = (y_send, y_recv)
        made = {}
        for w in range(1 + kind):
            made["y", w] = remote(source(w, q, 0, n), at(q, 0, n, w), sems, (g, w), far_id)
            made["t", w] = remote(
                source(w, q ^ 3, 0, third), at(q ^ 3, 0, third, w), sems, (g, 2 + w), far_id
            )
        made["x2"] = remote(at(q, 0, n), at(q, 0, n), sems, (g, 4), x_id)
        made["z2"] = remote(at(q, 0, n), at(q, 0, n), sems, (g, 5), z_id)
        made["x3"] = remote(at(q ^ 2, third, third), at(q ^ 2, third, third), sems, (g, 6), x_id)
        made["z3"] = remote(at(q ^ 1, 2 * third, third), at(q ^ 1, 2 * third, third), sems, (g, 7), z_id)
        got = dict(made)
        got["x2"] = remote(at(q ^ 1, 0, n), at(q ^ 1, 0, n), sems, (g, 4), x_id)
        got["z2"] = remote(at(q ^ 2, 0, n), at(q ^ 2, 0, n), sems, (g, 5), z_id)
        got["x3"] = remote(at(q ^ 3, third, third), at(q ^ 3, third, third), sems, (g, 6), x_id)
        got["z3"] = remote(at(q ^ 3, 2 * third, third), at(q ^ 3, 2 * third, third), sems, (g, 7), z_id)
        moves.append((made, got, kind))

    def start_y(g, name):
        made, _, kind = moves[g]
        for w in range(1 + kind):
            made[name, w].start()

    start_y(0, "y")
    for g in range(1, len(order)):
        start_y(g, "y")
        start_y(g - 1, "t")
    start_y(len(order) - 1, "t")

    def pass_first(g):
        made, got, kind = moves[g]
        for w in range(1 + kind):
            got["y", w].wait_recv()
        made["x2"].start()
        made["z2"].start()

    def pass_second(g):
        made, got, _ = moves[g]
        got["x2"].wait_recv()
        got["z2"].wait_recv()
        made["x3"].start()
        made["z3"].start()

    def ready(g):
        _, got, kind = moves[g]
        got["x3"].wait_recv()
        got["z3"].wait_recv()
        for w in range(1 + kind):
            got["t", w].wait_recv()

    def save(name, layer, src, k):
        return pltpu.make_async_copy(src, saves[name].at[layer], save_sem.at[k])

    pending = {}

    def start_save(name, layer, src):
        k = list(saves).index(name)
        copy = save(name, layer, src, k)
        copy.start()
        pending[name] = copy

    def end_save(*names):
        for name in names:
            if name in pending:
                pending.pop(name).wait()

    def block(i):
        return pl.ds(pl.multiple_of(i * SEQ, SEQ), SEQ)

    def part(e, k):
        return remote(send.at[e], recv.at[e, k % 2], (p_send.at[e], p_recv.at[e]), k, core_id)

    sent = {}

    def send_part(e, k):
        sent[e] = part(e, k)
        sent[e].start()

    width = proj_st.shape[2] // 3
    heads = width // HEAD

    def attn_part(e, s, w, x_low, i, layer):
        b = (bias, far_bias)[s]
        r = block(i)
        proj = (mm_nt(x_low, w[: 3 * width, :]) + b[e * 4 + layer : e * 4 + layer + 1, : 3 * width]).astype(BF)
        visible = lax.broadcasted_iota(jnp.int32, (1, SEQ), 1) < meta[e * nc + i]
        mixed = []
        for h in range(heads):
            queries = proj[:, h * HEAD : (h + 1) * HEAD]
            keys = proj[:, width + h * HEAD : width + (h + 1) * HEAD]
            values = proj[:, 2 * width + h * HEAD : 2 * width + (h + 1) * HEAD]
            scores = jnp.where(visible, mm_nt(queries, keys) * SCALE, FILL)
            ex = jnp.exp(scores - jnp.max(scores, axis=1, keepdims=True))
            probs = (ex * (1.0 / jnp.sum(ex, axis=1, keepdims=True))).astype(BF)
            if e == 0:
                probs_st[s, i, h] = probs
            mixed.append(mm(probs, values).astype(BF))
        mixed = jnp.concatenate(mixed, axis=1)
        if e == 0:
            proj_st[s, r, :] = proj
            mixed_st[s, r, :] = mixed
        return mm(mixed, w[3 * width : 4 * width, :])

    def ffn_part(e, s, w, x_low, i, layer):
        b = (bias, far_bias)[s]
        r = block(i)
        u = mm(x_low, w[0]) + b[e * 4 + 2 + layer : e * 4 + 3 + layer, :]
        portion = 0.5 + 0.5 * lax.erf(u * (0.5**0.5))
        active = (u * portion).astype(BF)
        if e == 0:
            active_st[s, r, :] = active
            slope_st[s, r, :] = (
                portion + u * (jnp.exp(-0.5 * u * u) * ((2 * math.pi) ** -0.5))
            ).astype(BF)
        return mm(active, w[1])

    def crops(body):
        lax.fori_loop(0, nc, lambda i, _: (body(i), 0)[1], 0)

    def joined(e, k, r):
        return base[e, r, :] + (send[e, r, :].astype(F32) + recv[e, k % 2, r, :].astype(F32))

    def attn_own(e, layer):
        for copy in load_a(e, layer):
            copy.wait()
        if layer == 0:
            x_local[e].wait()
            x_remote[e].wait_recv()
        else:
            part(e, 2 * layer - 1).wait_recv()
        if e == 0:
            end_save("v1", "normed", "proj", "probs", "mixed")

        def body(i):
            r = block(i)
            if layer == 0:
                x_low = low[e, r, :]
                x = x_low.astype(F32)
            else:
                v = joined(e, 2 * layer - 1, r)
                if e == 0:
                    v_st[r, :] = v
                x = norm(v, gains[e][layer - 1, 1:2, :], shifts[e][layer - 1, 3:4, :])[2]
                x_low = x.astype(BF)
                low[e, r, :] = x_low
            base[e, r, :] = x + shifts[e][layer, 0:1, :]
            acc[e, r, :] = attn_part(e, 0, own_a.at[e], x_low, i, layer)

        crops(body)
        if layer + 1 < LAYERS:
            for copy in load_a(e, layer + 1):
                copy.start()
        if e == 0:
            start_save("hidden", layer, low.at[e])
            if layer > 0:
                start_save("v2", layer - 1, v_st)

    def attn_far(e, layer):
        if e in sent:
            sent[e].wait_send()

        def body(i):
            r = block(i)
            total = acc[e, r, :] + attn_part(e, 1, far.at[2 * layer + e, 0], low[e, r, :], i, layer)
            send[e, r, :] = total.astype(BF)

        crops(body)
        send_part(e, 2 * layer)
        if e == 0:
            start_save("proj", layer, proj_st)
            start_save("probs", layer, probs_st)
            start_save("mixed", layer, mixed_st)

    def ffn_own(e, layer):
        for copy in load_f(e, layer):
            copy.wait()
        part(e, 2 * layer).wait_recv()
        if e == 0:
            end_save("hidden", "v2", "active", "slope")

        def body(i):
            r = block(i)
            v = joined(e, 2 * layer, r)
            if e == 0:
                v_st[r, :] = v
            x = norm(v, gains[e][layer, 0:1, :], shifts[e][layer, 1:2, :])[2]
            x_low = x.astype(BF)
            low[e, r, :] = x_low
            base[e, r, :] = x + shifts[e][layer, 2:3, :]
            acc[e, r, :] = ffn_part(e, 0, own_f.at[e], x_low, i, layer)

        crops(body)
        if layer + 1 < LAYERS:
            for copy in load_f(e, layer + 1):
                copy.start()
        if e == 0:
            start_save("normed", layer, low.at[e])
            start_save("v1", layer, v_st)

    def ffn_far(e, layer):
        sent[e].wait_send()

        def body(i):
            r = block(i)
            total = acc[e, r, :] + ffn_part(
                e, 1, far.at[2 * layer + e, pl.ds(1, 2)], low[e, r, :], i, layer
            )
            send[e, r, :] = total.astype(BF)

        crops(body)
        send_part(e, 2 * layer + 1)
        if e == 0:
            start_save("active", layer, active_st)
            start_save("slope", layer, slope_st)

    def pool(e):
        part(e, 2 * LAYERS - 1).wait_recv()
        if e == 0:
            end_save("v1")

        def body(i):
            r = block(i)
            v = joined(e, 2 * LAYERS - 1, r)
            if e == 0:
                v_st[r, :] = v
            x = norm(v, gains[e][LAYERS - 1, 1:2, :], shifts[e][LAYERS - 1, 3:4, :])[2]
            visible = lax.broadcasted_iota(jnp.int32, (SEQ, 1), 0) < meta[e * nc + i]
            sums[e, pl.ds(i, 1), :] = rows(jnp.where(visible, x, 0.0))

        crops(body)
        if e == 0:
            start_save("v2", LAYERS - 1, v_st)

    far_copies = []

    def keep_far(g):
        layer, e, kind = order[g]
        if e == 0:
            src = (far.at[2 * layer, 0:1], far.at[2 * layer, 1:3])[kind]
            dst = (far_out.at[layer, 0:1], far_out.at[layer, 1:3])[kind]
            copy = pltpu.make_async_copy(src, dst, save_sem.at[9 + 2 * layer + kind])
            copy.start()
            far_copies.append(copy)

    AO, AF, FO, FF = attn_own, attn_far, ffn_own, ffn_far
    P1, P2 = pass_first, pass_second

    def P3(g):
        ready(g)
        keep_far(g)

    AO(0, 0)
    P1(0)
    AO(1, 0)
    P1(1)
    P2(0)
    P3(0)
    b_copy.wait_recv()
    AF(0, 0)
    P2(1)
    P3(1)
    AF(1, 0)
    P1(2)
    FO(0, 0)
    FO(1, 0)
    P2(2)
    P1(3)
    P3(2)
    FF(0, 0)
    P1(4)
    AO(0, 1)
    P2(3)
    P3(3)
    FF(1, 0)
    P1(5)
    P2(4)
    P3(4)
    AF(0, 1)
    AO(1, 1)
    P1(6)
    P2(5)
    P3(5)
    AF(1, 1)
    FO(0, 1)
    FO(1, 1)
    P1(7)
    P2(6)
    P3(6)
    FF(0, 1)
    P2(7)
    P3(7)
    FF(1, 1)
    pool(0)
    pool(1)
    contrast(dp_size, nc, d, half, bit_ids, count, inv_q, inv_k, sums, pair_out, grad_out, held, c_send, c_recv, remote)
    end_save(*saves)
    for copy in far_copies:
        copy.wait()
    for e in range(2):
        sent[e].wait_send()
        x_remote[e].wait_send()
    b_copy.wait_send()
    for made, _, kind in moves:
        for copy in made.values():
            copy.wait_send()


def flips(dp_size, with_core):
    d = lax.axis_index("dp")
    t = lax.axis_index("tensor")
    found = [(d, t ^ 2)]
    for b in range(dp_size.bit_length() - 1):
        found.append((d ^ (1 << b), t))
    if with_core:
        found.append((d, t ^ 1))
    return found


def greet(partners):
    barrier = pltpu.get_barrier_semaphore()
    for p in partners:
        pl.semaphore_signal(barrier, inc=1, device_id=p, device_id_type=MESH)
    pl.semaphore_wait(barrier, len(partners))


def contrast(
    dp_size, nc, d, half, bit_ids, count, inv_q, inv_k, sums, pair_out, grad_out, held, send, recv, remote
):
    wide = D + 128
    dp_bits = dp_size.bit_length() - 1
    low = jnp.int32(0)
    for k in range(dp_bits):
        low = low + (((d >> (dp_bits - 1 - k)) & 1) << k)
    me = low + half * dp_size

    def unit(s, inv):
        pooled = s * inv
        r = lax.rsqrt(jnp.sum(pooled * pooled, axis=1, keepdims=True) + EPS)
        return pooled * r, r

    unit_q, rate_q = unit(sums[0, 0:nc, :], inv_q[...])
    unit_k, _ = unit(sums[1, 0:nc, :], inv_k[...])
    held[me] = jnp.zeros((8, wide), F32)
    held[me, 0:nc, 0:D] = unit_k
    held[me, nc : 2 * nc, 0:D] = unit_q
    slot = half * nc + lax.broadcasted_iota(jnp.int32, (nc, 128), 0)
    lane = lax.broadcasted_iota(jnp.int32, (nc, 128), 1)
    held[me, 0:nc, D:wide] = jnp.where((slot < count[0]) & (lane == 0), 1.0, 0.0)
    for s, p in enumerate(bit_ids):
        mine = pl.ds((me >> s) << s, 1 << s)
        theirs = pl.ds(((me >> s) ^ 1) << s, 1 << s)
        remote(held.at[mine], held.at[mine], (send, recv), s, p).start()
        remote(held.at[theirs], held.at[theirs], (send, recv), s, p).wait_recv()
    for s, p in enumerate(bit_ids):
        mine = pl.ds((me >> s) << s, 1 << s)
        remote(held.at[mine], held.at[mine], (send, recv), s, p).wait_send()
    chips = held.shape[0]
    every = held[...].reshape(chips * 8, wide)
    keys = every[:, 0:D]
    here = jnp.concatenate([held[low], held[low + dp_size]], axis=0)[:, 0:D]

    def exact(a, b, dims):
        return lax.dot_general(
            a, b, (dims, ((), ())), precision=lax.Precision.HIGHEST, preferred_element_type=F32
        )

    one = jnp.where(lax.broadcasted_iota(jnp.int32, (16, 128), 1) == 0, 1.0, 0.0)
    live = exact(one, every[:, D:wide], ((1,), (1,))) > 0.5
    logits = exact(here, keys, ((1,), (1,))) / TEMPER
    masked = jnp.where(live, logits, FILL)
    highest = jnp.max(masked, axis=1, keepdims=True)
    e = jnp.exp(masked - highest)
    total = jnp.sum(e, axis=1, keepdims=True)
    row = lax.broadcasted_iota(jnp.int32, (16, 1), 0)
    chip = row // 8
    place = row % 8 - nc
    column = lax.broadcasted_iota(jnp.int32, (16, chips * 8), 1)
    own = column == (low + chip * dp_size) * 8 + place
    live_here = (place >= 0) & (place < nc) & (chip * nc + place < count[0])
    own_logit = jnp.sum(jnp.where(own, logits, 0.0), axis=1, keepdims=True)
    pair_out[...] = jnp.broadcast_to(
        jnp.where(live_here, highest + jnp.log(total) - own_logit, 0.0), (16, 128)
    )
    weighting = jnp.where(live_here, e / total - own.astype(F32), 0.0) * (SEQ / TEMPER)
    g_unit = exact(weighting, keys, ((1,), (0,)))
    g_unit = jnp.where(half == 0, g_unit[nc : 2 * nc], g_unit[8 + nc : 8 + 2 * nc])
    g_pooled = rate_q * (g_unit - unit_q * jnp.sum(unit_q * g_unit, axis=1, keepdims=True))
    grad_out[...] = g_pooled * inv_q[...]


def total_over(dp_size, v_ref, out_ref, held, got, send, recv):
    partners = flips(dp_size, True)
    greet(partners)
    held[0] = v_ref[...]
    for s, p in enumerate(partners):
        copy = pltpu.make_async_remote_copy(
            src_ref=held.at[s],
            dst_ref=got.at[s],
            send_sem=send.at[s],
            recv_sem=recv.at[s],
            device_id=p,
            device_id_type=MESH,
        )
        copy.start()
        copy.wait()
        held[s + 1] = held[s] + got[s]
    out_ref[...] = held[len(partners)]


def ffn_backward(top, meta, *refs):
    refs = list(refs)
    if top:
        g_sum = refs.pop(0)
    else:
        base, theirs = [refs.pop(0) for _ in range(2)]
    v, slope, own_in, own_down, far_in, far_down, gain = [refs.pop(0) for _ in range(7)]
    base_out, part_out, low_out, inner_out, vec_out, bias_out = refs
    crop = pl.program_id(0)

    @pl.when(crop == 0)
    def _():
        vec_out[...] = jnp.zeros_like(vec_out)
        bias_out[...] = jnp.zeros_like(bias_out)

    if top:
        visible = lax.broadcasted_iota(jnp.int32, (SEQ, 1), 0) < meta[crop]
        g = jnp.where(visible, g_sum[0], 0.0)
    else:
        g = base[...] + theirs[...].astype(F32)
    xh, rate, _ = norm(v[0], gain[1:2, :], 0.0)
    gc = norm_back(g, xh, rate, gain[1:2, :])
    vec_out[0:1, :] += rows(g * xh)
    vec_out[1:2, :] += rows(g)
    vec_out[2:3, :] += rows(gc)
    low = gc.astype(BF)
    low_out[...] = low
    part = None
    for s, (w_in, w_down) in enumerate(((own_in, own_down), (far_in, far_down))):
        w_in, w_down = [w[0] if len(w.shape) == 3 else w[0, 0] for w in (w_in, w_down)]
        inner = (mm_nt(low, w_down) * slope[0, s].astype(F32)).astype(BF)
        inner_out[s] = inner
        bias_out[s : s + 1, :] += rows(inner.astype(F32))
        term = mm_nt(inner, w_in)
        part = term if part is None else part + term
    base_out[...] = gc + part
    part_out[...] = part.astype(BF)


def attn_backward(meta, *refs):
    base, theirs, v, proj, probs, own, far, gain = refs[:8]
    base_out, part_out, low_out, proj_out, vec_out, bias_out = refs[8:]
    crop = pl.program_id(0)

    @pl.when(crop == 0)
    def _():
        vec_out[...] = jnp.zeros_like(vec_out)
        bias_out[...] = jnp.zeros_like(bias_out)

    g = base[...] + theirs[...].astype(F32)
    xh, rate, _ = norm(v[0], gain[0:1, :], 0.0)
    gr = norm_back(g, xh, rate, gain[0:1, :])
    vec_out[0:1, :] += rows(g * xh)
    vec_out[1:2, :] += rows(g)
    vec_out[2:3, :] += rows(gr)
    low = gr.astype(BF)
    low_out[...] = low
    width = proj.shape[3] // 3
    heads = width // HEAD
    part = None
    for s, w in enumerate((own[0], far[0, 0])):
        g_mixed = mm_nt(low, w[3 * width : 4 * width, :]).astype(BF)
        pr = proj[0, s]
        parts = [[], [], []]
        for h in range(heads):
            queries = pr[:, h * HEAD : (h + 1) * HEAD]
            keys = pr[:, width + h * HEAD : width + (h + 1) * HEAD]
            values = pr[:, 2 * width + h * HEAD : 2 * width + (h + 1) * HEAD]
            gm = g_mixed[:, h * HEAD : (h + 1) * HEAD]
            p_low = probs[0, s, 0, h]
            p = p_low.astype(F32)
            gp = mm_nt(gm, values)
            gs = (p * (gp - jnp.sum(p * gp, axis=1, keepdims=True))).astype(BF)
            parts[0].append((mm(gs, keys) * SCALE).astype(BF))
            parts[1].append((mm_tn(gs, queries) * SCALE).astype(BF))
            parts[2].append(mm_tn(p_low, gm).astype(BF))
        g_proj = jnp.concatenate(parts[0] + parts[1] + parts[2], axis=1)
        proj_out[s] = g_proj
        bias_out[s : s + 1, :] += rows(g_proj.astype(F32))
        term = mm(g_proj, w[: 3 * width, :])
        part = term if part is None else part + term
    base_out[...] = gr + part
    part_out[...] = part.astype(BF)


def ffn_weights(low, active, normed, inner, in_out, down_out):
    down_out[0] = mm_tn(low[...], active[0, 0])
    in_out[0] = mm_tn(normed[0], inner[0])


def attn_weights(low, mixed, hidden, g_proj, out):
    width = mixed.shape[3]
    out[0, :, 0 : 3 * width] = mm_tn(hidden[0], g_proj[0])
    out[0, :, 3 * width : 4 * width] = mm_tn(low[...], mixed[0, 0])


SMEM = pl.BlockSpec(memory_space=pltpu.SMEM)


def row_block(width):
    return pl.BlockSpec((SEQ, width), lambda i: (i, 0))


def shard_block(width):
    return pl.BlockSpec((2, SEQ, width), lambda i: (0, i, 0))


def whole_block(shape):
    return pl.BlockSpec(shape, lambda i: (0,) * len(shape))


def call(body, grid, ins, outs, scratch, flops, name):
    arrays = [a for a, _ in ins]
    size = sum(a.size * a.dtype.itemsize for a in arrays)
    size += sum(math.prod(s) * jnp.dtype(t).itemsize for s, t, _ in outs)
    return pl.pallas_call(
        body,
        grid=grid,
        in_specs=[s for _, s in ins],
        out_specs=[s for _, _, s in outs],
        out_shape=[jax.ShapeDtypeStruct(s, t) for s, t, _ in outs],
        scratch_shapes=scratch,
        compiler_params=pltpu.CompilerParams(vmem_limit_bytes=52 * MIB),
        cost_estimate=pl.CostEstimate(flops=int(flops), bytes_accessed=int(size), transcendentals=0),
        name=name,
    )(*arrays)


def on_device(mesh_shape, *args):
    (
        query_input,
        key_input,
        query_length,
        key_length,
        pair_count,
    ) = args[:5]
    encoders = (args[5:13], args[13:21])
    dp_size = mesh_shape["dp"]
    dp_bits = dp_size.bit_length() - 1
    d_pos = lax.axis_index("dp")
    t_pos = lax.axis_index("tensor")
    quarter = d_pos & 3
    core = t_pos & 1
    half = t_pos // 2
    share = query_input.shape[0]
    total_rows = 2 * share
    nc = total_rows // SEQ
    width = args[5].shape[3]

    def far_perm(x):
        return lax.ppermute(x, "tensor", [(i, i ^ 2) for i in range(4)])

    def core_perm(x):
        return lax.ppermute(x, "tensor", [(i, i ^ 1) for i in range(4)])

    def dp_perm(x, bit):
        return lax.ppermute(x, "dp", [(i, i ^ (1 << bit)) for i in range(dp_size)])

    blob_a = [
        jnp.concatenate(
            [w[0].transpose(0, 2, 3, 1).reshape(LAYERS, 3 * width, D), w[2]], axis=1
        )
        for w in encoders
    ]
    bias_rows = []
    for w in encoders:
        zero = jnp.zeros((LAYERS, width), F32)
        bias_rows += [jnp.concatenate([w[1][:, 0], zero, w[1][:, 1], zero], axis=1), w[4]]
    bias = jnp.concatenate(bias_rows, axis=0)
    lengths = [
        lax.dynamic_slice(v, (half * nc,), (nc,)) for v in (query_length, key_length)
    ]
    meta = jnp.concatenate(lengths)
    inverse = [(1.0 / v.astype(F32))[:, None] for v in lengths]
    grid = (nc,)
    gspec = whole_block((2, D))
    flat = row_block(D)
    big = (total_rows, D)
    heads = width // HEAD
    unit_flops = 2 * total_rows * D
    vmem = pl.BlockSpec(memory_space=pltpu.VMEM)
    hbm = pl.BlockSpec(memory_space=pl.ANY)
    hops = dp_bits + 1
    n_groups = 4 * LAYERS
    shaped = jax.ShapeDtypeStruct
    sem = pltpu.SemaphoreType.DMA
    rows_of = lambda *s: (LAYERS,) + s
    results = pl.pallas_call(
        functools.partial(forward, dp_size, nc),
        in_specs=[SMEM] * 2 + [hbm] * 8 + [vmem] * 7,
        out_specs=[hbm] * 10 + [vmem] * 2,
        out_shape=[
            shaped(rows_of(total_rows, D), BF),
            shaped(rows_of(2, total_rows, 3 * width), BF),
            shaped(rows_of(2, nc, heads, SEQ, SEQ), BF),
            shaped(rows_of(2, total_rows, width), BF),
            shaped(rows_of(total_rows, D), F32),
            shaped(rows_of(total_rows, D), BF),
            shaped(rows_of(2, total_rows, BLOB), BF),
            shaped(rows_of(2, total_rows, BLOB), BF),
            shaped(rows_of(total_rows, D), F32),
            shaped(rows_of(3, BLOB, D), BF),
            shaped((16, 128), F32),
            shaped((nc, D), F32),
        ],
        scratch_shapes=[
            pltpu.VMEM((2,) + big, BF),
            pltpu.VMEM((2,) + big, F32),
            pltpu.VMEM((2,) + big, F32),
            pltpu.VMEM((2,) + big, BF),
            pltpu.VMEM((2, 2) + big, BF),
            pltpu.VMEM((2, BLOB, D), BF),
            pltpu.VMEM((2, 2, BLOB, D), BF),
            pltpu.VMEM((2 * LAYERS, 3, BLOB, D), BF),
            pltpu.VMEM(big, F32),
            pltpu.VMEM((2, total_rows, 3 * width), BF),
            pltpu.VMEM((2, nc, heads, SEQ, SEQ), BF),
            pltpu.VMEM((2, total_rows, width), BF),
            pltpu.VMEM((2, total_rows, BLOB), BF),
            pltpu.VMEM((2, total_rows, BLOB), BF),
            pltpu.VMEM(bias.shape, F32),
            pltpu.VMEM((2, 8, D), F32),
            pltpu.VMEM((2 * dp_size, 8, D + 128), F32),
            sem((n_groups, 8)),
            sem((n_groups, 8)),
            sem((2, 2 * LAYERS)),
            sem((2, 2 * LAYERS)),
            sem((2,)),
            sem((2,)),
            sem((2, 4)),
            sem((9 + 2 * LAYERS,)),
            sem((hops,)),
            sem((hops,)),
            sem((2,)),
        ],
        compiler_params=pltpu.CompilerParams(
            collective_id=0, has_side_effects=True, vmem_limit_bytes=int(60.5 * MIB)
        ),
        cost_estimate=pl.CostEstimate(
            flops=unit_flops * 80 * BLOB // 4, bytes_accessed=100 * MIB, transcendentals=0
        ),
        name="forward",
    )(
        meta,
        pair_count,
        query_input,
        key_input,
        *blob_a,
        encoders[0][3],
        encoders[1][3],
        encoders[0][5],
        encoders[1][5],
        encoders[0][6],
        encoders[1][6],
        encoders[0][7],
        encoders[1][7],
        bias,
        *inverse,
    )
    kept = dict(
        zip(("hidden", "proj", "probs", "mixed", "v1", "normed", "active", "slope", "v2"), results)
    )
    far, pair_rows, g_sum = results[9:]
    per_pair = jnp.concatenate([pair_rows[nc : 2 * nc, 0], pair_rows[8 + nc : 8 + 2 * nc, 0]])

    def scatter(full, order):
        cur = full.reshape((2,) + (2,) * dp_bits + (D // dp_size, BLOB))
        axes = ["y"] + list(reversed(range(dp_bits)))
        for name in order:
            at = axes.index(name)
            bit = jnp.int32(0) if name == "y" else (d_pos >> name) & 1
            keep = lax.dynamic_index_in_dim(cur, bit, at, keepdims=False)
            send = lax.dynamic_index_in_dim(cur, 1 - bit, at, keepdims=False)
            got = far_perm(send) if name == "y" else dp_perm(send, name)
            cur = keep + got
            axes.pop(at)
        return cur

    rest = list(range(2, dp_bits))
    order_in = ["y", 0, 1] + rest
    order_down = [0, "y", 1] + rest
    order_attn = [1, "y", 0] + rest

    vec_spec = whole_block((8, D))
    grad_in = [None] * LAYERS
    grad_down = [None] * LAYERS
    grad_attn = [None] * LAYERS
    vectors = [None] * LAYERS
    g_state = None
    for layer in reversed(range(LAYERS)):
        w = encoders[0]
        gains = w[6]
        top = layer == LAYERS - 1

        def layer_rows(dims, kind):
            if kind == 0:
                return pl.BlockSpec((1, SEQ, dims), lambda i: (layer, i, 0))
            return pl.BlockSpec((1, 2, SEQ, dims), lambda i: (layer, 0, i, 0))

        own_spec = pl.BlockSpec((1, BLOB, D), lambda i: (layer, 0, 0))
        far_specs = [pl.BlockSpec((1, 1, BLOB, D), lambda i, k=k: (layer, k, 0, 0)) for k in range(3)]
        ins = [(meta, SMEM)]
        if top:
            ins += [(g_sum.reshape(nc, 1, D), pl.BlockSpec((1, 1, D), lambda i: (i, 0, 0)))]
        else:
            ins += [(a, flat) for a in g_state]
        ins += [(kept["v2"], layer_rows(D, 0)), (kept["slope"], layer_rows(BLOB, 1))]
        ins += [(w[3], own_spec), (w[5], own_spec), (far, far_specs[1]), (far, far_specs[2])]
        ins += [(gains[layer], gspec)]
        base, part, low, inner, vec_f, bias_f = call(
            functools.partial(ffn_backward, top),
            grid,
            ins,
            [
                (big, F32, flat),
                (big, BF, flat),
                (big, BF, flat),
                ((2, total_rows, BLOB), BF, shard_block(BLOB)),
                ((8, D), F32, vec_spec),
                ((8, BLOB), F32, whole_block((8, BLOB))),
            ],
            [],
            unit_flops * 4 * BLOB,
            f"ffn_backward_{layer}",
        )
        other = core_perm(part)
        one_shard = pl.BlockSpec((1, total_rows, BLOB), lambda i: (i, 0, 0))
        full_out = pl.BlockSpec((1, D, BLOB), lambda i: (i, 0, 0))
        layer_whole = pl.BlockSpec((1,) + big, lambda i: (layer, 0, 0))

        def layer_shard(dims):
            return pl.BlockSpec((1, 1, total_rows, dims), lambda i: (layer, i, 0, 0))

        g_in, g_down = call(
            ffn_weights,
            (2,),
            [
                (low, whole_block(big)),
                (kept["active"], layer_shard(BLOB)),
                (kept["normed"], layer_whole),
                (inner, one_shard),
            ],
            [((2, D, BLOB), F32, full_out), ((2, D, BLOB), F32, full_out)],
            [],
            unit_flops * 4 * BLOB,
            f"ffn_weights_{layer}",
        )
        grad_in[layer] = scatter(g_in, order_in)
        grad_down[layer] = scatter(g_down, order_down)
        ins = [(meta, SMEM), (base, flat), (other, flat)]
        ins += [(kept["v1"], layer_rows(D, 0)), (kept["proj"], layer_rows(3 * width, 1))]
        ins += [
            (kept["probs"], pl.BlockSpec((1, 2, 1, heads, SEQ, SEQ), lambda i: (layer, 0, i, 0, 0, 0)))
        ]
        ins += [(blob_a[0], own_spec), (far, far_specs[0]), (gains[layer], gspec)]
        base, part, low, g_proj, vec_a, bias_a = call(
            attn_backward,
            grid,
            ins,
            [
                (big, F32, flat),
                (big, BF, flat),
                (big, BF, flat),
                ((2, total_rows, 3 * width), BF, shard_block(3 * width)),
                ((8, D), F32, vec_spec),
                ((8, 3 * width), F32, whole_block((8, 3 * width))),
            ],
            [],
            unit_flops * 14 * width,
            f"attn_backward_{layer}",
        )
        if layer > 0:
            g_state = (base, core_perm(part))
        else:
            mine = lax.dynamic_slice(base, (core * share, 0), (share, D))
            away = lax.dynamic_slice(part, ((1 - core) * share, 0), (share, D))
            query_grad = mine + core_perm(away).astype(F32)
        (g_attn,) = call(
            attn_weights,
            (2,),
            [
                (low, whole_block(big)),
                (kept["mixed"], layer_shard(width)),
                (kept["hidden"], layer_whole),
                (g_proj, pl.BlockSpec((1, total_rows, 3 * width), lambda i: (i, 0, 0))),
            ],
            [((2, D, BLOB), F32, full_out)],
            [],
            unit_flops * 8 * width,
            f"attn_weights_{layer}",
        )
        grad_attn[layer] = scatter(g_attn, order_attn)
        vectors[layer] = (vec_f, bias_f, vec_a, bias_a)

    first = jnp.where(core == 0, 1.0, 0.0)
    packed = []
    for vec_f, bias_f, vec_a, bias_a in vectors:
        norms = jnp.stack([vec_a[0], vec_f[0], vec_a[2], vec_a[1], vec_f[2], vec_f[1]]) * first
        inner_rows = jnp.zeros((4, BLOB), F32)
        inner_rows = lax.dynamic_update_slice(inner_rows, bias_f[0:1], (t_pos, 0))
        inner_rows = lax.dynamic_update_slice(inner_rows, bias_f[1:2], (t_pos ^ 2, 0))
        qv = jnp.zeros((4, 2, width), F32)
        for s, at in ((0, t_pos), (1, t_pos ^ 2)):
            both = jnp.stack([bias_a[s, :width], bias_a[s, 2 * width :]])
            qv = lax.dynamic_update_slice(qv, both[None], (at, 0, 0))
        packed.append(jnp.concatenate([norms, inner_rows, qv.transpose(1, 0, 2).reshape(2, 4 * width)]))
    packed = jnp.concatenate(packed)
    hops += 1
    summed = pl.pallas_call(
        functools.partial(total_over, dp_size),
        in_specs=[vmem],
        out_specs=vmem,
        out_shape=jax.ShapeDtypeStruct(packed.shape, F32),
        scratch_shapes=[
            pltpu.VMEM((hops + 1,) + packed.shape, F32),
            pltpu.VMEM((hops,) + packed.shape, F32),
            pltpu.SemaphoreType.DMA((hops,)),
            pltpu.SemaphoreType.DMA((hops,)),
        ],
        compiler_params=pltpu.CompilerParams(
            collective_id=1, has_side_effects=True, vmem_limit_bytes=16 * MIB
        ),
        name="total_over",
    )(packed)
    summed = summed.reshape(LAYERS, 12, D)
    grad_gain = summed[:, 0:2]
    grad_shift = summed[:, 2:6]
    grad_in_bias = summed[:, 6:10].reshape(LAYERS, 4 * BLOB)
    grad_qv_bias = summed[:, 10:12]

    attn = jnp.stack(grad_attn)
    return (
        per_pair,
        query_grad,
        attn[:, :, : 3 * width].reshape(LAYERS, D // dp_size, 3, width),
        attn[:, :, 3 * width :].transpose(0, 2, 1),
        jnp.stack(grad_in),
        jnp.stack(grad_down).transpose(0, 2, 1),
        grad_qv_bias,
        grad_in_bias,
        grad_gain,
        grad_shift,
    )


def solution(mesh):
    split = P(("dp", "tensor"), None)
    weights = (
        P(None, None, None, "tensor"),
        P(None, None, "tensor"),
        P(None, "tensor", None),
        P(None, None, "tensor"),
        P(None, "tensor"),
        P(None, "tensor", None),
        P(),
        P(),
    )
    return jax.shard_map(
        functools.partial(on_device, dict(mesh.shape)),
        mesh=mesh,
        in_specs=(split, split, P("dp"), P("dp"), P("dp")) + weights + weights,
        out_specs=(
            P("dp"),
            split,
            P(None, "dp", None, "tensor"),
            P(None, "tensor", "dp"),
            P(None, "dp", "tensor"),
            P(None, "tensor", "dp"),
            P(),
            P(),
            P(),
            P(),
        ),
        check_vma=False,
    )
```

```python
import functools
import math

import jax
import jax.numpy as jnp
from jax import lax
from jax.experimental import pallas as pl
from jax.experimental.pallas import tpu as pltpu
from jax.sharding import PartitionSpec as P

D = 768
HEAD = 64
SEQ = 256
LAYERS = 2
BLOB = 768
EPS = 1e-06
TEMPER = 0.05
FILL = -1e30
BF = jnp.bfloat16
F32 = jnp.float32
MESH = pl.DeviceIdType.MESH
SCALE = HEAD ** (-0.5)
MIB = 2**20


def mm(a, b):
    return jnp.dot(a, b, preferred_element_type=F32)


def mm_nt(a, b):
    return lax.dot_general(a, b, (((1,), (1,)), ((), ())), preferred_element_type=F32)


def mm_tn(a, b):
    return lax.dot_general(a, b, (((0,), (0,)), ((), ())), preferred_element_type=F32)


def norm(v, gain, shift):
    center = v - jnp.mean(v, axis=-1, keepdims=True)
    rate = lax.rsqrt(jnp.mean(center * center, axis=-1, keepdims=True) + EPS)
    xhat = center * rate
    return xhat, rate, xhat * gain + shift


def norm_back(g, xhat, rate, gain):
    gx = g * gain
    return rate * (
        gx
        - jnp.mean(gx, axis=-1, keepdims=True)
        - xhat * jnp.mean(gx * xhat, axis=-1, keepdims=True)
    )


def rows(v):
    return jnp.sum(v, axis=0, keepdims=True)


def groups():
    return [(layer, e, kind) for layer in range(LAYERS) for kind in range(2) for e in range(2)]


def forward(dp_size, nc, *refs):
    refs = list(refs)

    def take(n):
        return [refs.pop(0) for _ in range(n)]

    meta, count = take(2)
    x_in, blob_a, w_in, w_down, gains, shifts = [take(2) for _ in range(6)]
    bias, inv_q, inv_k = take(3)
    saves = dict(
        zip(("hidden", "proj", "probs", "mixed", "v1", "normed", "active", "slope", "v2"), take(9))
    )
    far_out, pair_out, grad_out = take(3)
    low, base, acc, send, recv, own_a, own_f, far = take(8)
    v_st, proj_st, probs_st, mixed_st, active_st, slope_st = take(6)
    far_bias, sums, held = take(3)
    y_send, y_recv, p_send, p_recv, x_send, x_recv, own_sem, save_sem, c_send, c_recv, b_sem = take(11)

    d = lax.axis_index("dp")
    t = lax.axis_index("tensor")
    core = t & 1
    half = t // 2
    q = d & 3
    share = x_in[0].shape[0]
    far_id, core_id, x_id, z_id = (d, t ^ 2), (d, t ^ 1), (d ^ 1, t), (d ^ 2, t)
    dp_bits = dp_size.bit_length() - 1
    bit_ids = [(d ^ (1 << k), t) for k in reversed(range(dp_bits))] + [far_id]
    greet(bit_ids + [core_id])

    def remote(src, dst, sems, at, device):
        return pltpu.make_async_remote_copy(
            src_ref=src,
            dst_ref=dst,
            send_sem=sems[0].at[at],
            recv_sem=sems[1].at[at],
            device_id=device,
            device_id_type=MESH,
        )

    mine = pl.ds(pl.multiple_of(core * share, 16), share)
    x_local = []
    x_remote = []
    for e in range(2):
        x_local.append(pltpu.make_async_copy(x_in[e], low.at[e, mine], own_sem.at[e, 2]))
        x_remote.append(remote(x_in[e], low.at[e, mine], (x_send, x_recv), e, core_id))

    def load_a(e, layer):
        return [pltpu.make_async_copy(blob_a[e].at[layer], own_a.at[e], own_sem.at[e, 0])]

    def load_f(e, layer):
        return [
            pltpu.make_async_copy(w_in[e].at[layer], own_f.at[e, 0], own_sem.at[e, 1]),
            pltpu.make_async_copy(w_down[e].at[layer], own_f.at[e, 1], own_sem.at[e, 3]),
        ]

    x_local[0].start()
    x_remote[0].start()
    for copy in load_a(0, 0):
        copy.start()
    b_copy = pltpu.make_async_remote_copy(
        src_ref=bias,
        dst_ref=far_bias,
        send_sem=b_sem.at[0],
        recv_sem=b_sem.at[1],
        device_id=far_id,
        device_id_type=MESH,
    )
    b_copy.start()
    x_local[1].start()
    x_remote[1].start()
    for copy in load_a(1, 0) + load_f(0, 0) + load_f(1, 0):
        copy.start()

    n = BLOB // 4
    third = n // 3
    order = groups()
    moves = []
    for g, (layer, e, kind) in enumerate(order):
        u = layer * 2 + e

        def at(quarter, start, size, which=None):
            row = pl.ds(pl.multiple_of(quarter * n + start, 16), size)
            if kind == 0:
                return far.at[u, 0, row]
            return far.at[u, pl.ds(1, 2), row] if which is None else far.at[u, 1 + which, row]

        def source(which, quarter, start, size):
            row = pl.ds(pl.multiple_of(quarter * n + start, 16), size)
            ref = blob_a[e] if kind == 0 else (w_in[e], w_down[e])[which]
            return ref.at[layer, row]

        sems = (y_send, y_recv)
        made = {}
        for w in range(1 + kind):
            made["y", w] = remote(source(w, q, 0, n), at(q, 0, n, w), sems, (g, w), far_id)
            made["t", w] = remote(
                source(w, q ^ 3, 0, third), at(q ^ 3, 0, third, w), sems, (g, 2 + w), far_id
            )
        made["x2"] = remote(at(q, 0, n), at(q, 0, n), sems, (g, 4), x_id)
        made["z2"] = remote(at(q, 0, n), at(q, 0, n), sems, (g, 5), z_id)
        made["x3"] = remote(at(q ^ 2, third, third), at(q ^ 2, third, third), sems, (g, 6), x_id)
        made["z3"] = remote(at(q ^ 1, 2 * third, third), at(q ^ 1, 2 * third, third), sems, (g, 7), z_id)
        got = dict(made)
        got["x2"] = remote(at(q ^ 1, 0, n), at(q ^ 1, 0, n), sems, (g, 4), x_id)
        got["z2"] = remote(at(q ^ 2, 0, n), at(q ^ 2, 0, n), sems, (g, 5), z_id)
        got["x3"] = remote(at(q ^ 3, third, third), at(q ^ 3, third, third), sems, (g, 6), x_id)
        got["z3"] = remote(at(q ^ 3, 2 * third, third), at(q ^ 3, 2 * third, third), sems, (g, 7), z_id)
        moves.append((made, got, kind))

    def start_y(g, name):
        made, _, kind = moves[g]
        for w in range(1 + kind):
            made[name, w].start()

    start_y(0, "y")
    for g in range(1, len(order)):
        start_y(g, "y")
        start_y(g - 1, "t")
    start_y(len(order) - 1, "t")

    def pass_first(g):
        made, got, kind = moves[g]
        for w in range(1 + kind):
            got["y", w].wait_recv()
        made["x2"].start()
        made["z2"].start()

    def pass_second(g):
        made, got, _ = moves[g]
        got["x2"].wait_recv()
        got["z2"].wait_recv()
        made["x3"].start()
        made["z3"].start()

    def ready(g):
        _, got, kind = moves[g]
        got["x3"].wait_recv()
        got["z3"].wait_recv()
        for w in range(1 + kind):
            got["t", w].wait_recv()

    def save(name, layer, src, k):
        return pltpu.make_async_copy(src, saves[name].at[layer], save_sem.at[k])

    pending = {}

    def start_save(name, layer, src):
        k = list(saves).index(name)
        copy = save(name, layer, src, k)
        copy.start()
        pending[name] = copy

    def end_save(*names):
        for name in names:
            if name in pending:
                pending.pop(name).wait()

    def block(i):
        return pl.ds(pl.multiple_of(i * SEQ, SEQ), SEQ)

    def part(e, k):
        return remote(send.at[e], recv.at[e, k % 2], (p_send.at[e], p_recv.at[e]), k, core_id)

    sent = {}

    def send_part(e, k):
        sent[e] = part(e, k)
        sent[e].start()

    width = proj_st.shape[2] // 3
    heads = width // HEAD

    def attn_part(e, s, w, x_low, i, layer):
        b = (bias, far_bias)[s]
        r = block(i)
        proj = (mm_nt(x_low, w[: 3 * width, :]) + b[e * 4 + layer : e * 4 + layer + 1, : 3 * width]).astype(BF)
        visible = lax.broadcasted_iota(jnp.int32, (1, SEQ), 1) < meta[e * nc + i]
        mixed = []
        for h in range(heads):
            queries = proj[:, h * HEAD : (h + 1) * HEAD]
            keys = proj[:, width + h * HEAD : width + (h + 1) * HEAD]
            values = proj[:, 2 * width + h * HEAD : 2 * width + (h + 1) * HEAD]
            scores = jnp.where(visible, mm_nt(queries, keys) * SCALE, FILL)
            ex = jnp.exp(scores - jnp.max(scores, axis=1, keepdims=True))
            probs = (ex * (1.0 / jnp.sum(ex, axis=1, keepdims=True))).astype(BF)
            if e == 0:
                probs_st[s, i, h] = probs
            mixed.append(mm(probs, values).astype(BF))
        mixed = jnp.concatenate(mixed, axis=1)
        if e == 0:
            proj_st[s, r, :] = proj
            mixed_st[s, r, :] = mixed
        return mm(mixed, w[3 * width : 4 * width, :])

    def ffn_part(e, s, w, x_low, i, layer):
        b = (bias, far_bias)[s]
        r = block(i)
        u = mm(x_low, w[0]) + b[e * 4 + 2 + layer : e * 4 + 3 + layer, :]
        portion = 0.5 + 0.5 * lax.erf(u * (0.5**0.5))
        active = (u * portion).astype(BF)
        if e == 0:
            active_st[s, r, :] = active
            slope_st[s, r, :] = (
                portion + u * (jnp.exp(-0.5 * u * u) * ((2 * math.pi) ** -0.5))
            ).astype(BF)
        return mm(active, w[1])

    def crops(body):
        lax.fori_loop(0, nc, lambda i, _: (body(i), 0)[1], 0)

    def joined(e, k, r):
        return base[e, r, :] + (send[e, r, :].astype(F32) + recv[e, k % 2, r, :].astype(F32))

    def attn_own(e, layer):
        for copy in load_a(e, layer):
            copy.wait()
        if layer == 0:
            x_local[e].wait()
            x_remote[e].wait_recv()
        else:
            part(e, 2 * layer - 1).wait_recv()
        if e == 0:
            end_save("v1", "normed", "proj", "probs", "mixed")

        def body(i):
            r = block(i)
            if layer == 0:
                x_low = low[e, r, :]
                x = x_low.astype(F32)
            else:
                v = joined(e, 2 * layer - 1, r)
                if e == 0:
                    v_st[r, :] = v
                x = norm(v, gains[e][layer - 1, 1:2, :], shifts[e][layer - 1, 3:4, :])[2]
                x_low = x.astype(BF)
                low[e, r, :] = x_low
            base[e, r, :] = x + shifts[e][layer, 0:1, :]
            acc[e, r, :] = attn_part(e, 0, own_a.at[e], x_low, i, layer)

        crops(body)
        if layer + 1 < LAYERS:
            for copy in load_a(e, layer + 1):
                copy.start()
        if e == 0:
            start_save("hidden", layer, low.at[e])
            if layer > 0:
                start_save("v2", layer - 1, v_st)

    def attn_far(e, layer):
        if e in sent:
            sent[e].wait_send()

        def body(i):
            r = block(i)
            total = acc[e, r, :] + attn_part(e, 1, far.at[2 * layer + e, 0], low[e, r, :], i, layer)
            send[e, r, :] = total.astype(BF)

        crops(body)
        send_part(e, 2 * layer)
        if e == 0:
            start_save("proj", layer, proj_st)
            start_save("probs", layer, probs_st)
            start_save("mixed", layer, mixed_st)

    def ffn_own(e, layer):
        for copy in load_f(e, layer):
            copy.wait()
        part(e, 2 * layer).wait_recv()
        if e == 0:
            end_save("hidden", "v2", "active", "slope")

        def body(i):
            r = block(i)
            v = joined(e, 2 * layer, r)
            if e == 0:
                v_st[r, :] = v
            x = norm(v, gains[e][layer, 0:1, :], shifts[e][layer, 1:2, :])[2]
            x_low = x.astype(BF)
            low[e, r, :] = x_low
            base[e, r, :] = x + shifts[e][layer, 2:3, :]
            acc[e, r, :] = ffn_part(e, 0, own_f.at[e], x_low, i, layer)

        crops(body)
        if layer + 1 < LAYERS:
            for copy in load_f(e, layer + 1):
                copy.start()
        if e == 0:
            start_save("normed", layer, low.at[e])
            start_save("v1", layer, v_st)

    def ffn_far(e, layer):
        sent[e].wait_send()

        def body(i):
            r = block(i)
            total = acc[e, r, :] + ffn_part(
                e, 1, far.at[2 * layer + e, pl.ds(1, 2)], low[e, r, :], i, layer
            )
            send[e, r, :] = total.astype(BF)

        crops(body)
        send_part(e, 2 * layer + 1)
        if e == 0:
            start_save("active", layer, active_st)
            start_save("slope", layer, slope_st)

    def pool(e):
        part(e, 2 * LAYERS - 1).wait_recv()
        if e == 0:
            end_save("v1")

        def body(i):
            r = block(i)
            v = joined(e, 2 * LAYERS - 1, r)
            if e == 0:
                v_st[r, :] = v
            x = norm(v, gains[e][LAYERS - 1, 1:2, :], shifts[e][LAYERS - 1, 3:4, :])[2]
            visible = lax.broadcasted_iota(jnp.int32, (SEQ, 1), 0) < meta[e * nc + i]
            sums[e, pl.ds(i, 1), :] = rows(jnp.where(visible, x, 0.0))

        crops(body)
        if e == 0:
            start_save("v2", LAYERS - 1, v_st)

    far_copies = []

    def keep_far(g):
        layer, e, kind = order[g]
        if e == 0:
            src = (far.at[2 * layer, 0:1], far.at[2 * layer, 1:3])[kind]
            dst = (far_out.at[layer, 0:1], far_out.at[layer, 1:3])[kind]
            copy = pltpu.make_async_copy(src, dst, save_sem.at[9 + 2 * layer + kind])
            copy.start()
            far_copies.append(copy)

    AO, AF, FO, FF = attn_own, attn_far, ffn_own, ffn_far
    P1, P2 = pass_first, pass_second

    def P3(g):
        ready(g)
        keep_far(g)

    AO(0, 0)
    P1(0)
    AO(1, 0)
    P1(1)
    P2(0)
    P3(0)
    b_copy.wait_recv()
    AF(0, 0)
    P2(1)
    P3(1)
    AF(1, 0)
    P1(2)
    FO(0, 0)
    FO(1, 0)
    P2(2)
    P1(3)
    P3(2)
    FF(0, 0)
    P1(4)
    AO(0, 1)
    P2(3)
    P3(3)
    FF(1, 0)
    P1(5)
    P2(4)
    P3(4)
    AF(0, 1)
    AO(1, 1)
    P1(6)
    P2(5)
    P3(5)
    AF(1, 1)
    FO(0, 1)
    FO(1, 1)
    P1(7)
    P2(6)
    P3(6)
    FF(0, 1)
    P2(7)
    P3(7)
    FF(1, 1)
    pool(0)
    pool(1)
    contrast(dp_size, nc, d, half, bit_ids, count, inv_q, inv_k, sums, pair_out, grad_out, held, c_send, c_recv, remote)
    end_save(*saves)
    for copy in far_copies:
        copy.wait()
    for e in range(2):
        sent[e].wait_send()
        x_remote[e].wait_send()
    b_copy.wait_send()
    for made, _, kind in moves:
        for copy in made.values():
            copy.wait_send()


def greet(partners):
    barrier = pltpu.get_barrier_semaphore()
    for p in partners:
        pl.semaphore_signal(barrier, inc=1, device_id=p, device_id_type=MESH)
    pl.semaphore_wait(barrier, len(partners))


def contrast(
    dp_size, nc, d, half, bit_ids, count, inv_q, inv_k, sums, pair_out, grad_out, held, send, recv, remote
):
    wide = D + 128
    dp_bits = dp_size.bit_length() - 1
    low = jnp.int32(0)
    for k in range(dp_bits):
        low = low + (((d >> (dp_bits - 1 - k)) & 1) << k)
    me = low + half * dp_size

    def unit(s, inv):
        pooled = s * inv
        r = lax.rsqrt(jnp.sum(pooled * pooled, axis=1, keepdims=True) + EPS)
        return pooled * r, r

    unit_q, rate_q = unit(sums[0, 0:nc, :], inv_q[...])
    unit_k, _ = unit(sums[1, 0:nc, :], inv_k[...])
    held[me] = jnp.zeros((8, wide), F32)
    held[me, 0:nc, 0:D] = unit_k
    held[me, nc : 2 * nc, 0:D] = unit_q
    slot = half * nc + lax.broadcasted_iota(jnp.int32, (nc, 128), 0)
    lane = lax.broadcasted_iota(jnp.int32, (nc, 128), 1)
    held[me, 0:nc, D:wide] = jnp.where((slot < count[0]) & (lane == 0), 1.0, 0.0)
    for s, p in enumerate(bit_ids):
        mine = pl.ds((me >> s) << s, 1 << s)
        theirs = pl.ds(((me >> s) ^ 1) << s, 1 << s)
        remote(held.at[mine], held.at[mine], (send, recv), s, p).start()
        remote(held.at[theirs], held.at[theirs], (send, recv), s, p).wait_recv()
    for s, p in enumerate(bit_ids):
        mine = pl.ds((me >> s) << s, 1 << s)
        remote(held.at[mine], held.at[mine], (send, recv), s, p).wait_send()
    chips = held.shape[0]
    every = held[...].reshape(chips * 8, wide)
    keys = every[:, 0:D]
    here = jnp.concatenate([held[low], held[low + dp_size]], axis=0)[:, 0:D]

    def exact(a, b, dims):
        return lax.dot_general(
            a, b, (dims, ((), ())), precision=lax.Precision.HIGHEST, preferred_element_type=F32
        )

    one = jnp.where(lax.broadcasted_iota(jnp.int32, (16, 128), 1) == 0, 1.0, 0.0)
    live = exact(one, every[:, D:wide], ((1,), (1,))) > 0.5
    logits = exact(here, keys, ((1,), (1,))) / TEMPER
    masked = jnp.where(live, logits, FILL)
    highest = jnp.max(masked, axis=1, keepdims=True)
    e = jnp.exp(masked - highest)
    total = jnp.sum(e, axis=1, keepdims=True)
    row = lax.broadcasted_iota(jnp.int32, (16, 1), 0)
    chip = row // 8
    place = row % 8 - nc
    column = lax.broadcasted_iota(jnp.int32, (16, chips * 8), 1)
    own = column == (low + chip * dp_size) * 8 + place
    live_here = (place >= 0) & (place < nc) & (chip * nc + place < count[0])
    own_logit = jnp.sum(jnp.where(own, logits, 0.0), axis=1, keepdims=True)
    pair_out[...] = jnp.broadcast_to(
        jnp.where(live_here, highest + jnp.log(total) - own_logit, 0.0), (16, 128)
    )
    weighting = jnp.where(live_here, e / total - own.astype(F32), 0.0) * (SEQ / TEMPER)
    g_unit = exact(weighting, keys, ((1,), (0,)))
    g_unit = jnp.where(half == 0, g_unit[nc : 2 * nc], g_unit[8 + nc : 8 + 2 * nc])
    g_pooled = rate_q * (g_unit - unit_q * jnp.sum(unit_q * g_unit, axis=1, keepdims=True))
    grad_out[...] = g_pooled * inv_q[...]


ROWS = D // 8
VEC_ROWS = 16
CODE_TOP = 32000.0
FIRST_SLOT = (0, 8, 12, 14)


def backward(dp_size, nc, *refs):
    refs = list(refs)

    def take(n):
        return [refs.pop(0) for _ in range(n)]

    meta, g_sum = take(2)
    names = ("hidden", "proj", "probs", "mixed", "v1", "normed", "active", "slope", "v2")
    saves = dict(zip(names, take(9)))
    blob_a, w_in, w_down, far, gains = take(5)
    query_out, grads_out, vec_out = take(3)
    wf, wa, v_in, sl, act, nm, pj, pr, mx, low, base, part, got_part = take(13)
    temp, kept8, code8, kept4, code4, got, scale8, scale4, got_scale = take(9)
    vec, vec_got = take(2)
    load_sem, out_sem, p_send, p_recv, r_send, r_recv, s_send, s_recv, v_send, v_recv = take(10)

    d = lax.axis_index("dp")
    t = lax.axis_index("tensor")
    core = t & 1
    dp_bits = dp_size.bit_length() - 1
    spare = dp_bits - 3
    m = d >> spare
    share = query_out.shape[0]
    width = mx.shape[2]
    heads = width // HEAD
    far_id, core_id = (d, t ^ 2), (d, t ^ 1)
    bit_ids = [(d ^ (1 << k), t) for k in range(dp_bits)]
    top_ids = bit_ids[spare:]
    everyone = [far_id] + bit_ids + [core_id]
    greet(everyone)

    def remote(src, dst, send, recv, device):
        return pltpu.make_async_remote_copy(
            src_ref=src,
            dst_ref=dst,
            send_sem=send,
            recv_sem=recv,
            device_id=device,
            device_id_type=MESH,
        )

    def loads(name, layer):
        pairs = {
            "v1": [(saves["v1"].at[layer], v_in)],
            "v2": [(saves["v2"].at[layer], v_in)],
            "slope": [(saves["slope"].at[layer], sl)],
            "active": [(saves["active"].at[layer], act)],
            "normed": [(saves["normed"].at[layer], nm)],
            "hidden": [(saves["hidden"].at[layer], nm)],
            "proj": [(saves["proj"].at[layer], pj)],
            "probs": [(saves["probs"].at[layer], pr)],
            "mixed": [(saves["mixed"].at[layer], mx)],
            "wf": [
                (w_in.at[layer], wf.at[0, 0]),
                (w_down.at[layer], wf.at[0, 1]),
                (far.at[layer, pl.ds(1, 2)], wf.at[1]),
            ],
            "wa": [(blob_a.at[layer], wa.at[0]), (far.at[layer, 0], wa.at[1])],
        }[name]
        at = ("v1", "v2", "slope", "active", "normed", "hidden", "proj", "probs", "mixed", "wf", "wa").index(name)
        return [
            pltpu.make_async_copy(s, o, load_sem.at[at, k]) for k, (s, o) in enumerate(pairs)
        ]

    def load(layer, *which):
        for name in which:
            for copy in loads(name, layer):
                copy.start()

    def loaded(layer, *which):
        for name in which:
            for copy in loads(name, layer):
                copy.wait()

    top = LAYERS - 1
    load(top, "v2", "wf", "slope", "active", "normed", "probs", "proj", "wa", "mixed")
    vec[0] = jnp.zeros_like(vec[0])

    def block(i):
        return pl.ds(pl.multiple_of(i * SEQ, SEQ), SEQ)

    def add_row(at, value):
        vec[0, pl.ds(at, 1), :] += value

    sent = []

    def exchange(k, slot):
        return remote(part, got_part.at[slot], p_send.at[k], p_recv.at[k], core_id)

    def send_part(k, slot):
        copy = exchange(k, slot)
        copy.start()
        sent.append(copy)

    def free_part():
        while sent:
            sent.pop().wait_send()

    orders = (("y", 0, 1, 2), (0, "y", 1, 2), (1, "y", 0, 2))

    def stage(blob, k):
        kind = blob % 3
        bit = orders[kind][k]
        device = far_id if bit == "y" else top_ids[bit]
        n = 8 >> k
        src = code8.at[kind] if k == 0 else code4.at[kind, pl.ds(0, n)]
        src_scale = scale8.at[kind] if k == 0 else scale4.at[kind, pl.ds(0, n)]
        slots = pl.ds(FIRST_SLOT[k], n)
        return (
            remote(src, got.at[blob, slots], r_send.at[blob, k], r_recv.at[blob, k], device),
            remote(src_scale, got_scale.at[blob, slots], s_send.at[blob, k], s_recv.at[blob, k], device),
        ), n

    def encode(x, codes, scales, kind, slot):
        high = jnp.maximum(jnp.max(jnp.abs(x)), 1e-30)
        codes[kind, slot] = jnp.round(x * (CODE_TOP / high)).astype(jnp.int32).astype(jnp.int16)
        scales[kind, slot] = jnp.full((8, 128), 1.0 / CODE_TOP, F32) * high

    def decode(blob, slot):
        return got[blob, slot].astype(jnp.int32).astype(F32) * got_scale[blob, slot, 0:1, 0:1]

    def relative(kind, s, sub, flag):
        if kind == 0:
            return ((sub >> 2) & 1) | (((sub >> 1) & 1) << 1) | ((sub & 1) << 2)
        if kind == 1:
            return flag | (((sub >> 1) & 1) << 1) | ((sub & 1) << 2)
        return (flag << 1) | ((sub >> 1) & 1) | ((sub & 1) << 2)

    def chunk(r):
        return temp[pl.ds(pl.multiple_of((r ^ m) * ROWS, 16), ROWS), :]

    def loop(n, body):
        lax.fori_loop(0, n, lambda i, _: (body(i), 0)[1], 0)

    def split(kind, s):
        if kind == 0:
            if s == 1:
                loop(8, lambda j: encode(chunk(relative(0, 1, j, 0)), code8, scale8, kind, j))
            else:

                def keep(j):
                    kept8[kind, j] = chunk(relative(0, 0, j, 0))

                loop(8, keep)
        else:

            def both(j):
                encode(chunk(relative(kind, s, j, 1)), code8, scale8, kind, s * 4 + j)
                kept8[kind, s * 4 + j] = chunk(relative(kind, s, j, 0))

            loop(4, both)

    flying = {}
    out_copies = {}

    def start_stage(blob, k):
        copies, _ = stage(blob, k)
        for copy in copies:
            copy.start()
        flying[blob, k] = copies

    def end_stage(blob, k):
        for copy in flying.pop((blob, k), ()):
            copy.wait_send()

    def receive(blob, k):
        kind = blob % 3
        copies, n = stage(blob, k)
        for copy in copies:
            copy.wait_recv()
        kept = kept8 if k == 0 else kept4
        half = n // 2
        if k > 0:
            end_stage(blob, k)
        if half:

            def send_on(j):
                x = kept[kind, half + j] + decode(blob, FIRST_SLOT[k] + half + j)
                encode(x, code4, scale4, kind, j)

            loop(half, send_on)
            start_stage(blob, k + 1)
            if k == 0 and kind in out_copies:
                out_copies.pop(kind).wait()

            def stay(j):
                kept4[kind, j] = kept[kind, j] + decode(blob, FIRST_SLOT[k] + j)

            loop(half, stay)
            if k == 0:
                end_stage(blob, 0)
        else:
            kept4[kind, 3] = kept[kind, 0] + decode(blob, FIRST_SLOT[k])
            out_copies[kind] = pltpu.make_async_copy(
                kept4.at[kind, 3], grads_out.at[blob], out_sem.at[kind]
            )
            out_copies[kind].start()

    def nothing(i):
        pass

    def ffn_back(layer, pump=nothing):
        is_top = layer == top
        loaded(layer, "v2", "slope", "wf")
        if not is_top:
            exchange(2 * (top - layer) - 1, 1).wait_recv()
        free_part()
        at = VEC_ROWS * layer

        def body(i):
            r = block(i)
            if is_top:
                visible = lax.broadcasted_iota(jnp.int32, (SEQ, 1), 0) < meta[i]
                g = jnp.where(visible, g_sum[pl.ds(i, 1), :], 0.0)
            else:
                g = base[r, :] + got_part[1, r, :].astype(F32)
            gain = gains[layer, 1:2, :]
            xh, rate, _ = norm(v_in[r, :], gain, 0.0)
            gc = norm_back(g, xh, rate, gain)
            add_row(at + 1, rows(g * xh))
            add_row(at + 5, rows(g))
            add_row(at + 4, rows(gc))
            g_low = gc.astype(BF)
            low[r, :] = g_low
            total = None
            for s in range(2):
                inner = (mm_nt(g_low, wf[s, 1]) * sl[s, r, :].astype(F32)).astype(BF)
                sl[s, r, :] = inner
                add_row(at + 6 + (t ^ (2 * s)), rows(inner.astype(F32)))
                term = mm_nt(inner, wf[s, 0])
                total = term if total is None else total + term
            base[r, :] = gc + total
            part[r, :] = total.astype(BF)
            pump(i)

        loop(nc, body)
        send_part(2 * (top - layer), 0)
        load(layer, "v1")
        if layer > 0:
            load(layer - 1, "wf")

    def ffn_grads(layer):
        loaded(layer, "active", "normed")
        blob = 3 * (top - layer)
        temp[...] = mm_tn(nm[...], sl[1])
        split(0, 1)
        start_stage(blob, 0)
        for s in range(2):
            temp[...] = mm_tn(low[...], act[s])
            split(1, s)
        start_stage(blob + 1, 0)
        temp[...] = mm_tn(nm[...], sl[0])
        split(0, 0)
        load(layer, "hidden")
        if layer > 0:
            load(layer - 1, "slope", "active")

    def attn_back(layer, pump=nothing):
        loaded(layer, "v1", "proj", "probs", "wa")
        exchange(2 * (top - layer), 0).wait_recv()
        free_part()
        at = VEC_ROWS * layer

        def body(i):
            r = block(i)
            g = base[r, :] + got_part[0, r, :].astype(F32)
            gain = gains[layer, 0:1, :]
            xh, rate, _ = norm(v_in[r, :], gain, 0.0)
            gr = norm_back(g, xh, rate, gain)
            add_row(at, rows(g * xh))
            add_row(at + 3, rows(g))
            add_row(at + 2, rows(gr))
            g_low = gr.astype(BF)
            low[r, :] = g_low
            total = None
            for s in range(2):
                g_mixed = mm_nt(g_low, wa[s, 3 * width : 4 * width, :]).astype(BF)
                here = pj[s, r, :]
                parts = [[], [], []]
                for h in range(heads):
                    queries = here[:, h * HEAD : (h + 1) * HEAD]
                    keys = here[:, width + h * HEAD : width + (h + 1) * HEAD]
                    values = here[:, 2 * width + h * HEAD : 2 * width + (h + 1) * HEAD]
                    gm = g_mixed[:, h * HEAD : (h + 1) * HEAD]
                    p_low = pr[s, i, h]
                    p = p_low.astype(F32)
                    gp = mm_nt(gm, values)
                    gs = (p * (gp - jnp.sum(p * gp, axis=1, keepdims=True))).astype(BF)
                    parts[0].append((mm(gs, keys) * SCALE).astype(BF))
                    parts[1].append((mm_tn(gs, queries) * SCALE).astype(BF))
                    parts[2].append(mm_tn(p_low, gm).astype(BF))
                g_proj = jnp.concatenate(parts[0] + parts[1] + parts[2], axis=1)
                pj[s, r, :] = g_proj
                vec[0, pl.ds(at + 10 + (t ^ (2 * s)), 1), 0 : 3 * width] += rows(g_proj.astype(F32))
                term = mm(g_proj, wa[s, 0 : 3 * width, :])
                total = term if total is None else total + term
            base[r, :] = gr + total
            part[r, :] = total.astype(BF)
            pump(i)

        loop(nc, body)
        send_part(2 * (top - layer) + 1, 1)
        if layer > 0:
            load(layer - 1, "v2", "probs", "wa")

    def attn_grads(layer):
        loaded(layer, "hidden", "mixed")
        blob = 3 * (top - layer) + 2
        for s in range(2):
            temp[:, 0 : 3 * width] = mm_tn(nm[...], pj[s])
            temp[:, 3 * width : 4 * width] = mm_tn(low[...], mx[s])
            split(2, s)
        start_stage(blob, 0)
        if layer > 0:
            load(layer - 1, "proj", "mixed", "normed")

    vec_copies = []

    def vec_start(s):
        copy = remote(vec.at[0], vec_got.at[s], v_send.at[s], v_recv.at[s], everyone[s])
        copy.start()
        vec_copies.append(copy)

    def vec_next(s):
        vec_copies[s].wait()
        vec[0] = vec[0] + vec_got[s]
        if s + 1 < len(everyone):
            vec_start(s + 1)

    def pumps(table):
        def pump(i):
            for at, actions in table.items():

                @pl.when(i == at)
                def _():
                    for blob, k in actions:
                        receive(blob, k)

        return pump

    ffn_back(1)
    ffn_grads(1)
    attn_back(1)
    attn_grads(1)
    ffn_back(0)
    receive(0, 0)
    receive(1, 0)
    ffn_grads(0)
    receive(0, 1)
    receive(1, 1)
    attn_back(0)
    first = jnp.where((lax.broadcasted_iota(jnp.int32, (LAYERS * VEC_ROWS, D), 0) % VEC_ROWS >= 6) | (core == 0), 1.0, 0.0)
    vec[0] = vec[0] * first
    vec_start(0)
    receive(2, 0)
    receive(0, 2)
    receive(1, 2)
    attn_grads(0)
    receive(0, 3)
    receive(1, 3)
    vec_next(0)
    receive(3, 0)
    receive(4, 0)
    receive(2, 1)
    vec_next(1)
    receive(2, 2)
    receive(3, 1)
    receive(4, 1)
    vec_next(2)
    receive(2, 3)
    receive(5, 0)
    vec_next(3)
    receive(3, 2)
    receive(4, 2)
    for s in range(4, len(everyone)):
        vec_next(s)
    receive(5, 1)
    receive(3, 3)
    receive(4, 3)
    receive(5, 2)
    exchange(2 * LAYERS - 1, 1).wait_recv()
    mine = pl.ds(pl.multiple_of(core * share, 16), share)
    v_in[0:share, :] = base[mine, :] + got_part[1, mine, :].astype(F32)
    query_copy = pltpu.make_async_copy(v_in.at[0:share], query_out, out_sem.at[3])
    query_copy.start()
    receive(5, 3)
    query_copy.wait()
    for copy in out_copies.values():
        copy.wait()
    vec_out[...] = vec[0]
    free_part()
    for blob, k in list(flying):
        end_stage(blob, k)


SMEM = pl.BlockSpec(memory_space=pltpu.SMEM)


def on_device(mesh_shape, *args):
    (
        query_input,
        key_input,
        query_length,
        key_length,
        pair_count,
    ) = args[:5]
    encoders = (args[5:13], args[13:21])
    dp_size = mesh_shape["dp"]
    dp_bits = dp_size.bit_length() - 1
    d_pos = lax.axis_index("dp")
    t_pos = lax.axis_index("tensor")
    quarter = d_pos & 3
    core = t_pos & 1
    half = t_pos // 2
    share = query_input.shape[0]
    total_rows = 2 * share
    nc = total_rows // SEQ
    width = args[5].shape[3]

    blob_a = [
        jnp.concatenate(
            [w[0].transpose(0, 2, 3, 1).reshape(LAYERS, 3 * width, D), w[2]], axis=1
        )
        for w in encoders
    ]
    bias_rows = []
    for w in encoders:
        zero = jnp.zeros((LAYERS, width), F32)
        bias_rows += [jnp.concatenate([w[1][:, 0], zero, w[1][:, 1], zero], axis=1), w[4]]
    bias = jnp.concatenate(bias_rows, axis=0)
    lengths = [
        lax.dynamic_slice(v, (half * nc,), (nc,)) for v in (query_length, key_length)
    ]
    meta = jnp.concatenate(lengths)
    inverse = [(1.0 / v.astype(F32))[:, None] for v in lengths]
    big = (total_rows, D)
    heads = width // HEAD
    unit_flops = 2 * total_rows * D
    vmem = pl.BlockSpec(memory_space=pltpu.VMEM)
    hbm = pl.BlockSpec(memory_space=pl.ANY)
    hops = dp_bits + 1
    n_groups = 4 * LAYERS
    shaped = jax.ShapeDtypeStruct
    sem = pltpu.SemaphoreType.DMA
    rows_of = lambda *s: (LAYERS,) + s
    results = pl.pallas_call(
        functools.partial(forward, dp_size, nc),
        in_specs=[SMEM] * 2 + [hbm] * 8 + [vmem] * 7,
        out_specs=[hbm] * 10 + [vmem] * 2,
        out_shape=[
            shaped(rows_of(total_rows, D), BF),
            shaped(rows_of(2, total_rows, 3 * width), BF),
            shaped(rows_of(2, nc, heads, SEQ, SEQ), BF),
            shaped(rows_of(2, total_rows, width), BF),
            shaped(rows_of(total_rows, D), F32),
            shaped(rows_of(total_rows, D), BF),
            shaped(rows_of(2, total_rows, BLOB), BF),
            shaped(rows_of(2, total_rows, BLOB), BF),
            shaped(rows_of(total_rows, D), F32),
            shaped(rows_of(3, BLOB, D), BF),
            shaped((16, 128), F32),
            shaped((nc, D), F32),
        ],
        scratch_shapes=[
            pltpu.VMEM((2,) + big, BF),
            pltpu.VMEM((2,) + big, F32),
            pltpu.VMEM((2,) + big, F32),
            pltpu.VMEM((2,) + big, BF),
            pltpu.VMEM((2, 2) + big, BF),
            pltpu.VMEM((2, BLOB, D), BF),
            pltpu.VMEM((2, 2, BLOB, D), BF),
            pltpu.VMEM((2 * LAYERS, 3, BLOB, D), BF),
            pltpu.VMEM(big, F32),
            pltpu.VMEM((2, total_rows, 3 * width), BF),
            pltpu.VMEM((2, nc, heads, SEQ, SEQ), BF),
            pltpu.VMEM((2, total_rows, width), BF),
            pltpu.VMEM((2, total_rows, BLOB), BF),
            pltpu.VMEM((2, total_rows, BLOB), BF),
            pltpu.VMEM(bias.shape, F32),
            pltpu.VMEM((2, 8, D), F32),
            pltpu.VMEM((2 * dp_size, 8, D + 128), F32),
            sem((n_groups, 8)),
            sem((n_groups, 8)),
            sem((2, 2 * LAYERS)),
            sem((2, 2 * LAYERS)),
            sem((2,)),
            sem((2,)),
            sem((2, 4)),
            sem((9 + 2 * LAYERS,)),
            sem((hops,)),
            sem((hops,)),
            sem((2,)),
        ],
        compiler_params=pltpu.CompilerParams(
            collective_id=0, has_side_effects=True, vmem_limit_bytes=int(60.5 * MIB)
        ),
        cost_estimate=pl.CostEstimate(
            flops=unit_flops * 80 * BLOB // 4, bytes_accessed=100 * MIB, transcendentals=0
        ),
        name="forward",
    )(
        meta,
        pair_count,
        query_input,
        key_input,
        *blob_a,
        encoders[0][3],
        encoders[1][3],
        encoders[0][5],
        encoders[1][5],
        encoders[0][6],
        encoders[1][6],
        encoders[0][7],
        encoders[1][7],
        bias,
        *inverse,
    )
    far, pair_rows, g_sum = results[9:]
    per_pair = jnp.concatenate([pair_rows[nc : 2 * nc, 0], pair_rows[8 + nc : 8 + 2 * nc, 0]])

    n_peers = dp_bits + 2
    mat = (BLOB, D)
    blobs = 3 * LAYERS
    query_grad, grads, summed = pl.pallas_call(
        functools.partial(backward, dp_size, nc),
        in_specs=[SMEM, vmem] + [hbm] * 13 + [vmem],
        out_specs=[hbm, hbm, vmem],
        out_shape=[
            shaped((share, D), F32),
            shaped((blobs, ROWS, BLOB), F32),
            shaped((LAYERS * VEC_ROWS, D), F32),
        ],
        scratch_shapes=[
            pltpu.VMEM((2, 2) + mat, BF),
            pltpu.VMEM((2,) + mat, BF),
            pltpu.VMEM(big, F32),
            pltpu.VMEM((2, total_rows, BLOB), BF),
            pltpu.VMEM((2, total_rows, BLOB), BF),
            pltpu.VMEM(big, BF),
            pltpu.VMEM((2, total_rows, 3 * width), BF),
            pltpu.VMEM((2, nc, heads, SEQ, SEQ), BF),
            pltpu.VMEM((2, total_rows, width), BF),
            pltpu.VMEM(big, BF),
            pltpu.VMEM(big, F32),
            pltpu.VMEM(big, BF),
            pltpu.VMEM((2,) + big, BF),
            pltpu.VMEM((D, BLOB), F32),
            pltpu.VMEM((3, 8, ROWS, BLOB), F32),
            pltpu.VMEM((3, 8, ROWS, BLOB), jnp.int16),
            pltpu.VMEM((3, 4, ROWS, BLOB), F32),
            pltpu.VMEM((3, 4, ROWS, BLOB), jnp.int16),
            pltpu.VMEM((blobs, 15, ROWS, BLOB), jnp.int16),
            pltpu.VMEM((3, 8, 8, 128), F32),
            pltpu.VMEM((3, 4, 8, 128), F32),
            pltpu.VMEM((blobs, 15, 8, 128), F32),
            pltpu.VMEM((1, LAYERS * VEC_ROWS, D), F32),
            pltpu.VMEM((n_peers, LAYERS * VEC_ROWS, D), F32),
            sem((11, 3)),
            sem((4,)),
            sem((2 * LAYERS,)),
            sem((2 * LAYERS,)),
            sem((blobs, 4)),
            sem((blobs, 4)),
            sem((blobs, 4)),
            sem((blobs, 4)),
            sem((n_peers,)),
            sem((n_peers,)),
        ],
        compiler_params=pltpu.CompilerParams(
            collective_id=1, has_side_effects=True, vmem_limit_bytes=int(62 * MIB)
        ),
        cost_estimate=pl.CostEstimate(
            flops=unit_flops * 40 * BLOB // 2, bytes_accessed=60 * MIB, transcendentals=0
        ),
        name="backward",
    )(meta, g_sum, *results[:9], blob_a[0], encoders[0][3], encoders[0][5], far, encoders[0][6])

    rows_left = ROWS
    for bit in reversed(range(dp_bits - 3)):
        rows_left //= 2
        pair = grads.reshape(blobs, 2, rows_left, BLOB)
        mine = (d_pos >> bit) & 1
        send = lax.dynamic_index_in_dim(pair, 1 - mine, 1, keepdims=False)
        grads = lax.dynamic_index_in_dim(pair, mine, 1, keepdims=False) + lax.ppermute(
            send, "dp", [(i, i ^ (1 << bit)) for i in range(dp_size)]
        )
    by_layer = [grads[3 * (LAYERS - 1 - layer) :][:3] for layer in range(LAYERS)]
    grad_in, grad_down, attn = [jnp.stack([g[k] for g in by_layer]) for k in range(3)]
    summed = summed.reshape(LAYERS, VEC_ROWS, D)
    qv = summed[:, 10:14].reshape(LAYERS, 4, 4, width)
    grad_qv_bias = jnp.stack(
        [qv[:, :, 0].reshape(LAYERS, 4 * width), qv[:, :, 2].reshape(LAYERS, 4 * width)], axis=1
    )
    return (
        per_pair,
        query_grad,
        attn[:, :, : 3 * width].reshape(LAYERS, D // dp_size, 3, width),
        attn[:, :, 3 * width :].transpose(0, 2, 1),
        grad_in,
        grad_down.transpose(0, 2, 1),
        grad_qv_bias,
        summed[:, 6:10].reshape(LAYERS, 4 * BLOB),
        summed[:, 0:2],
        summed[:, 2:6],
    )


def solution(mesh):
    split = P(("dp", "tensor"), None)
    weights = (
        P(None, None, None, "tensor"),
        P(None, None, "tensor"),
        P(None, "tensor", None),
        P(None, None, "tensor"),
        P(None, "tensor"),
        P(None, "tensor", None),
        P(),
        P(),
    )
    return jax.shard_map(
        functools.partial(on_device, dict(mesh.shape)),
        mesh=mesh,
        in_specs=(split, split, P("dp"), P("dp"), P("dp")) + weights + weights,
        out_specs=(
            P("dp"),
            split,
            P(None, "dp", None, "tensor"),
            P(None, "tensor", "dp"),
            P(None, "dp", "tensor"),
            P(None, "tensor", "dp"),
            P(),
            P(),
            P(),
            P(),
        ),
        check_vma=False,
    )
```

```python
import functools
import math

import jax
import jax.numpy as jnp
from jax import lax
from jax.experimental import pallas as pl
from jax.experimental.pallas import tpu as pltpu
from jax.sharding import PartitionSpec as P

D = 768
HEAD = 64
SEQ = 256
LAYERS = 2
BLOB = 768
EPS = 1e-06
TEMPER = 0.05
FILL = -1e30
BF = jnp.bfloat16
F32 = jnp.float32
MESH = pl.DeviceIdType.MESH
SCALE = HEAD ** (-0.5)
MIB = 2**20


def mm(a, b):
    return jnp.dot(a, b, preferred_element_type=F32)


def mm_nt(a, b):
    return lax.dot_general(a, b, (((1,), (1,)), ((), ())), preferred_element_type=F32)


def mm_tn(a, b):
    return lax.dot_general(a, b, (((0,), (0,)), ((), ())), preferred_element_type=F32)


def norm(v, gain, shift):
    center = v - jnp.mean(v, axis=-1, keepdims=True)
    rate = lax.rsqrt(jnp.mean(center * center, axis=-1, keepdims=True) + EPS)
    xhat = center * rate
    return xhat, rate, xhat * gain + shift


def norm_back(g, xhat, rate, gain):
    gx = g * gain
    return rate * (
        gx
        - jnp.mean(gx, axis=-1, keepdims=True)
        - xhat * jnp.mean(gx * xhat, axis=-1, keepdims=True)
    )


def rows(v):
    return jnp.sum(v, axis=0, keepdims=True)


PLAN = (
    ('AO', 0, 0, ()),
    ('AO', 1, 0, ((1, 1, 0),)),
    (1, 1),
    (2, 0),
    (1, 2),
    (2, 1),
    (3, 0),
    ('AF', 0, 0, ((1, 1, 3),)),
    (2, 2),
    (3, 1),
    ('AF', 1, 0, ((1, 1, 4),)),
    ('FO', 0, 0, ((0, 2, 3),)),
    ('FO', 1, 0, ((0, 1, 5), (2, 2, 4))),
    (3, 2),
    (3, 3),
    ('FF', 0, 0, ((1, 1, 6),)),
    (2, 5),
    (3, 4),
    (1, 7),
    (2, 6),
    (3, 5),
    ('FF', 1, 0, ((1, 1, 8),)),
    ('AO', 0, 1, ((0, 2, 7),)),
    ('AO', 1, 1, ((0, 1, 9), (2, 2, 8))),
    (3, 6),
    ('AF', 0, 1, ((1, 1, 10),)),
    (3, 7),
    ('AF', 1, 1, ((0, 2, 9),)),
    ('FO', 0, 1, ((0, 1, 11), (1, 2, 10))),
    ('FO', 1, 1, ()),
    (3, 8),
    (3, 9),
    ('FF', 0, 1, ((1, 2, 11),)),
    (3, 10),
    (3, 11),
    ('FF', 1, 1, ()),
)
GROUPS = (
    (0, 0, 0),
    (0, 1, 0),
    (0, 0, 1),
    (0, 0, 2),
    (0, 1, 1),
    (0, 1, 2),
    (1, 0, 0),
    (1, 1, 0),
    (1, 0, 1),
    (1, 0, 2),
    (1, 1, 1),
    (1, 1, 2),
)
T_DELAY = 2


def forward(dp_size, nc, *refs):
    refs = list(refs)

    def take(n):
        return [refs.pop(0) for _ in range(n)]

    meta, count = take(2)
    x_in, blob_a, w_in, w_down, gains, shifts = [take(2) for _ in range(6)]
    bias, inv_q, inv_k = take(3)
    saves = dict(
        zip(("hidden", "proj", "probs", "mixed", "v1", "normed", "active", "slope", "v2"), take(9))
    )
    far_out, pair_out, grad_out = take(3)
    low, base, acc, send, recv, own_a, own_f, far = take(8)
    v_st, proj_st, probs_st, mixed_st, active_st, slope_st = take(6)
    far_bias, sums, held = take(3)
    y_send, y_recv, p_send, p_recv, x_send, x_recv, own_sem, save_sem, c_send, c_recv, b_sem = take(11)

    d = lax.axis_index("dp")
    t = lax.axis_index("tensor")
    core = t & 1
    half = t // 2
    q = d & 3
    share = x_in[0].shape[0]
    far_id, core_id, x_id, z_id = (d, t ^ 2), (d, t ^ 1), (d ^ 1, t), (d ^ 2, t)
    dp_bits = dp_size.bit_length() - 1
    bit_ids = [(d ^ (1 << k), t) for k in reversed(range(dp_bits))] + [far_id]
    greet(bit_ids + [core_id])

    def remote(src, dst, sems, at, device):
        return pltpu.make_async_remote_copy(
            src_ref=src,
            dst_ref=dst,
            send_sem=sems[0].at[at],
            recv_sem=sems[1].at[at],
            device_id=device,
            device_id_type=MESH,
        )

    mine = pl.ds(pl.multiple_of(core * share, 16), share)
    x_local = []
    x_remote = []
    for e in range(2):
        x_local.append(pltpu.make_async_copy(x_in[e], low.at[e, mine], own_sem.at[e, 2]))
        x_remote.append(remote(x_in[e], low.at[e, mine], (x_send, x_recv), e, core_id))

    def load_a(e, layer):
        return [pltpu.make_async_copy(blob_a[e].at[layer], own_a.at[e], own_sem.at[e, 0])]

    def load_f(e, layer):
        return [
            pltpu.make_async_copy(w_in[e].at[layer], own_f.at[e, 0], own_sem.at[e, 1]),
            pltpu.make_async_copy(w_down[e].at[layer], own_f.at[e, 1], own_sem.at[e, 3]),
        ]

    x_local[0].start()
    x_remote[0].start()
    for copy in load_a(0, 0):
        copy.start()
    b_copy = pltpu.make_async_remote_copy(
        src_ref=bias,
        dst_ref=far_bias,
        send_sem=b_sem.at[0],
        recv_sem=b_sem.at[1],
        device_id=far_id,
        device_id_type=MESH,
    )
    b_copy.start()
    x_local[1].start()
    x_remote[1].start()
    for copy in load_a(1, 0) + load_f(0, 0) + load_f(1, 0):
        copy.start()

    n = BLOB // 4
    third = n // 3
    moves = []
    for g, (layer, e, which) in enumerate(GROUPS):

        def at(quarter, start, size):
            row = pl.ds(pl.multiple_of(quarter * n + start, 16), size)
            return far.at[layer * 2 + e, which, row]

        def source(quarter, size):
            row = pl.ds(pl.multiple_of(quarter * n, 16), size)
            return (blob_a, w_in, w_down)[which][e].at[layer, row]

        def move(src, dst, k, device):
            return remote(src, dst, (y_send, y_recv), (g, k), device)

        made = (
            move(source(q, n), at(q, 0, n), 0, far_id),
            move(source(q ^ 3, third), at(q ^ 3, 0, third), 1, far_id),
            move(at(q, 0, n), at(q, 0, n), 2, x_id),
            move(at(q, 0, n), at(q, 0, n), 3, z_id),
            move(at(q ^ 2, third, third), at(q ^ 2, third, third), 4, x_id),
            move(at(q ^ 1, 2 * third, third), at(q ^ 1, 2 * third, third), 5, z_id),
        )
        got = made[:2] + (
            move(at(q ^ 1, 0, n), at(q ^ 1, 0, n), 2, x_id),
            move(at(q ^ 2, 0, n), at(q ^ 2, 0, n), 3, z_id),
            move(at(q ^ 3, third, third), at(q ^ 3, third, third), 4, x_id),
            move(at(q ^ 3, 2 * third, third), at(q ^ 3, 2 * third, third), 5, z_id),
        )
        moves.append((made, got))

    for g in range(len(GROUPS) + T_DELAY):
        if g < len(GROUPS):
            moves[g][0][0].start()
        if g >= T_DELAY:
            moves[g - T_DELAY][0][1].start()

    def stage(k, g):
        made, got = moves[g]
        if k == 1:
            got[0].wait_recv()
            made[2].start()
            made[3].start()
        elif k == 2:
            got[2].wait_recv()
            got[3].wait_recv()
            made[4].start()
            made[5].start()
        else:
            got[1].wait_recv()
            got[4].wait_recv()
            got[5].wait_recv()
            layer, e, which = GROUPS[g]
            if e == 0:
                copy = pltpu.make_async_copy(
                    far.at[2 * layer, which], far_out.at[layer, which], save_sem.at[9 + 3 * layer + which]
                )
                copy.start()
                far_copies.append(copy)

    far_copies = []

    def save(name, layer, src, k):
        return pltpu.make_async_copy(src, saves[name].at[layer], save_sem.at[k])

    pending = {}

    def start_save(name, layer, src):
        k = list(saves).index(name)
        copy = save(name, layer, src, k)
        copy.start()
        pending[name] = copy

    def end_save(*names):
        for name in names:
            if name in pending:
                pending.pop(name).wait()

    def block(i):
        return pl.ds(pl.multiple_of(i * SEQ, SEQ), SEQ)

    def part(e, k):
        return remote(send.at[e], recv.at[e, k % 2], (p_send.at[e], p_recv.at[e]), k, core_id)

    sent = {}

    def send_part(e, k):
        sent[e] = part(e, k)
        sent[e].start()

    width = proj_st.shape[2] // 3
    heads = width // HEAD

    def attn_part(e, s, w, x_low, i, layer):
        b = (bias, far_bias)[s]
        r = block(i)
        proj = (mm_nt(x_low, w[: 3 * width, :]) + b[e * 4 + layer : e * 4 + layer + 1, : 3 * width]).astype(BF)
        visible = lax.broadcasted_iota(jnp.int32, (1, SEQ), 1) < meta[e * nc + i]
        mixed = []
        for h in range(heads):
            queries = proj[:, h * HEAD : (h + 1) * HEAD]
            keys = proj[:, width + h * HEAD : width + (h + 1) * HEAD]
            values = proj[:, 2 * width + h * HEAD : 2 * width + (h + 1) * HEAD]
            scores = jnp.where(visible, mm_nt(queries, keys) * SCALE, FILL)
            ex = jnp.exp(scores - jnp.max(scores, axis=1, keepdims=True))
            probs = (ex * (1.0 / jnp.sum(ex, axis=1, keepdims=True))).astype(BF)
            if e == 0:
                probs_st[s, i, h] = probs
            mixed.append(mm(probs, values).astype(BF))
        mixed = jnp.concatenate(mixed, axis=1)
        if e == 0:
            proj_st[s, r, :] = proj
            mixed_st[s, r, :] = mixed
        return mm(mixed, w[3 * width : 4 * width, :])

    def ffn_part(e, s, w, x_low, i, layer):
        b = (bias, far_bias)[s]
        r = block(i)
        u = mm(x_low, w[0]) + b[e * 4 + 2 + layer : e * 4 + 3 + layer, :]
        portion = 0.5 + 0.5 * lax.erf(u * (0.5**0.5))
        active = (u * portion).astype(BF)
        if e == 0:
            active_st[s, r, :] = active
            slope_st[s, r, :] = (
                portion + u * (jnp.exp(-0.5 * u * u) * ((2 * math.pi) ** -0.5))
            ).astype(BF)
        return mm(active, w[1])

    def crops(body, hooks):
        def step(i, _):
            body(i)
            for c in range(nc - 1):
                due = [h[1:] for h in hooks if h[0] == c]
                if due:

                    @pl.when(i == c)
                    def _():
                        for k, g in due:
                            stage(k, g)

            return 0

        lax.fori_loop(0, nc, step, 0)
        for c, k, g in hooks:
            if c >= nc - 1:
                stage(k, g)

    def joined(e, k, r):
        return base[e, r, :] + (send[e, r, :].astype(F32) + recv[e, k % 2, r, :].astype(F32))

    def attn_own(e, layer, hooks):
        for copy in load_a(e, layer):
            copy.wait()
        if layer == 0:
            x_local[e].wait()
            x_remote[e].wait_recv()
        else:
            part(e, 2 * layer - 1).wait_recv()
        if e == 0:
            end_save("v1", "normed", "proj", "probs", "mixed")

        def body(i):
            r = block(i)
            if layer == 0:
                x_low = low[e, r, :]
                x = x_low.astype(F32)
            else:
                v = joined(e, 2 * layer - 1, r)
                if e == 0:
                    v_st[r, :] = v
                x = norm(v, gains[e][layer - 1, 1:2, :], shifts[e][layer - 1, 3:4, :])[2]
                x_low = x.astype(BF)
                low[e, r, :] = x_low
            base[e, r, :] = x + shifts[e][layer, 0:1, :]
            acc[e, r, :] = attn_part(e, 0, own_a.at[e], x_low, i, layer)

        crops(body, hooks)
        if layer + 1 < LAYERS:
            for copy in load_a(e, layer + 1):
                copy.start()
        if e == 0:
            start_save("hidden", layer, low.at[e])
            if layer > 0:
                start_save("v2", layer - 1, v_st)

    def attn_far(e, layer, hooks):
        if e in sent:
            sent[e].wait_send()

        def body(i):
            r = block(i)
            total = acc[e, r, :] + attn_part(e, 1, far.at[2 * layer + e, 0], low[e, r, :], i, layer)
            send[e, r, :] = total.astype(BF)

        crops(body, hooks)
        send_part(e, 2 * layer)
        if e == 0:
            start_save("proj", layer, proj_st)
            start_save("probs", layer, probs_st)
            start_save("mixed", layer, mixed_st)

    def ffn_own(e, layer, hooks):
        for copy in load_f(e, layer):
            copy.wait()
        part(e, 2 * layer).wait_recv()
        if e == 0:
            end_save("hidden", "v2", "active", "slope")

        def body(i):
            r = block(i)
            v = joined(e, 2 * layer, r)
            if e == 0:
                v_st[r, :] = v
            x = norm(v, gains[e][layer, 0:1, :], shifts[e][layer, 1:2, :])[2]
            x_low = x.astype(BF)
            low[e, r, :] = x_low
            base[e, r, :] = x + shifts[e][layer, 2:3, :]
            acc[e, r, :] = ffn_part(e, 0, own_f.at[e], x_low, i, layer)

        crops(body, hooks)
        if layer + 1 < LAYERS:
            for copy in load_f(e, layer + 1):
                copy.start()
        if e == 0:
            start_save("normed", layer, low.at[e])
            start_save("v1", layer, v_st)

    def ffn_far(e, layer, hooks):
        sent[e].wait_send()

        def body(i):
            r = block(i)
            total = acc[e, r, :] + ffn_part(
                e, 1, far.at[2 * layer + e, pl.ds(1, 2)], low[e, r, :], i, layer
            )
            send[e, r, :] = total.astype(BF)

        crops(body, hooks)
        send_part(e, 2 * layer + 1)
        if e == 0:
            start_save("active", layer, active_st)
            start_save("slope", layer, slope_st)

    def pool(e):
        part(e, 2 * LAYERS - 1).wait_recv()
        if e == 0:
            end_save("v1")

        def body(i):
            r = block(i)
            v = joined(e, 2 * LAYERS - 1, r)
            if e == 0:
                v_st[r, :] = v
            x = norm(v, gains[e][LAYERS - 1, 1:2, :], shifts[e][LAYERS - 1, 3:4, :])[2]
            visible = lax.broadcasted_iota(jnp.int32, (SEQ, 1), 0) < meta[e * nc + i]
            sums[e, pl.ds(i, 1), :] = rows(jnp.where(visible, x, 0.0))

        crops(body, ())
        if e == 0:
            start_save("v2", LAYERS - 1, v_st)

    steps = {"AO": attn_own, "AF": attn_far, "FO": ffn_own, "FF": ffn_far}
    first_far = True
    for entry in PLAN:
        if len(entry) == 2:
            stage(*entry)
        else:
            if entry[0] == "AF" and first_far:
                b_copy.wait_recv()
                first_far = False
            steps[entry[0]](*entry[1:])
    pool(0)
    pool(1)
    contrast(dp_size, nc, d, half, bit_ids, count, inv_q, inv_k, sums, pair_out, grad_out, held, c_send, c_recv, remote)
    end_save(*saves)
    for copy in far_copies:
        copy.wait()
    for e in range(2):
        sent[e].wait_send()
        x_remote[e].wait_send()
    b_copy.wait_send()
    for made, _ in moves:
        for copy in made:
            copy.wait_send()


def greet(partners):
    barrier = pltpu.get_barrier_semaphore()
    for p in partners:
        pl.semaphore_signal(barrier, inc=1, device_id=p, device_id_type=MESH)
    pl.semaphore_wait(barrier, len(partners))


def contrast(
    dp_size, nc, d, half, bit_ids, count, inv_q, inv_k, sums, pair_out, grad_out, held, send, recv, remote
):
    wide = D + 128
    dp_bits = dp_size.bit_length() - 1
    low = jnp.int32(0)
    for k in range(dp_bits):
        low = low + (((d >> (dp_bits - 1 - k)) & 1) << k)
    me = low + half * dp_size

    def unit(s, inv):
        pooled = s * inv
        r = lax.rsqrt(jnp.sum(pooled * pooled, axis=1, keepdims=True) + EPS)
        return pooled * r, r

    unit_q, rate_q = unit(sums[0, 0:nc, :], inv_q[...])
    unit_k, _ = unit(sums[1, 0:nc, :], inv_k[...])
    held[me] = jnp.zeros((8, wide), F32)
    held[me, 0:nc, 0:D] = unit_k
    held[me, nc : 2 * nc, 0:D] = unit_q
    slot = half * nc + lax.broadcasted_iota(jnp.int32, (nc, 128), 0)
    lane = lax.broadcasted_iota(jnp.int32, (nc, 128), 1)
    held[me, 0:nc, D:wide] = jnp.where((slot < count[0]) & (lane == 0), 1.0, 0.0)
    for s, p in enumerate(bit_ids):
        mine = pl.ds((me >> s) << s, 1 << s)
        theirs = pl.ds(((me >> s) ^ 1) << s, 1 << s)
        remote(held.at[mine], held.at[mine], (send, recv), s, p).start()
        remote(held.at[theirs], held.at[theirs], (send, recv), s, p).wait_recv()
    for s, p in enumerate(bit_ids):
        mine = pl.ds((me >> s) << s, 1 << s)
        remote(held.at[mine], held.at[mine], (send, recv), s, p).wait_send()
    chips = held.shape[0]
    every = held[...].reshape(chips * 8, wide)
    keys = every[:, 0:D]
    here = jnp.concatenate([held[low], held[low + dp_size]], axis=0)[:, 0:D]

    def exact(a, b, dims):
        return lax.dot_general(
            a, b, (dims, ((), ())), precision=lax.Precision.HIGHEST, preferred_element_type=F32
        )

    one = jnp.where(lax.broadcasted_iota(jnp.int32, (16, 128), 1) == 0, 1.0, 0.0)
    live = exact(one, every[:, D:wide], ((1,), (1,))) > 0.5
    logits = exact(here, keys, ((1,), (1,))) / TEMPER
    masked = jnp.where(live, logits, FILL)
    highest = jnp.max(masked, axis=1, keepdims=True)
    e = jnp.exp(masked - highest)
    total = jnp.sum(e, axis=1, keepdims=True)
    row = lax.broadcasted_iota(jnp.int32, (16, 1), 0)
    chip = row // 8
    place = row % 8 - nc
    column = lax.broadcasted_iota(jnp.int32, (16, chips * 8), 1)
    own = column == (low + chip * dp_size) * 8 + place
    live_here = (place >= 0) & (place < nc) & (chip * nc + place < count[0])
    own_logit = jnp.sum(jnp.where(own, logits, 0.0), axis=1, keepdims=True)
    pair_out[...] = jnp.broadcast_to(
        jnp.where(live_here, highest + jnp.log(total) - own_logit, 0.0), (16, 128)
    )
    weighting = jnp.where(live_here, e / total - own.astype(F32), 0.0) * (SEQ / TEMPER)
    g_unit = exact(weighting, keys, ((1,), (0,)))
    g_unit = jnp.where(half == 0, g_unit[nc : 2 * nc], g_unit[8 + nc : 8 + 2 * nc])
    g_pooled = rate_q * (g_unit - unit_q * jnp.sum(unit_q * g_unit, axis=1, keepdims=True))
    grad_out[...] = g_pooled * inv_q[...]


ROWS = D // 8
VEC_ROWS = 16
CODE_TOP = 32000.0
FIRST_SLOT = (0, 8, 12, 14)


def backward(dp_size, nc, *refs):
    refs = list(refs)

    def take(n):
        return [refs.pop(0) for _ in range(n)]

    meta, g_sum = take(2)
    names = ("hidden", "proj", "probs", "mixed", "v1", "normed", "active", "slope", "v2")
    saves = dict(zip(names, take(9)))
    blob_a, w_in, w_down, far, gains = take(5)
    query_out, grads_out, vec_out = take(3)
    wf, wa, v_in, sl, act, nm, pj, pr, mx, low, base, part, got_part = take(13)
    temp, kept8, code8, kept4, code4, got, scale8, scale4, got_scale = take(9)
    vec, vec_got = take(2)
    load_sem, out_sem, p_send, p_recv, r_send, r_recv, s_send, s_recv, v_send, v_recv = take(10)

    d = lax.axis_index("dp")
    t = lax.axis_index("tensor")
    core = t & 1
    dp_bits = dp_size.bit_length() - 1
    spare = dp_bits - 3
    m = d >> spare
    share = query_out.shape[0]
    width = mx.shape[2]
    heads = width // HEAD
    far_id, core_id = (d, t ^ 2), (d, t ^ 1)
    bit_ids = [(d ^ (1 << k), t) for k in range(dp_bits)]
    top_ids = bit_ids[spare:]
    everyone = [far_id] + bit_ids + [core_id]
    greet(everyone)

    def remote(src, dst, send, recv, device):
        return pltpu.make_async_remote_copy(
            src_ref=src,
            dst_ref=dst,
            send_sem=send,
            recv_sem=recv,
            device_id=device,
            device_id_type=MESH,
        )

    def loads(name, layer):
        pairs = {
            "v1": [(saves["v1"].at[layer], v_in)],
            "v2": [(saves["v2"].at[layer], v_in)],
            "slope": [(saves["slope"].at[layer], sl)],
            "active": [(saves["active"].at[layer], act)],
            "normed": [(saves["normed"].at[layer], nm)],
            "hidden": [(saves["hidden"].at[layer], nm)],
            "proj": [(saves["proj"].at[layer], pj)],
            "probs": [(saves["probs"].at[layer], pr)],
            "mixed": [(saves["mixed"].at[layer], mx)],
            "wf": [
                (w_in.at[layer], wf.at[0, 0]),
                (w_down.at[layer], wf.at[0, 1]),
                (far.at[layer, pl.ds(1, 2)], wf.at[1]),
            ],
            "wa": [(blob_a.at[layer], wa.at[0]), (far.at[layer, 0], wa.at[1])],
        }[name]
        at = ("v1", "v2", "slope", "active", "normed", "hidden", "proj", "probs", "mixed", "wf", "wa").index(name)
        return [
            pltpu.make_async_copy(s, o, load_sem.at[at, k]) for k, (s, o) in enumerate(pairs)
        ]

    def load(layer, *which):
        for name in which:
            for copy in loads(name, layer):
                copy.start()

    def loaded(layer, *which):
        for name in which:
            for copy in loads(name, layer):
                copy.wait()

    top = LAYERS - 1
    load(top, "v2", "wf", "slope", "active", "normed", "probs", "proj", "wa", "mixed")
    vec[0] = jnp.zeros_like(vec[0])

    def block(i):
        return pl.ds(pl.multiple_of(i * SEQ, SEQ), SEQ)

    def add_row(at, value):
        vec[0, pl.ds(at, 1), :] += value

    sent = []

    def exchange(k, slot):
        return remote(part, got_part.at[slot], p_send.at[k], p_recv.at[k], core_id)

    def send_part(k, slot):
        copy = exchange(k, slot)
        copy.start()
        sent.append(copy)

    def free_part():
        while sent:
            sent.pop().wait_send()

    orders = (("y", 0, 1, 2), (0, "y", 1, 2), (1, "y", 0, 2))

    def stage(blob, k):
        kind = blob % 3
        bit = orders[kind][k]
        device = far_id if bit == "y" else top_ids[bit]
        n = 8 >> k
        src = code8.at[kind] if k == 0 else code4.at[kind, pl.ds(0, n)]
        src_scale = scale8.at[kind] if k == 0 else scale4.at[kind, pl.ds(0, n)]
        slots = pl.ds(FIRST_SLOT[k], n)
        return (
            remote(src, got.at[blob, slots], r_send.at[blob, k], r_recv.at[blob, k], device),
            remote(src_scale, got_scale.at[blob, slots], s_send.at[blob, k], s_recv.at[blob, k], device),
        ), n

    def encode(x, codes, scales, kind, slot):
        high = jnp.maximum(jnp.max(jnp.abs(x)), 1e-30)
        codes[kind, slot] = jnp.round(x * (CODE_TOP / high)).astype(jnp.int32).astype(jnp.int16)
        scales[kind, slot] = jnp.full((8, 128), 1.0 / CODE_TOP, F32) * high

    def decode(blob, slot):
        return got[blob, slot].astype(jnp.int32).astype(F32) * got_scale[blob, slot, 0:1, 0:1]

    def relative(kind, s, sub, flag):
        if kind == 0:
            return ((sub >> 2) & 1) | (((sub >> 1) & 1) << 1) | ((sub & 1) << 2)
        if kind == 1:
            return flag | (((sub >> 1) & 1) << 1) | ((sub & 1) << 2)
        return (flag << 1) | ((sub >> 1) & 1) | ((sub & 1) << 2)

    def chunk(r):
        return temp[pl.ds(pl.multiple_of((r ^ m) * ROWS, 16), ROWS), :]

    def loop(n, body):
        lax.fori_loop(0, n, lambda i, _: (body(i), 0)[1], 0)

    def split(kind, s):
        if kind == 0:
            if s == 1:
                loop(8, lambda j: encode(chunk(relative(0, 1, j, 0)), code8, scale8, kind, j))
            else:

                def keep(j):
                    kept8[kind, j] = chunk(relative(0, 0, j, 0))

                loop(8, keep)
        else:

            def both(j):
                encode(chunk(relative(kind, s, j, 1)), code8, scale8, kind, s * 4 + j)
                kept8[kind, s * 4 + j] = chunk(relative(kind, s, j, 0))

            loop(4, both)

    flying = {}
    out_copies = {}

    def start_stage(blob, k):
        copies, _ = stage(blob, k)
        for copy in copies:
            copy.start()
        flying[blob, k] = copies

    def end_stage(blob, k):
        for copy in flying.pop((blob, k), ()):
            copy.wait_send()

    def receive(blob, k):
        kind = blob % 3
        copies, n = stage(blob, k)
        for copy in copies:
            copy.wait_recv()
        kept = kept8 if k == 0 else kept4
        half = n // 2
        if k > 0:
            end_stage(blob, k)
        if half:

            def send_on(j):
                x = kept[kind, half + j] + decode(blob, FIRST_SLOT[k] + half + j)
                encode(x, code4, scale4, kind, j)

            loop(half, send_on)
            start_stage(blob, k + 1)
            if k == 0 and kind in out_copies:
                out_copies.pop(kind).wait()

            def stay(j):
                kept4[kind, j] = kept[kind, j] + decode(blob, FIRST_SLOT[k] + j)

            loop(half, stay)
            if k == 0:
                end_stage(blob, 0)
        else:
            kept4[kind, 3] = kept[kind, 0] + decode(blob, FIRST_SLOT[k])
            out_copies[kind] = pltpu.make_async_copy(
                kept4.at[kind, 3], grads_out.at[blob], out_sem.at[kind]
            )
            out_copies[kind].start()

    def nothing(i):
        pass

    def ffn_back(layer, pump=nothing):
        is_top = layer == top
        loaded(layer, "v2", "slope", "wf")
        if not is_top:
            exchange(2 * (top - layer) - 1, 1).wait_recv()
        free_part()
        at = VEC_ROWS * layer

        def body(i):
            r = block(i)
            if is_top:
                visible = lax.broadcasted_iota(jnp.int32, (SEQ, 1), 0) < meta[i]
                g = jnp.where(visible, g_sum[pl.ds(i, 1), :], 0.0)
            else:
                g = base[r, :] + got_part[1, r, :].astype(F32)
            gain = gains[layer, 1:2, :]
            xh, rate, _ = norm(v_in[r, :], gain, 0.0)
            gc = norm_back(g, xh, rate, gain)
            add_row(at + 1, rows(g * xh))
            add_row(at + 5, rows(g))
            add_row(at + 4, rows(gc))
            g_low = gc.astype(BF)
            low[r, :] = g_low
            total = None
            for s in range(2):
                inner = (mm_nt(g_low, wf[s, 1]) * sl[s, r, :].astype(F32)).astype(BF)
                sl[s, r, :] = inner
                add_row(at + 6 + (t ^ (2 * s)), rows(inner.astype(F32)))
                term = mm_nt(inner, wf[s, 0])
                total = term if total is None else total + term
            base[r, :] = gc + total
            part[r, :] = total.astype(BF)
            pump(i)

        loop(nc, body)
        send_part(2 * (top - layer), 0)
        load(layer, "v1")
        if layer > 0:
            load(layer - 1, "wf")

    def ffn_grads(layer):
        loaded(layer, "active", "normed")
        blob = 3 * (top - layer)
        temp[...] = mm_tn(nm[...], sl[1])
        split(0, 1)
        start_stage(blob, 0)
        for s in range(2):
            temp[...] = mm_tn(low[...], act[s])
            split(1, s)
        start_stage(blob + 1, 0)
        temp[...] = mm_tn(nm[...], sl[0])
        split(0, 0)
        load(layer, "hidden")
        if layer > 0:
            load(layer - 1, "slope", "active")

    def attn_back(layer, pump=nothing):
        loaded(layer, "v1", "proj", "probs", "wa")
        exchange(2 * (top - layer), 0).wait_recv()
        free_part()
        at = VEC_ROWS * layer

        def body(i):
            r = block(i)
            g = base[r, :] + got_part[0, r, :].astype(F32)
            gain = gains[layer, 0:1, :]
            xh, rate, _ = norm(v_in[r, :], gain, 0.0)
            gr = norm_back(g, xh, rate, gain)
            add_row(at, rows(g * xh))
            add_row(at + 3, rows(g))
            add_row(at + 2, rows(gr))
            g_low = gr.astype(BF)
            low[r, :] = g_low
            total = None
            for s in range(2):
                g_mixed = mm_nt(g_low, wa[s, 3 * width : 4 * width, :]).astype(BF)
                here = pj[s, r, :]
                parts = [[], [], []]
                for h in range(heads):
                    queries = here[:, h * HEAD : (h + 1) * HEAD]
                    keys = here[:, width + h * HEAD : width + (h + 1) * HEAD]
                    values = here[:, 2 * width + h * HEAD : 2 * width + (h + 1) * HEAD]
                    gm = g_mixed[:, h * HEAD : (h + 1) * HEAD]
                    p_low = pr[s, i, h]
                    p = p_low.astype(F32)
                    gp = mm_nt(gm, values)
                    gs = (p * (gp - jnp.sum(p * gp, axis=1, keepdims=True))).astype(BF)
                    parts[0].append((mm(gs, keys) * SCALE).astype(BF))
                    parts[1].append((mm_tn(gs, queries) * SCALE).astype(BF))
                    parts[2].append(mm_tn(p_low, gm).astype(BF))
                g_proj = jnp.concatenate(parts[0] + parts[1] + parts[2], axis=1)
                pj[s, r, :] = g_proj
                vec[0, pl.ds(at + 10 + (t ^ (2 * s)), 1), 0 : 3 * width] += rows(g_proj.astype(F32))
                term = mm(g_proj, wa[s, 0 : 3 * width, :])
                total = term if total is None else total + term
            base[r, :] = gr + total
            part[r, :] = total.astype(BF)
            pump(i)

        loop(nc, body)
        send_part(2 * (top - layer) + 1, 1)
        if layer > 0:
            load(layer - 1, "v2", "probs", "wa")

    def attn_grads(layer):
        loaded(layer, "hidden", "mixed")
        blob = 3 * (top - layer) + 2
        for s in range(2):
            temp[:, 0 : 3 * width] = mm_tn(nm[...], pj[s])
            temp[:, 3 * width : 4 * width] = mm_tn(low[...], mx[s])
            split(2, s)
        start_stage(blob, 0)
        if layer > 0:
            load(layer - 1, "proj", "mixed", "normed")

    vec_copies = []

    def vec_start(s):
        copy = remote(vec.at[0], vec_got.at[s], v_send.at[s], v_recv.at[s], everyone[s])
        copy.start()
        vec_copies.append(copy)

    def vec_next(s):
        vec_copies[s].wait()
        vec[0] = vec[0] + vec_got[s]
        if s + 1 < len(everyone):
            vec_start(s + 1)

    def pumps(table):
        def pump(i):
            for at, actions in table.items():

                @pl.when(i == at)
                def _():
                    for blob, k in actions:
                        receive(blob, k)

        return pump

    ffn_back(1)
    ffn_grads(1)
    attn_back(1)
    attn_grads(1)
    ffn_back(0)
    receive(0, 0)
    receive(1, 0)
    ffn_grads(0)
    receive(0, 1)
    receive(1, 1)
    attn_back(0)
    first = jnp.where((lax.broadcasted_iota(jnp.int32, (LAYERS * VEC_ROWS, D), 0) % VEC_ROWS >= 6) | (core == 0), 1.0, 0.0)
    vec[0] = vec[0] * first
    vec_start(0)
    receive(2, 0)
    receive(0, 2)
    receive(1, 2)
    attn_grads(0)
    receive(0, 3)
    receive(1, 3)
    vec_next(0)
    receive(3, 0)
    receive(4, 0)
    receive(2, 1)
    vec_next(1)
    receive(2, 2)
    receive(3, 1)
    receive(4, 1)
    vec_next(2)
    receive(2, 3)
    receive(5, 0)
    vec_next(3)
    receive(3, 2)
    receive(4, 2)
    for s in range(4, len(everyone)):
        vec_next(s)
    receive(5, 1)
    receive(3, 3)
    receive(4, 3)
    receive(5, 2)
    exchange(2 * LAYERS - 1, 1).wait_recv()
    mine = pl.ds(pl.multiple_of(core * share, 16), share)
    v_in[0:share, :] = base[mine, :] + got_part[1, mine, :].astype(F32)
    query_copy = pltpu.make_async_copy(v_in.at[0:share], query_out, out_sem.at[3])
    query_copy.start()
    receive(5, 3)
    query_copy.wait()
    for copy in out_copies.values():
        copy.wait()
    vec_out[...] = vec[0]
    free_part()
    for blob, k in list(flying):
        end_stage(blob, k)


SMEM = pl.BlockSpec(memory_space=pltpu.SMEM)


def on_device(mesh_shape, *args):
    (
        query_input,
        key_input,
        query_length,
        key_length,
        pair_count,
    ) = args[:5]
    encoders = (args[5:13], args[13:21])
    dp_size = mesh_shape["dp"]
    dp_bits = dp_size.bit_length() - 1
    d_pos = lax.axis_index("dp")
    t_pos = lax.axis_index("tensor")
    quarter = d_pos & 3
    core = t_pos & 1
    half = t_pos // 2
    share = query_input.shape[0]
    total_rows = 2 * share
    nc = total_rows // SEQ
    width = args[5].shape[3]

    blob_a = [
        jnp.concatenate(
            [w[0].transpose(0, 2, 3, 1).reshape(LAYERS, 3 * width, D), w[2]], axis=1
        )
        for w in encoders
    ]
    bias_rows = []
    for w in encoders:
        zero = jnp.zeros((LAYERS, width), F32)
        bias_rows += [jnp.concatenate([w[1][:, 0], zero, w[1][:, 1], zero], axis=1), w[4]]
    bias = jnp.concatenate(bias_rows, axis=0)
    lengths = [
        lax.dynamic_slice(v, (half * nc,), (nc,)) for v in (query_length, key_length)
    ]
    meta = jnp.concatenate(lengths)
    inverse = [(1.0 / v.astype(F32))[:, None] for v in lengths]
    big = (total_rows, D)
    heads = width // HEAD
    unit_flops = 2 * total_rows * D
    vmem = pl.BlockSpec(memory_space=pltpu.VMEM)
    hbm = pl.BlockSpec(memory_space=pl.ANY)
    hops = dp_bits + 1
    shaped = jax.ShapeDtypeStruct
    sem = pltpu.SemaphoreType.DMA
    rows_of = lambda *s: (LAYERS,) + s
    results = pl.pallas_call(
        functools.partial(forward, dp_size, nc),
        in_specs=[SMEM] * 2 + [hbm] * 8 + [vmem] * 7,
        out_specs=[hbm] * 10 + [vmem] * 2,
        out_shape=[
            shaped(rows_of(total_rows, D), BF),
            shaped(rows_of(2, total_rows, 3 * width), BF),
            shaped(rows_of(2, nc, heads, SEQ, SEQ), BF),
            shaped(rows_of(2, total_rows, width), BF),
            shaped(rows_of(total_rows, D), F32),
            shaped(rows_of(total_rows, D), BF),
            shaped(rows_of(2, total_rows, BLOB), BF),
            shaped(rows_of(2, total_rows, BLOB), BF),
            shaped(rows_of(total_rows, D), F32),
            shaped(rows_of(3, BLOB, D), BF),
            shaped((16, 128), F32),
            shaped((nc, D), F32),
        ],
        scratch_shapes=[
            pltpu.VMEM((2,) + big, BF),
            pltpu.VMEM((2,) + big, F32),
            pltpu.VMEM((2,) + big, F32),
            pltpu.VMEM((2,) + big, BF),
            pltpu.VMEM((2, 2) + big, BF),
            pltpu.VMEM((2, BLOB, D), BF),
            pltpu.VMEM((2, 2, BLOB, D), BF),
            pltpu.VMEM((2 * LAYERS, 3, BLOB, D), BF),
            pltpu.VMEM(big, F32),
            pltpu.VMEM((2, total_rows, 3 * width), BF),
            pltpu.VMEM((2, nc, heads, SEQ, SEQ), BF),
            pltpu.VMEM((2, total_rows, width), BF),
            pltpu.VMEM((2, total_rows, BLOB), BF),
            pltpu.VMEM((2, total_rows, BLOB), BF),
            pltpu.VMEM(bias.shape, F32),
            pltpu.VMEM((2, 8, D), F32),
            pltpu.VMEM((2 * dp_size, 8, D + 128), F32),
            sem((len(GROUPS), 6)),
            sem((len(GROUPS), 6)),
            sem((2, 2 * LAYERS)),
            sem((2, 2 * LAYERS)),
            sem((2,)),
            sem((2,)),
            sem((2, 4)),
            sem((9 + 3 * LAYERS,)),
            sem((hops,)),
            sem((hops,)),
            sem((2,)),
        ],
        compiler_params=pltpu.CompilerParams(
            collective_id=0, has_side_effects=True, vmem_limit_bytes=int(60.5 * MIB)
        ),
        cost_estimate=pl.CostEstimate(
            flops=unit_flops * 80 * BLOB // 4, bytes_accessed=100 * MIB, transcendentals=0
        ),
        name="forward",
    )(
        meta,
        pair_count,
        query_input,
        key_input,
        *blob_a,
        encoders[0][3],
        encoders[1][3],
        encoders[0][5],
        encoders[1][5],
        encoders[0][6],
        encoders[1][6],
        encoders[0][7],
        encoders[1][7],
        bias,
        *inverse,
    )
    far, pair_rows, g_sum = results[9:]
    per_pair = jnp.concatenate([pair_rows[nc : 2 * nc, 0], pair_rows[8 + nc : 8 + 2 * nc, 0]])

    n_peers = dp_bits + 2
    mat = (BLOB, D)
    blobs = 3 * LAYERS
    query_grad, grads, summed = pl.pallas_call(
        functools.partial(backward, dp_size, nc),
        in_specs=[SMEM, vmem] + [hbm] * 13 + [vmem],
        out_specs=[hbm, hbm, vmem],
        out_shape=[
            shaped((share, D), F32),
            shaped((blobs, ROWS, BLOB), F32),
            shaped((LAYERS * VEC_ROWS, D), F32),
        ],
        scratch_shapes=[
            pltpu.VMEM((2, 2) + mat, BF),
            pltpu.VMEM((2,) + mat, BF),
            pltpu.VMEM(big, F32),
            pltpu.VMEM((2, total_rows, BLOB), BF),
            pltpu.VMEM((2, total_rows, BLOB), BF),
            pltpu.VMEM(big, BF),
            pltpu.VMEM((2, total_rows, 3 * width), BF),
            pltpu.VMEM((2, nc, heads, SEQ, SEQ), BF),
            pltpu.VMEM((2, total_rows, width), BF),
            pltpu.VMEM(big, BF),
            pltpu.VMEM(big, F32),
            pltpu.VMEM(big, BF),
            pltpu.VMEM((2,) + big, BF),
            pltpu.VMEM((D, BLOB), F32),
            pltpu.VMEM((3, 8, ROWS, BLOB), F32),
            pltpu.VMEM((3, 8, ROWS, BLOB), jnp.int16),
            pltpu.VMEM((3, 4, ROWS, BLOB), F32),
            pltpu.VMEM((3, 4, ROWS, BLOB), jnp.int16),
            pltpu.VMEM((blobs, 15, ROWS, BLOB), jnp.int16),
            pltpu.VMEM((3, 8, 8, 128), F32),
            pltpu.VMEM((3, 4, 8, 128), F32),
            pltpu.VMEM((blobs, 15, 8, 128), F32),
            pltpu.VMEM((1, LAYERS * VEC_ROWS, D), F32),
            pltpu.VMEM((n_peers, LAYERS * VEC_ROWS, D), F32),
            sem((11, 3)),
            sem((4,)),
            sem((2 * LAYERS,)),
            sem((2 * LAYERS,)),
            sem((blobs, 4)),
            sem((blobs, 4)),
            sem((blobs, 4)),
            sem((blobs, 4)),
            sem((n_peers,)),
            sem((n_peers,)),
        ],
        compiler_params=pltpu.CompilerParams(
            collective_id=1, has_side_effects=True, vmem_limit_bytes=int(62 * MIB)
        ),
        cost_estimate=pl.CostEstimate(
            flops=unit_flops * 40 * BLOB // 2, bytes_accessed=60 * MIB, transcendentals=0
        ),
        name="backward",
    )(meta, g_sum, *results[:9], blob_a[0], encoders[0][3], encoders[0][5], far, encoders[0][6])

    rows_left = ROWS
    for bit in reversed(range(dp_bits - 3)):
        rows_left //= 2
        pair = grads.reshape(blobs, 2, rows_left, BLOB)
        mine = (d_pos >> bit) & 1
        send = lax.dynamic_index_in_dim(pair, 1 - mine, 1, keepdims=False)
        grads = lax.dynamic_index_in_dim(pair, mine, 1, keepdims=False) + lax.ppermute(
            send, "dp", [(i, i ^ (1 << bit)) for i in range(dp_size)]
        )
    by_layer = [grads[3 * (LAYERS - 1 - layer) :][:3] for layer in range(LAYERS)]
    grad_in, grad_down, attn = [jnp.stack([g[k] for g in by_layer]) for k in range(3)]
    summed = summed.reshape(LAYERS, VEC_ROWS, D)
    qv = summed[:, 10:14].reshape(LAYERS, 4, 4, width)
    grad_qv_bias = jnp.stack(
        [qv[:, :, 0].reshape(LAYERS, 4 * width), qv[:, :, 2].reshape(LAYERS, 4 * width)], axis=1
    )
    return (
        per_pair,
        query_grad,
        attn[:, :, : 3 * width].reshape(LAYERS, D // dp_size, 3, width),
        attn[:, :, 3 * width :].transpose(0, 2, 1),
        grad_in,
        grad_down.transpose(0, 2, 1),
        grad_qv_bias,
        summed[:, 6:10].reshape(LAYERS, 4 * BLOB),
        summed[:, 0:2],
        summed[:, 2:6],
    )


def solution(mesh):
    split = P(("dp", "tensor"), None)
    weights = (
        P(None, None, None, "tensor"),
        P(None, None, "tensor"),
        P(None, "tensor", None),
        P(None, None, "tensor"),
        P(None, "tensor"),
        P(None, "tensor", None),
        P(),
        P(),
    )
    return jax.shard_map(
        functools.partial(on_device, dict(mesh.shape)),
        mesh=mesh,
        in_specs=(split, split, P("dp"), P("dp"), P("dp")) + weights + weights,
        out_specs=(
            P("dp"),
            split,
            P(None, "dp", None, "tensor"),
            P(None, "tensor", "dp"),
            P(None, "dp", "tensor"),
            P(None, "tensor", "dp"),
            P(),
            P(),
            P(),
            P(),
        ),
        check_vma=False,
    )
```

```python
import functools
import math

import jax
import jax.numpy as jnp
from jax import lax
from jax.experimental import pallas as pl
from jax.experimental.pallas import tpu as pltpu
from jax.sharding import PartitionSpec as P

D = 768
HEAD = 64
SEQ = 256
LAYERS = 2
BLOB = 768
EPS = 1e-06
TEMPER = 0.05
FILL = -1e30
BF = jnp.bfloat16
F32 = jnp.float32
MESH = pl.DeviceIdType.MESH
SCALE = HEAD ** (-0.5)
MIB = 2**20


def mm(a, b):
    return jnp.dot(a, b, preferred_element_type=F32)


def mm_nt(a, b):
    return lax.dot_general(a, b, (((1,), (1,)), ((), ())), preferred_element_type=F32)


def mm_tn(a, b):
    return lax.dot_general(a, b, (((0,), (0,)), ((), ())), preferred_element_type=F32)


def norm(v, gain, shift):
    center = v - jnp.mean(v, axis=-1, keepdims=True)
    rate = lax.rsqrt(jnp.mean(center * center, axis=-1, keepdims=True) + EPS)
    xhat = center * rate
    return xhat, rate, xhat * gain + shift


def norm_back(g, xhat, rate, gain):
    gx = g * gain
    return rate * (
        gx
        - jnp.mean(gx, axis=-1, keepdims=True)
        - xhat * jnp.mean(gx * xhat, axis=-1, keepdims=True)
    )


def rows(v):
    return jnp.sum(v, axis=0, keepdims=True)


PLAN = (
    ('AO', 0, 0, ()),
    ('AO', 1, 0, ((1, 1, 0),)),
    (1, 1),
    (2, 0),
    (1, 2),
    (2, 1),
    (3, 0),
    ('AF', 0, 0, ((1, 1, 3),)),
    (2, 2),
    (3, 1),
    ('AF', 1, 0, ((1, 1, 4),)),
    ('FO', 0, 0, ((0, 2, 3),)),
    ('FO', 1, 0, ((0, 1, 5), (2, 2, 4))),
    (3, 2),
    (3, 3),
    ('FF', 0, 0, ((1, 1, 6),)),
    (2, 5),
    (3, 4),
    (1, 7),
    (2, 6),
    (3, 5),
    ('FF', 1, 0, ((1, 1, 8),)),
    ('AO', 0, 1, ((0, 2, 7),)),
    ('AO', 1, 1, ((0, 1, 9), (2, 2, 8))),
    (3, 6),
    ('AF', 0, 1, ((1, 1, 10),)),
    (3, 7),
    ('AF', 1, 1, ((0, 2, 9),)),
    ('FO', 0, 1, ((0, 1, 11), (1, 2, 10))),
    ('FO', 1, 1, ()),
    (3, 8),
    (3, 9),
    ('FF', 0, 1, ((1, 2, 11),)),
    (3, 10),
    (3, 11),
    ('FF', 1, 1, ()),
)
GROUPS = (
    (0, 0, 0),
    (0, 1, 0),
    (0, 0, 1),
    (0, 0, 2),
    (0, 1, 1),
    (0, 1, 2),
    (1, 0, 0),
    (1, 1, 0),
    (1, 0, 1),
    (1, 0, 2),
    (1, 1, 1),
    (1, 1, 2),
)
T_DELAY = 2


def forward(dp_size, nc, *refs):
    refs = list(refs)

    def take(n):
        return [refs.pop(0) for _ in range(n)]

    meta, count = take(2)
    x_in, blob_a, w_in, w_down, gains, shifts = [take(2) for _ in range(6)]
    bias, inv_q, inv_k = take(3)
    saves = dict(
        zip(("hidden", "proj", "probs", "mixed", "v1", "normed", "active", "slope", "v2"), take(9))
    )
    far_out, pair_out, grad_out = take(3)
    low, base, acc, send, recv, own_a, own_f, far = take(8)
    v_st, proj_st, probs_st, mixed_st, active_st, slope_st = take(6)
    far_bias, sums, held = take(3)
    y_send, y_recv, p_send, p_recv, x_send, x_recv, own_sem, save_sem, c_send, c_recv, b_sem = take(11)

    d = lax.axis_index("dp")
    t = lax.axis_index("tensor")
    core = t & 1
    half = t // 2
    q = d & 3
    share = x_in[0].shape[0]
    far_id, core_id, x_id, z_id = (d, t ^ 2), (d, t ^ 1), (d ^ 1, t), (d ^ 2, t)
    dp_bits = dp_size.bit_length() - 1
    bit_ids = [(d ^ (1 << k), t) for k in reversed(range(dp_bits))] + [far_id]
    greet(bit_ids + [core_id])

    def remote(src, dst, sems, at, device):
        return pltpu.make_async_remote_copy(
            src_ref=src,
            dst_ref=dst,
            send_sem=sems[0].at[at],
            recv_sem=sems[1].at[at],
            device_id=device,
            device_id_type=MESH,
        )

    mine = pl.ds(pl.multiple_of(core * share, 16), share)
    x_local = []
    x_remote = []
    for e in range(2):
        x_local.append(pltpu.make_async_copy(x_in[e], low.at[e, mine], own_sem.at[e, 2]))
        x_remote.append(remote(x_in[e], low.at[e, mine], (x_send, x_recv), e, core_id))

    def load_a(e, layer):
        return [pltpu.make_async_copy(blob_a[e].at[layer], own_a.at[e], own_sem.at[e, 0])]

    def load_f(e, layer):
        return [
            pltpu.make_async_copy(w_in[e].at[layer], own_f.at[e, 0], own_sem.at[e, 1]),
            pltpu.make_async_copy(w_down[e].at[layer], own_f.at[e, 1], own_sem.at[e, 3]),
        ]

    x_local[0].start()
    x_remote[0].start()
    for copy in load_a(0, 0):
        copy.start()
    b_copy = pltpu.make_async_remote_copy(
        src_ref=bias,
        dst_ref=far_bias,
        send_sem=b_sem.at[0],
        recv_sem=b_sem.at[1],
        device_id=far_id,
        device_id_type=MESH,
    )
    b_copy.start()
    x_local[1].start()
    x_remote[1].start()
    for copy in load_a(1, 0) + load_f(0, 0) + load_f(1, 0):
        copy.start()

    n = BLOB // 4
    third = n // 3
    moves = []
    for g, (layer, e, which) in enumerate(GROUPS):

        def at(quarter, start, size):
            row = pl.ds(pl.multiple_of(quarter * n + start, 16), size)
            return far.at[layer * 2 + e, which, row]

        def source(quarter, size):
            row = pl.ds(pl.multiple_of(quarter * n, 16), size)
            return (blob_a, w_in, w_down)[which][e].at[layer, row]

        def move(src, dst, k, device):
            return remote(src, dst, (y_send, y_recv), (g, k), device)

        made = (
            move(source(q, n), at(q, 0, n), 0, far_id),
            move(source(q ^ 3, third), at(q ^ 3, 0, third), 1, far_id),
            move(at(q, 0, n), at(q, 0, n), 2, x_id),
            move(at(q, 0, n), at(q, 0, n), 3, z_id),
            move(at(q ^ 2, third, third), at(q ^ 2, third, third), 4, x_id),
            move(at(q ^ 1, 2 * third, third), at(q ^ 1, 2 * third, third), 5, z_id),
        )
        got = made[:2] + (
            move(at(q ^ 1, 0, n), at(q ^ 1, 0, n), 2, x_id),
            move(at(q ^ 2, 0, n), at(q ^ 2, 0, n), 3, z_id),
            move(at(q ^ 3, third, third), at(q ^ 3, third, third), 4, x_id),
            move(at(q ^ 3, 2 * third, third), at(q ^ 3, 2 * third, third), 5, z_id),
        )
        moves.append((made, got))

    for g in range(len(GROUPS) + T_DELAY):
        if g < len(GROUPS):
            moves[g][0][0].start()
        if g >= T_DELAY:
            moves[g - T_DELAY][0][1].start()

    def stage(k, g):
        made, got = moves[g]
        if k == 1:
            got[0].wait_recv()
            made[2].start()
            made[3].start()
        elif k == 2:
            got[2].wait_recv()
            got[3].wait_recv()
            made[4].start()
            made[5].start()
        else:
            got[1].wait_recv()
            got[4].wait_recv()
            got[5].wait_recv()
            layer, e, which = GROUPS[g]
            if e == 0:
                copy = pltpu.make_async_copy(
                    far.at[2 * layer, which], far_out.at[layer, which], save_sem.at[9 + 3 * layer + which]
                )
                copy.start()
                far_copies.append(copy)

    far_copies = []

    def save(name, layer, src, k):
        return pltpu.make_async_copy(src, saves[name].at[layer], save_sem.at[k])

    pending = {}

    def start_save(name, layer, src):
        k = list(saves).index(name)
        copy = save(name, layer, src, k)
        copy.start()
        pending[name] = copy

    def end_save(*names):
        for name in names:
            if name in pending:
                pending.pop(name).wait()

    def block(i):
        return pl.ds(pl.multiple_of(i * SEQ, SEQ), SEQ)

    def part(e, k):
        return remote(send.at[e], recv.at[e, k % 2], (p_send.at[e], p_recv.at[e]), k, core_id)

    sent = {}

    def send_part(e, k):
        sent[e] = part(e, k)
        sent[e].start()

    width = proj_st.shape[2] // 3
    heads = width // HEAD

    def attn_part(e, s, w, x_low, i, layer):
        b = (bias, far_bias)[s]
        r = block(i)
        proj = (mm_nt(x_low, w[: 3 * width, :]) + b[e * 4 + layer : e * 4 + layer + 1, : 3 * width]).astype(BF)
        visible = lax.broadcasted_iota(jnp.int32, (SEQ, 1), 0) < meta[e * nc + i]
        mixed = []
        for h in range(heads):
            queries = proj[:, h * HEAD : (h + 1) * HEAD]
            keys = proj[:, width + h * HEAD : width + (h + 1) * HEAD]
            values = proj[:, 2 * width + h * HEAD : 2 * width + (h + 1) * HEAD]
            scores = jnp.where(visible, mm_nt(keys, queries) * SCALE, FILL)
            ex = jnp.exp(scores - jnp.max(scores, axis=0, keepdims=True))
            probs = (ex * (1.0 / jnp.sum(ex, axis=0, keepdims=True))).astype(BF)
            if e == 0:
                probs_st[s, i, h] = probs
            mixed.append(mm_tn(probs, values).astype(BF))
        mixed = jnp.concatenate(mixed, axis=1)
        if e == 0:
            proj_st[s, r, :] = proj
            mixed_st[s, r, :] = mixed
        return mm(mixed, w[3 * width : 4 * width, :])

    def ffn_part(e, s, w, x_low, i, layer):
        b = (bias, far_bias)[s]
        r = block(i)
        u = mm(x_low, w[0]) + b[e * 4 + 2 + layer : e * 4 + 3 + layer, :]
        portion = 0.5 + 0.5 * lax.erf(u * (0.5**0.5))
        active = (u * portion).astype(BF)
        if e == 0:
            active_st[s, r, :] = active
            slope_st[s, r, :] = (
                portion + u * (jnp.exp(-0.5 * u * u) * ((2 * math.pi) ** -0.5))
            ).astype(BF)
        return mm(active, w[1])

    def crops(body, hooks):
        def step(i, _):
            body(i)
            for c in range(nc - 1):
                due = [h[1:] for h in hooks if h[0] == c]
                if due:

                    @pl.when(i == c)
                    def _():
                        for k, g in due:
                            stage(k, g)

            return 0

        lax.fori_loop(0, nc, step, 0)
        for c, k, g in hooks:
            if c >= nc - 1:
                stage(k, g)

    def joined(e, k, r):
        return base[e, r, :] + (send[e, r, :].astype(F32) + recv[e, k % 2, r, :].astype(F32))

    def attn_own(e, layer, hooks):
        for copy in load_a(e, layer):
            copy.wait()
        if layer == 0:
            x_local[e].wait()
            x_remote[e].wait_recv()
        else:
            part(e, 2 * layer - 1).wait_recv()
        if e == 0:
            end_save("v1", "normed", "proj", "probs", "mixed")

        def body(i):
            r = block(i)
            if layer == 0:
                x_low = low[e, r, :]
                x = x_low.astype(F32)
            else:
                v = joined(e, 2 * layer - 1, r)
                if e == 0:
                    v_st[r, :] = v
                x = norm(v, gains[e][layer - 1, 1:2, :], shifts[e][layer - 1, 3:4, :])[2]
                x_low = x.astype(BF)
                low[e, r, :] = x_low
            base[e, r, :] = x + shifts[e][layer, 0:1, :]
            acc[e, r, :] = attn_part(e, 0, own_a.at[e], x_low, i, layer)

        crops(body, hooks)
        if layer + 1 < LAYERS:
            for copy in load_a(e, layer + 1):
                copy.start()
        if e == 0:
            start_save("hidden", layer, low.at[e])
            if layer > 0:
                start_save("v2", layer - 1, v_st)

    def attn_far(e, layer, hooks):
        if e in sent:
            sent[e].wait_send()

        def body(i):
            r = block(i)
            total = acc[e, r, :] + attn_part(e, 1, far.at[2 * layer + e, 0], low[e, r, :], i, layer)
            send[e, r, :] = total.astype(BF)

        crops(body, hooks)
        send_part(e, 2 * layer)
        if e == 0:
            start_save("proj", layer, proj_st)
            start_save("probs", layer, probs_st)
            start_save("mixed", layer, mixed_st)

    def ffn_own(e, layer, hooks):
        for copy in load_f(e, layer):
            copy.wait()
        part(e, 2 * layer).wait_recv()
        if e == 0:
            end_save("hidden", "v2", "active", "slope")

        def body(i):
            r = block(i)
            v = joined(e, 2 * layer, r)
            if e == 0:
                v_st[r, :] = v
            x = norm(v, gains[e][layer, 0:1, :], shifts[e][layer, 1:2, :])[2]
            x_low = x.astype(BF)
            low[e, r, :] = x_low
            base[e, r, :] = x + shifts[e][layer, 2:3, :]
            acc[e, r, :] = ffn_part(e, 0, own_f.at[e], x_low, i, layer)

        crops(body, hooks)
        if layer + 1 < LAYERS:
            for copy in load_f(e, layer + 1):
                copy.start()
        if e == 0:
            start_save("normed", layer, low.at[e])
            start_save("v1", layer, v_st)

    def ffn_far(e, layer, hooks):
        sent[e].wait_send()

        def body(i):
            r = block(i)
            total = acc[e, r, :] + ffn_part(
                e, 1, far.at[2 * layer + e, pl.ds(1, 2)], low[e, r, :], i, layer
            )
            send[e, r, :] = total.astype(BF)

        crops(body, hooks)
        send_part(e, 2 * layer + 1)
        if e == 0:
            start_save("active", layer, active_st)
            start_save("slope", layer, slope_st)

    def pool(e):
        part(e, 2 * LAYERS - 1).wait_recv()
        if e == 0:
            end_save("v1")

        def body(i):
            r = block(i)
            v = joined(e, 2 * LAYERS - 1, r)
            if e == 0:
                v_st[r, :] = v
            x = norm(v, gains[e][LAYERS - 1, 1:2, :], shifts[e][LAYERS - 1, 3:4, :])[2]
            visible = lax.broadcasted_iota(jnp.int32, (SEQ, 1), 0) < meta[e * nc + i]
            sums[e, pl.ds(i, 1), :] = rows(jnp.where(visible, x, 0.0))

        crops(body, ())
        if e == 0:
            start_save("v2", LAYERS - 1, v_st)

    steps = {"AO": attn_own, "AF": attn_far, "FO": ffn_own, "FF": ffn_far}
    first_far = True
    for entry in PLAN:
        if len(entry) == 2:
            stage(*entry)
        else:
            if entry[0] == "AF" and first_far:
                b_copy.wait_recv()
                first_far = False
            steps[entry[0]](*entry[1:])
    pool(0)
    pool(1)
    contrast(dp_size, nc, d, half, bit_ids, count, inv_q, inv_k, sums, pair_out, grad_out, held, c_send, c_recv, remote)
    end_save(*saves)
    for copy in far_copies:
        copy.wait()
    for e in range(2):
        sent[e].wait_send()
        x_remote[e].wait_send()
    b_copy.wait_send()
    for made, _ in moves:
        for copy in made:
            copy.wait_send()


def greet(partners):
    barrier = pltpu.get_barrier_semaphore()
    for p in partners:
        pl.semaphore_signal(barrier, inc=1, device_id=p, device_id_type=MESH)
    pl.semaphore_wait(barrier, len(partners))


def contrast(
    dp_size, nc, d, half, bit_ids, count, inv_q, inv_k, sums, pair_out, grad_out, held, send, recv, remote
):
    wide = D + 128
    dp_bits = dp_size.bit_length() - 1
    low = jnp.int32(0)
    for k in range(dp_bits):
        low = low + (((d >> (dp_bits - 1 - k)) & 1) << k)
    me = low + half * dp_size

    def unit(s, inv):
        pooled = s * inv
        r = lax.rsqrt(jnp.sum(pooled * pooled, axis=1, keepdims=True) + EPS)
        return pooled * r, r

    unit_q, rate_q = unit(sums[0, 0:nc, :], inv_q[...])
    unit_k, _ = unit(sums[1, 0:nc, :], inv_k[...])
    held[me] = jnp.zeros((8, wide), F32)
    held[me, 0:nc, 0:D] = unit_k
    held[me, nc : 2 * nc, 0:D] = unit_q
    slot = half * nc + lax.broadcasted_iota(jnp.int32, (nc, 128), 0)
    lane = lax.broadcasted_iota(jnp.int32, (nc, 128), 1)
    held[me, 0:nc, D:wide] = jnp.where((slot < count[0]) & (lane == 0), 1.0, 0.0)
    for s, p in enumerate(bit_ids):
        mine = pl.ds((me >> s) << s, 1 << s)
        theirs = pl.ds(((me >> s) ^ 1) << s, 1 << s)
        remote(held.at[mine], held.at[mine], (send, recv), s, p).start()
        remote(held.at[theirs], held.at[theirs], (send, recv), s, p).wait_recv()
    for s, p in enumerate(bit_ids):
        mine = pl.ds((me >> s) << s, 1 << s)
        remote(held.at[mine], held.at[mine], (send, recv), s, p).wait_send()
    chips = held.shape[0]
    every = held[...].reshape(chips * 8, wide)
    keys = every[:, 0:D]
    here = jnp.concatenate([held[low], held[low + dp_size]], axis=0)[:, 0:D]

    def exact(a, b, dims):
        return lax.dot_general(
            a, b, (dims, ((), ())), precision=lax.Precision.HIGHEST, preferred_element_type=F32
        )

    one = jnp.where(lax.broadcasted_iota(jnp.int32, (16, 128), 1) == 0, 1.0, 0.0)
    live = exact(one, every[:, D:wide], ((1,), (1,))) > 0.5
    logits = exact(here, keys, ((1,), (1,))) / TEMPER
    masked = jnp.where(live, logits, FILL)
    highest = jnp.max(masked, axis=1, keepdims=True)
    e = jnp.exp(masked - highest)
    total = jnp.sum(e, axis=1, keepdims=True)
    row = lax.broadcasted_iota(jnp.int32, (16, 1), 0)
    chip = row // 8
    place = row % 8 - nc
    column = lax.broadcasted_iota(jnp.int32, (16, chips * 8), 1)
    own = column == (low + chip * dp_size) * 8 + place
    live_here = (place >= 0) & (place < nc) & (chip * nc + place < count[0])
    own_logit = jnp.sum(jnp.where(own, logits, 0.0), axis=1, keepdims=True)
    pair_out[...] = jnp.broadcast_to(
        jnp.where(live_here, highest + jnp.log(total) - own_logit, 0.0), (16, 128)
    )
    weighting = jnp.where(live_here, e / total - own.astype(F32), 0.0) * (SEQ / TEMPER)
    g_unit = exact(weighting, keys, ((1,), (0,)))
    g_unit = jnp.where(half == 0, g_unit[nc : 2 * nc], g_unit[8 + nc : 8 + 2 * nc])
    g_pooled = rate_q * (g_unit - unit_q * jnp.sum(unit_q * g_unit, axis=1, keepdims=True))
    grad_out[...] = g_pooled * inv_q[...]


ROWS = D // 8
VEC_ROWS = 16
CODE_TOP = 32000.0
FIRST_SLOT = (0, 8, 12, 14)
BLOBS = (
    (1, 0, 0, 384, 'xzwy'),
    (1, 0, 384, 384, 'ywzx'),
    (1, 1, 0, 384, 'zwxy'),
    (1, 1, 384, 384, 'xywz'),
    (1, 2, 0, 384, 'xyzw'),
    (1, 2, 384, 384, 'yxwz'),
    (0, 0, 0, 384, 'zyxw'),
    (0, 0, 384, 384, 'yxwz'),
    (0, 1, 0, 384, 'xwyz'),
    (0, 1, 384, 384, 'xzyw'),
    (0, 2, 0, 384, 'yxzw'),
    (0, 2, 384, 384, 'yxzw'),
)
BACK_PLAN = (
    ('FB', 1, ()),
    ('FW', 1, ()),
    ('AB', 1, ((1, 1, 0), (2, 0, 0))),
    ('AW', 1, ((0, 2, 0),)),
    ('FB', 0, ((1, 3, 0), (1, 1, 1), (1, 0, 1))),
    ('FW', 0, ((0, 5, 0), (2, 1, 2), (2, 4, 0), (2, 3, 1), (2, 2, 1))),
    ('AB', 0, ((0, 5, 1), (0, 1, 3), (0, 0, 2), (1, 2, 2))),
    ('AW', 0, ((0, 4, 1), (0, 0, 3), (0, 7, 0), (0, 6, 0), (0, 2, 3), (0, 3, 2), (0, -1, 0))),
    ("END", 0, ((4, 2), (5, 2), (3, 3), (8, 0), (5, 3), (4, 3), (9, 0), (10, 0), (7, 1), (-1, 1), (8, 1), (9, 1), (11, 0), (10, 1), (-1, 2), (7, 2), (6, 1), (10, 2), (11, 1), (8, 2), (7, 3), (-1, 3), (6, 2), (9, 2), (10, 3), (-1, 4), (11, 2), (8, 3), (6, 3), (9, 3), (11, 3))),
)
VEC_STAGES = 5


def backward(dp_size, nc, *refs):
    refs = list(refs)

    def take(n):
        return [refs.pop(0) for _ in range(n)]

    meta, g_sum = take(2)
    names = ("hidden", "proj", "probs", "mixed", "v1", "normed", "active", "slope", "v2")
    saves = dict(zip(names, take(9)))
    blob_a, w_in, w_down, far, gains = take(5)
    query_out, grads_out, vec_out = take(3)
    wf, wa, v_in, sl, act, nm, pj, pr, mx, low, base, part, got_part = take(13)
    temp, kept8, code8, kept4, code4, got, scale8, scale4, got_scale, bounds = take(10)
    vec, vec_got = take(2)
    load_sem, out_sem, p_send, p_recv, r_send, r_recv, s_send, s_recv, v_send, v_recv = take(10)

    d = lax.axis_index("dp")
    t = lax.axis_index("tensor")
    core = t & 1
    dp_bits = dp_size.bit_length() - 1
    spare = dp_bits - 3
    m = d >> spare
    share = query_out.shape[0]
    width = mx.shape[2]
    heads = width // HEAD
    far_id, core_id = (d, t ^ 2), (d, t ^ 1)
    bit_ids = [(d ^ (1 << k), t) for k in range(dp_bits)]
    top_ids = bit_ids[spare:]
    everyone = [far_id] + bit_ids + [core_id]
    greet(everyone)

    def remote(src, dst, send, recv, device):
        return pltpu.make_async_remote_copy(
            src_ref=src,
            dst_ref=dst,
            send_sem=send,
            recv_sem=recv,
            device_id=device,
            device_id_type=MESH,
        )

    def loads(name, layer):
        pairs = {
            "v1": [(saves["v1"].at[layer], v_in)],
            "v2": [(saves["v2"].at[layer], v_in)],
            "slope": [(saves["slope"].at[layer], sl)],
            "active": [(saves["active"].at[layer], act)],
            "normed": [(saves["normed"].at[layer], nm)],
            "hidden": [(saves["hidden"].at[layer], nm)],
            "proj": [(saves["proj"].at[layer], pj)],
            "probs": [(saves["probs"].at[layer], pr)],
            "mixed": [(saves["mixed"].at[layer], mx)],
            "wf": [
                (w_in.at[layer], wf.at[0, 0]),
                (w_down.at[layer], wf.at[0, 1]),
                (far.at[layer, pl.ds(1, 2)], wf.at[1]),
            ],
            "wa": [(blob_a.at[layer], wa.at[0]), (far.at[layer, 0], wa.at[1])],
        }[name]
        at = ("v1", "v2", "slope", "active", "normed", "hidden", "proj", "probs", "mixed", "wf", "wa").index(name)
        return [
            pltpu.make_async_copy(s, o, load_sem.at[at, k]) for k, (s, o) in enumerate(pairs)
        ]

    def load(layer, *which):
        for name in which:
            for copy in loads(name, layer):
                copy.start()

    def loaded(layer, *which):
        for name in which:
            for copy in loads(name, layer):
                copy.wait()

    top = LAYERS - 1
    load(top, "v2", "wf", "slope", "active", "normed", "probs", "proj", "wa", "mixed")
    vec[0] = jnp.zeros_like(vec[0])

    def block(i):
        return pl.ds(pl.multiple_of(i * SEQ, SEQ), SEQ)

    def add_row(at, value):
        vec[0, pl.ds(at, 1), :] += value

    sent = []

    def exchange(k, slot):
        return remote(part, got_part.at[slot], p_send.at[k], p_recv.at[k], core_id)

    def send_part(k, slot):
        copy = exchange(k, slot)
        copy.start()
        sent.append(copy)

    def free_part():
        while sent:
            sent.pop().wait_send()

    bit_of = {"x": 0, "z": 1, "w": 2}

    def stage(blob, k):
        layer, kind, c0, cn, order = BLOBS[blob]
        device = far_id if order[k] == "y" else top_ids[bit_of[order[k]]]
        n = 8 >> k
        cols = pl.ds(c0, cn)
        codes, scales = (code8, scale8) if k == 0 else (code4, scale4)
        return (
            remote(
                codes.at[kind, pl.ds(0, n), :, cols],
                got.at[3 * layer + kind, pl.ds(FIRST_SLOT[k], n), :, cols],
                r_send.at[blob, k],
                r_recv.at[blob, k],
                device,
            ),
            remote(
                scales.at[blob, pl.ds(0, n)],
                got_scale.at[blob, pl.ds(FIRST_SLOT[k], n)],
                s_send.at[blob, k],
                s_recv.at[blob, k],
                device,
            ),
        ), n

    def groups(blob):
        c0, cn = BLOBS[blob][2:4]
        return [(g, slice(c0 + 128 * g, c0 + 128 * g + 128)) for g in range(cn // 128)]

    def encode(x, bound):
        return jnp.round(x * (CODE_TOP / bound)).astype(jnp.int32).astype(jnp.int16)

    def decode(blob, k, j, g, lanes):
        layer, kind = BLOBS[blob][:2]
        code = got[3 * layer + kind, FIRST_SLOT[k] + j, :, lanes]
        bound = got_scale[blob, FIRST_SLOT[k] + j, g : g + 1, :]
        return code.astype(jnp.int32).astype(F32) * (bound * (1.0 / CODE_TOP)), bound

    def place(order, s, j, flag):
        rest = order[1:]
        free = [link for link in rest if link != "y"]
        r = 0 if order[0] == "y" else flag << bit_of[order[0]]
        slot = 0
        for at, link in enumerate(rest):
            if link == "y":
                bit = s
            else:
                bit = (j >> (len(free) - 1 - free.index(link))) & 1
                r = r | (bit << bit_of[link])
            slot = slot | (bit << (2 - at))
        return r, slot

    def chunk(r, lanes):
        return temp[pl.ds(pl.multiple_of((r ^ m) * ROWS, 16), ROWS), lanes]

    def loop(n, body):
        lax.fori_loop(0, n, lambda i, _: (body(i), 0)[1], 0)

    def blobs_of(layer, kind):
        return [b for b, entry in enumerate(BLOBS) if entry[:2] == (layer, kind)]

    def largest():
        return jnp.maximum(jnp.max(jnp.abs(temp[...]), axis=0, keepdims=True), 1e-30)

    def split(blob, s, bound):
        kind, order = BLOBS[blob][1], BLOBS[blob][4]

        def keep(j):
            r, slot = place(order, s, j, 0)
            for g, lanes in groups(blob):
                kept8[kind, slot, :, lanes] = chunk(r, lanes)
                bounds[blob, slot, g : g + 1, :] = bound[:, lanes]

        def code(j):
            r, slot = place(order, s, j, 1)
            for g, lanes in groups(blob):
                code8[kind, slot, :, lanes] = encode(chunk(r, lanes), bound[:, lanes])
                scale8[blob, slot, g : g + 1, :] = bound[:, lanes]

        def both(j):
            code(j)
            keep(j)

        if order[0] == "y":
            loop(8, code if s == 1 else keep)
        else:
            loop(4, both)

    def start_stage(blob, k):
        for copy in stage(blob, k)[0]:
            copy.start()

    def end_stage(blob, k):
        for copy in stage(blob, k)[0]:
            copy.wait_send()

    def out_copy(blob):
        layer, kind, c0, cn, _ = BLOBS[blob]
        cols = pl.ds(c0, cn)
        return pltpu.make_async_copy(
            kept4.at[kind, 3, :, cols], grads_out.at[3 * layer + kind, :, cols], out_sem.at[1 + blob]
        )

    going_out = []

    def receive(blob, k):
        if blob < 0:
            vec_next(k)
            return
        layer, kind = BLOBS[blob][:2]
        copies, n = stage(blob, k)
        for copy in copies:
            copy.wait_recv()
        kept = kept8 if k == 0 else kept4
        half = n // 2
        if k == 0:
            for other in [b for b in going_out if BLOBS[b][1] == kind]:
                out_copy(other).wait()
                going_out.remove(other)
        else:
            end_stage(blob, k)
        if half:

            def send_on(j):
                for g, lanes in groups(blob):
                    value, bound = decode(blob, k, half + j, g, lanes)
                    bound = bound + bounds[blob, half + j, g : g + 1, :]
                    code4[kind, j, :, lanes] = encode(kept[kind, half + j, :, lanes] + value, bound)
                    scale4[blob, j, g : g + 1, :] = bound

            loop(half, send_on)
            start_stage(blob, k + 1)

            def stay(j):
                for g, lanes in groups(blob):
                    value, bound = decode(blob, k, j, g, lanes)
                    kept4[kind, j, :, lanes] = kept[kind, j, :, lanes] + value
                    bounds[blob, j, g : g + 1, :] += bound

            loop(half, stay)
            if k == 0:
                end_stage(blob, 0)
        else:
            for g, lanes in groups(blob):
                kept4[kind, 3, :, lanes] = kept[kind, 0, :, lanes] + decode(blob, k, 0, g, lanes)[0]
            out_copy(blob).start()
            going_out.append(blob)

    def crops(body, hooks):
        def step(i, _):
            body(i)
            for c in range(nc - 1):
                due = [h[1:] for h in hooks if h[0] == c]
                if due:

                    @pl.when(i == c)
                    def _():
                        for blob, k in due:
                            receive(blob, k)

            return 0

        lax.fori_loop(0, nc, step, 0)

    def after(hooks, c):
        for at, blob, k in hooks:
            if at == c:
                receive(blob, k)

    def ffn_back(layer, hooks):
        is_top = layer == top
        loaded(layer, "v2", "slope", "wf")
        if not is_top:
            exchange(2 * (top - layer) - 1, 1).wait_recv()
        free_part()
        at = VEC_ROWS * layer

        def body(i):
            r = block(i)
            if is_top:
                visible = lax.broadcasted_iota(jnp.int32, (SEQ, 1), 0) < meta[i]
                g = jnp.where(visible, g_sum[pl.ds(i, 1), :], 0.0)
            else:
                g = base[r, :] + got_part[1, r, :].astype(F32)
            gain = gains[layer, 1:2, :]
            xh, rate, _ = norm(v_in[r, :], gain, 0.0)
            gc = norm_back(g, xh, rate, gain)
            add_row(at + 1, rows(g * xh))
            add_row(at + 5, rows(g))
            add_row(at + 4, rows(gc))
            g_low = gc.astype(BF)
            low[r, :] = g_low
            total = None
            for s in range(2):
                inner = (mm_nt(g_low, wf[s, 1]) * sl[s, r, :].astype(F32)).astype(BF)
                sl[s, r, :] = inner
                add_row(at + 6 + (t ^ (2 * s)), rows(inner.astype(F32)))
                term = mm_nt(inner, wf[s, 0])
                total = term if total is None else total + term
            base[r, :] = gc + total
            part[r, :] = total.astype(BF)

        crops(body, hooks)
        send_part(2 * (top - layer), 0)
        load(layer, "v1")
        if layer > 0:
            load(layer - 1, "wf")
        after(hooks, nc - 1)

    def ffn_grads(layer, hooks):
        loaded(layer, "active", "normed")
        inner, outer = blobs_of(layer, 0), blobs_of(layer, 1)

        def made(blobs, s):
            bound = largest()
            for blob in blobs:
                split(blob, s, bound)
                if s == 1 and BLOBS[blob][4][0] == "y":
                    start_stage(blob, 0)

        def whole(blobs):
            for blob in blobs:
                if BLOBS[blob][4][0] != "y":
                    start_stage(blob, 0)

        temp[...] = mm_tn(nm[...], sl[1])
        made(inner, 1)
        after(hooks, 0)
        temp[...] = mm_tn(low[...], act[1])
        made(outer, 1)
        after(hooks, 1)
        temp[...] = mm_tn(nm[...], sl[0])
        made(inner, 0)
        whole(inner)
        after(hooks, 2)
        temp[...] = mm_tn(low[...], act[0])
        made(outer, 0)
        whole(outer)
        load(layer, "hidden")
        if layer > 0:
            load(layer - 1, "slope", "active")
        after(hooks, 3)

    def attn_back(layer, hooks):
        loaded(layer, "v1", "proj", "probs", "wa")
        exchange(2 * (top - layer), 0).wait_recv()
        free_part()
        at = VEC_ROWS * layer

        def body(i):
            r = block(i)
            g = base[r, :] + got_part[0, r, :].astype(F32)
            gain = gains[layer, 0:1, :]
            xh, rate, _ = norm(v_in[r, :], gain, 0.0)
            gr = norm_back(g, xh, rate, gain)
            add_row(at, rows(g * xh))
            add_row(at + 3, rows(g))
            add_row(at + 2, rows(gr))
            g_low = gr.astype(BF)
            low[r, :] = g_low
            total = None
            for s in range(2):
                g_mixed = mm_nt(g_low, wa[s, 3 * width : 4 * width, :]).astype(BF)
                here = pj[s, r, :]
                parts = [[], [], []]
                for h in range(heads):
                    queries = here[:, h * HEAD : (h + 1) * HEAD]
                    keys = here[:, width + h * HEAD : width + (h + 1) * HEAD]
                    values = here[:, 2 * width + h * HEAD : 2 * width + (h + 1) * HEAD]
                    gm = g_mixed[:, h * HEAD : (h + 1) * HEAD]
                    p_low = pr[s, i, h]
                    p = p_low.astype(F32)
                    gp = mm_nt(values, gm)
                    gs = (p * (gp - jnp.sum(p * gp, axis=0, keepdims=True))).astype(BF)
                    parts[0].append((mm_tn(gs, keys) * SCALE).astype(BF))
                    parts[1].append((mm(gs, queries) * SCALE).astype(BF))
                    parts[2].append(mm(p_low, gm).astype(BF))
                g_proj = jnp.concatenate(parts[0] + parts[1] + parts[2], axis=1)
                pj[s, r, :] = g_proj
                vec[0, pl.ds(at + 10 + (t ^ (2 * s)), 1), 0 : 3 * width] += rows(g_proj.astype(F32))
                term = mm(g_proj, wa[s, 0 : 3 * width, :])
                total = term if total is None else total + term
            base[r, :] = gr + total
            part[r, :] = total.astype(BF)

        crops(body, hooks)
        send_part(2 * (top - layer) + 1, 1)
        if layer > 0:
            load(layer - 1, "v2", "probs", "wa")
        else:
            first = (lax.broadcasted_iota(jnp.int32, vec.shape[1:], 0) % VEC_ROWS >= 6) | (core == 0)
            vec[0] = jnp.where(first, vec[0], 0.0)
            vec_start(0)
        after(hooks, nc - 1)

    def attn_grads(layer, hooks):
        loaded(layer, "hidden", "mixed")
        for s in (1, 0):
            temp[:, 0 : 3 * width] = mm_tn(nm[...], pj[s])
            temp[:, 3 * width : 4 * width] = mm_tn(low[...], mx[s])
            bound = largest()
            for blob in blobs_of(layer, 2):
                split(blob, s, bound)
                if s == (BLOBS[blob][4][0] == "y"):
                    start_stage(blob, 0)
            if s == 0 and layer > 0:
                load(layer - 1, "proj", "mixed", "normed")
            after(hooks, 1 - s)

    def vec_copy(s):
        return remote(vec.at[0], vec_got.at[s], v_send.at[s], v_recv.at[s], everyone[s])

    def vec_start(s):
        vec_copy(s).start()

    def vec_next(s):
        vec_copy(s).wait()
        vec[0] = vec[0] + vec_got[s]
        if s + 1 < len(everyone):
            vec_start(s + 1)

    steps = {"FB": ffn_back, "FW": ffn_grads, "AB": attn_back, "AW": attn_grads}
    for name, layer, hooks in BACK_PLAN:
        if name == "END":
            break
        steps[name](layer, hooks)
    exchange(2 * LAYERS - 1, 1).wait_recv()
    mine = pl.ds(pl.multiple_of(core * share, 16), share)
    v_in[0:share, :] = base[mine, :] + got_part[1, mine, :].astype(F32)
    query_copy = pltpu.make_async_copy(v_in.at[0:share], query_out, out_sem.at[0])
    query_copy.start()
    for blob, k in BACK_PLAN[-1][2]:
        receive(blob, k)
    for s in range(VEC_STAGES, len(everyone)):
        vec_next(s)
    query_copy.wait()
    for blob in going_out:
        out_copy(blob).wait()
    vec_out[...] = vec[0]
    free_part()


SMEM = pl.BlockSpec(memory_space=pltpu.SMEM)


def on_device(mesh_shape, *args):
    (
        query_input,
        key_input,
        query_length,
        key_length,
        pair_count,
    ) = args[:5]
    encoders = (args[5:13], args[13:21])
    dp_size = mesh_shape["dp"]
    dp_bits = dp_size.bit_length() - 1
    d_pos = lax.axis_index("dp")
    t_pos = lax.axis_index("tensor")
    quarter = d_pos & 3
    core = t_pos & 1
    half = t_pos // 2
    share = query_input.shape[0]
    total_rows = 2 * share
    nc = total_rows // SEQ
    width = args[5].shape[3]

    blob_a = [
        jnp.concatenate(
            [w[0].transpose(0, 2, 3, 1).reshape(LAYERS, 3 * width, D), w[2]], axis=1
        )
        for w in encoders
    ]
    bias_rows = []
    for w in encoders:
        zero = jnp.zeros((LAYERS, width), F32)
        bias_rows += [jnp.concatenate([w[1][:, 0], zero, w[1][:, 1], zero], axis=1), w[4]]
    bias = jnp.concatenate(bias_rows, axis=0)
    lengths = [
        lax.dynamic_slice(v, (half * nc,), (nc,)) for v in (query_length, key_length)
    ]
    meta = jnp.concatenate(lengths)
    inverse = [(1.0 / v.astype(F32))[:, None] for v in lengths]
    big = (total_rows, D)
    heads = width // HEAD
    unit_flops = 2 * total_rows * D
    vmem = pl.BlockSpec(memory_space=pltpu.VMEM)
    hbm = pl.BlockSpec(memory_space=pl.ANY)
    hops = dp_bits + 1
    shaped = jax.ShapeDtypeStruct
    sem = pltpu.SemaphoreType.DMA
    rows_of = lambda *s: (LAYERS,) + s
    results = pl.pallas_call(
        functools.partial(forward, dp_size, nc),
        in_specs=[SMEM] * 2 + [hbm] * 8 + [vmem] * 7,
        out_specs=[hbm] * 10 + [vmem] * 2,
        out_shape=[
            shaped(rows_of(total_rows, D), BF),
            shaped(rows_of(2, total_rows, 3 * width), BF),
            shaped(rows_of(2, nc, heads, SEQ, SEQ), BF),
            shaped(rows_of(2, total_rows, width), BF),
            shaped(rows_of(total_rows, D), F32),
            shaped(rows_of(total_rows, D), BF),
            shaped(rows_of(2, total_rows, BLOB), BF),
            shaped(rows_of(2, total_rows, BLOB), BF),
            shaped(rows_of(total_rows, D), F32),
            shaped(rows_of(3, BLOB, D), BF),
            shaped((16, 128), F32),
            shaped((nc, D), F32),
        ],
        scratch_shapes=[
            pltpu.VMEM((2,) + big, BF),
            pltpu.VMEM((2,) + big, F32),
            pltpu.VMEM((2,) + big, F32),
            pltpu.VMEM((2,) + big, BF),
            pltpu.VMEM((2, 2) + big, BF),
            pltpu.VMEM((2, BLOB, D), BF),
            pltpu.VMEM((2, 2, BLOB, D), BF),
            pltpu.VMEM((2 * LAYERS, 3, BLOB, D), BF),
            pltpu.VMEM(big, F32),
            pltpu.VMEM((2, total_rows, 3 * width), BF),
            pltpu.VMEM((2, nc, heads, SEQ, SEQ), BF),
            pltpu.VMEM((2, total_rows, width), BF),
            pltpu.VMEM((2, total_rows, BLOB), BF),
            pltpu.VMEM((2, total_rows, BLOB), BF),
            pltpu.VMEM(bias.shape, F32),
            pltpu.VMEM((2, 8, D), F32),
            pltpu.VMEM((2 * dp_size, 8, D + 128), F32),
            sem((len(GROUPS), 6)),
            sem((len(GROUPS), 6)),
            sem((2, 2 * LAYERS)),
            sem((2, 2 * LAYERS)),
            sem((2,)),
            sem((2,)),
            sem((2, 4)),
            sem((9 + 3 * LAYERS,)),
            sem((hops,)),
            sem((hops,)),
            sem((2,)),
        ],
        compiler_params=pltpu.CompilerParams(
            collective_id=0, has_side_effects=True, vmem_limit_bytes=62 * MIB
        ),
        cost_estimate=pl.CostEstimate(
            flops=unit_flops * 80 * BLOB // 4, bytes_accessed=100 * MIB, transcendentals=0
        ),
        name="forward",
    )(
        meta,
        pair_count,
        query_input,
        key_input,
        *blob_a,
        encoders[0][3],
        encoders[1][3],
        encoders[0][5],
        encoders[1][5],
        encoders[0][6],
        encoders[1][6],
        encoders[0][7],
        encoders[1][7],
        bias,
        *inverse,
    )
    far, pair_rows, g_sum = results[9:]
    per_pair = jnp.concatenate([pair_rows[nc : 2 * nc, 0], pair_rows[8 + nc : 8 + 2 * nc, 0]])

    n_peers = dp_bits + 2
    mat = (BLOB, D)
    blobs = 3 * LAYERS
    query_grad, grads, summed = pl.pallas_call(
        functools.partial(backward, dp_size, nc),
        in_specs=[SMEM, vmem] + [hbm] * 13 + [vmem],
        out_specs=[hbm, hbm, vmem],
        out_shape=[
            shaped((share, D), F32),
            shaped((blobs, ROWS, BLOB), F32),
            shaped((LAYERS * VEC_ROWS, D), F32),
        ],
        scratch_shapes=[
            pltpu.VMEM((2, 2) + mat, BF),
            pltpu.VMEM((2,) + mat, BF),
            pltpu.VMEM(big, F32),
            pltpu.VMEM((2, total_rows, BLOB), BF),
            pltpu.VMEM((2, total_rows, BLOB), BF),
            pltpu.VMEM(big, BF),
            pltpu.VMEM((2, total_rows, 3 * width), BF),
            pltpu.VMEM((2, nc, heads, SEQ, SEQ), BF),
            pltpu.VMEM((2, total_rows, width), BF),
            pltpu.VMEM(big, BF),
            pltpu.VMEM(big, F32),
            pltpu.VMEM(big, BF),
            pltpu.VMEM((2,) + big, BF),
            pltpu.VMEM((D, BLOB), F32),
            pltpu.VMEM((3, 8, ROWS, BLOB), F32),
            pltpu.VMEM((3, 8, ROWS, BLOB), jnp.int16),
            pltpu.VMEM((3, 4, ROWS, BLOB), F32),
            pltpu.VMEM((3, 4, ROWS, BLOB), jnp.int16),
            pltpu.VMEM((blobs, 15, ROWS, BLOB), jnp.int16),
            pltpu.VMEM((len(BLOBS), 8, 8, 128), F32),
            pltpu.VMEM((len(BLOBS), 4, 8, 128), F32),
            pltpu.VMEM((len(BLOBS), 15, 8, 128), F32),
            pltpu.VMEM((len(BLOBS), 8, 8, 128), F32),
            pltpu.VMEM((1, LAYERS * VEC_ROWS, D), F32),
            pltpu.VMEM((n_peers, LAYERS * VEC_ROWS, D), F32),
            sem((11, 3)),
            sem((1 + len(BLOBS),)),
            sem((2 * LAYERS,)),
            sem((2 * LAYERS,)),
            sem((len(BLOBS), 4)),
            sem((len(BLOBS), 4)),
            sem((len(BLOBS), 4)),
            sem((len(BLOBS), 4)),
            sem((n_peers,)),
            sem((n_peers,)),
        ],
        compiler_params=pltpu.CompilerParams(
            collective_id=1, has_side_effects=True, vmem_limit_bytes=int(62.5 * MIB)
        ),
        cost_estimate=pl.CostEstimate(
            flops=unit_flops * 40 * BLOB // 2, bytes_accessed=60 * MIB, transcendentals=0
        ),
        name="backward",
    )(meta, g_sum, *results[:9], blob_a[0], encoders[0][3], encoders[0][5], far, encoders[0][6])

    rows_left = ROWS
    for bit in reversed(range(dp_bits - 3)):
        rows_left //= 2
        pair = grads.reshape(blobs, 2, rows_left, BLOB)
        mine = (d_pos >> bit) & 1
        send = lax.dynamic_index_in_dim(pair, 1 - mine, 1, keepdims=False)
        grads = lax.dynamic_index_in_dim(pair, mine, 1, keepdims=False) + lax.ppermute(
            send, "dp", [(i, i ^ (1 << bit)) for i in range(dp_size)]
        )
    grads = grads.reshape(LAYERS, 3, D // dp_size, BLOB)
    grad_in, grad_down, attn = grads[:, 0], grads[:, 1], grads[:, 2]
    summed = summed.reshape(LAYERS, VEC_ROWS, D)
    qv = summed[:, 10:14].reshape(LAYERS, 4, 4, width)
    grad_qv_bias = jnp.stack(
        [qv[:, :, 0].reshape(LAYERS, 4 * width), qv[:, :, 2].reshape(LAYERS, 4 * width)], axis=1
    )
    return (
        per_pair,
        query_grad,
        attn[:, :, : 3 * width].reshape(LAYERS, D // dp_size, 3, width),
        attn[:, :, 3 * width :].transpose(0, 2, 1),
        grad_in,
        grad_down.transpose(0, 2, 1),
        grad_qv_bias,
        summed[:, 6:10].reshape(LAYERS, 4 * BLOB),
        summed[:, 0:2],
        summed[:, 2:6],
    )


def solution(mesh):
    split = P(("dp", "tensor"), None)
    weights = (
        P(None, None, None, "tensor"),
        P(None, None, "tensor"),
        P(None, "tensor", None),
        P(None, None, "tensor"),
        P(None, "tensor"),
        P(None, "tensor", None),
        P(),
        P(),
    )
    return jax.shard_map(
        functools.partial(on_device, dict(mesh.shape)),
        mesh=mesh,
        in_specs=(split, split, P("dp"), P("dp"), P("dp")) + weights + weights,
        out_specs=(
            P("dp"),
            split,
            P(None, "dp", None, "tensor"),
            P(None, "tensor", "dp"),
            P(None, "dp", "tensor"),
            P(None, "tensor", "dp"),
            P(),
            P(),
            P(),
            P(),
        ),
        check_vma=False,
    )
```

```python
import functools
import math

import jax
import jax.numpy as jnp
from jax import lax
from jax.experimental import pallas as pl
from jax.experimental.pallas import tpu as pltpu
from jax.sharding import PartitionSpec as P

D = 768
HEAD = 64
SEQ = 256
LAYERS = 2
BLOB = 768
EPS = 1e-06
TEMPER = 0.05
FILL = -1e30
BF = jnp.bfloat16
F32 = jnp.float32
MESH = pl.DeviceIdType.MESH
SCALE = HEAD ** (-0.5)
MIB = 2**20


def mm(a, b):
    return jnp.dot(a, b, preferred_element_type=F32)


def mm_nt(a, b):
    return lax.dot_general(a, b, (((1,), (1,)), ((), ())), preferred_element_type=F32)


def mm_tn(a, b):
    return lax.dot_general(a, b, (((0,), (0,)), ((), ())), preferred_element_type=F32)


def norm(v, gain, shift):
    center = v - jnp.mean(v, axis=-1, keepdims=True)
    rate = lax.rsqrt(jnp.mean(center * center, axis=-1, keepdims=True) + EPS)
    xhat = center * rate
    return xhat, rate, xhat * gain + shift


def norm_back(g, xhat, rate, gain):
    gx = g * gain
    return rate * (
        gx
        - jnp.mean(gx, axis=-1, keepdims=True)
        - xhat * jnp.mean(gx * xhat, axis=-1, keepdims=True)
    )


def rows(v):
    return jnp.sum(v, axis=0, keepdims=True)


PLAN = (
    ('AO', 0, 0, ()),
    ('AO', 1, 0, ((1, 1, 0),)),
    (1, 1),
    (2, 0),
    (1, 2),
    (2, 1),
    (3, 0),
    ('AF', 0, 0, ((1, 1, 3),)),
    (2, 2),
    (3, 1),
    ('AF', 1, 0, ((1, 1, 4),)),
    ('FO', 0, 0, ((0, 2, 3),)),
    ('FO', 1, 0, ((0, 1, 5), (2, 2, 4))),
    (3, 2),
    (3, 3),
    ('FF', 0, 0, ((1, 1, 6),)),
    (2, 5),
    (3, 4),
    (1, 7),
    (2, 6),
    (3, 5),
    ('FF', 1, 0, ((1, 1, 8),)),
    ('AO', 0, 1, ((0, 2, 7),)),
    ('AO', 1, 1, ((0, 1, 9), (2, 2, 8))),
    (3, 6),
    ('AF', 0, 1, ((1, 1, 10),)),
    (3, 7),
    ('AF', 1, 1, ((0, 2, 9),)),
    ('FO', 0, 1, ((0, 1, 11), (1, 2, 10))),
    ('FO', 1, 1, ()),
    (3, 8),
    (3, 9),
    ('FF', 0, 1, ((1, 2, 11),)),
    (3, 10),
    (3, 11),
    ('FF', 1, 1, ()),
)
GROUPS = (
    (0, 0, 0),
    (0, 1, 0),
    (0, 0, 1),
    (0, 0, 2),
    (0, 1, 1),
    (0, 1, 2),
    (1, 0, 0),
    (1, 1, 0),
    (1, 0, 1),
    (1, 0, 2),
    (1, 1, 1),
    (1, 1, 2),
)
T_DELAY = 2


def forward(dp_size, nc, *refs):
    refs = list(refs)

    def take(n):
        return [refs.pop(0) for _ in range(n)]

    lengths = take(2)
    (count,) = take(1)
    x_in, blob_a, w_in, w_down, gains, shifts = [take(2) for _ in range(6)]
    qv_bias, in_bias = take(2), take(2)
    saves = dict(
        zip(("hidden", "proj", "probs", "mixed", "v1", "normed", "active", "slope", "v2"), take(9))
    )
    far_out, pair_out, grad_out = take(3)
    low, base, acc, send, recv, own_a, own_f, far = take(8)
    v_st, proj_st, probs_st, mixed_st, active_st, slope_st = take(6)
    bias, far_bias, sums, held, units = take(5)
    y_send, y_recv, p_send, p_recv, x_send, x_recv, own_sem, save_sem, c_send, c_recv, b_sem = take(11)

    d = lax.axis_index("dp")
    t = lax.axis_index("tensor")
    core = t & 1
    half = t // 2
    q = d & 3
    share = x_in[0].shape[0]
    far_id, core_id, x_id, z_id = (d, t ^ 2), (d, t ^ 1), (d ^ 1, t), (d ^ 2, t)
    dp_bits = dp_size.bit_length() - 1
    bit_ids = [(d ^ (1 << k), t) for k in reversed(range(dp_bits))] + [far_id]
    greet(bit_ids + [core_id])

    def remote(src, dst, sems, at, device):
        return pltpu.make_async_remote_copy(
            src_ref=src,
            dst_ref=dst,
            send_sem=sems[0].at[at],
            recv_sem=sems[1].at[at],
            device_id=device,
            device_id_type=MESH,
        )

    mine = pl.ds(pl.multiple_of(core * share, 16), share)
    x_local = []
    x_remote = []
    for e in range(2):
        x_local.append(pltpu.make_async_copy(x_in[e], low.at[e, mine], own_sem.at[e, 2]))
        x_remote.append(remote(x_in[e], low.at[e, mine], (x_send, x_recv), e, core_id))

    def load_a(e, layer):
        return [pltpu.make_async_copy(blob_a[e].at[layer], own_a.at[e], own_sem.at[e, 0])]

    def load_f(e, layer):
        return [
            pltpu.make_async_copy(w_in[e].at[layer], own_f.at[e, 0], own_sem.at[e, 1]),
            pltpu.make_async_copy(w_down[e].at[layer], own_f.at[e, 1], own_sem.at[e, 3]),
        ]

    x_local[0].start()
    x_remote[0].start()
    for copy in load_a(0, 0):
        copy.start()
    bias[...] = jnp.zeros_like(bias)
    part_width = proj_st.shape[2] // 3
    for e in range(2):
        for layer in range(LAYERS):
            for c, at in ((0, 0), (1, 2 * part_width)):
                bias[e * 4 + layer : e * 4 + layer + 1, at : at + part_width] = qv_bias[e][layer, c : c + 1, :]
            bias[e * 4 + 2 + layer : e * 4 + 3 + layer, :] = in_bias[e][layer : layer + 1, :]
    b_copy = pltpu.make_async_remote_copy(
        src_ref=bias,
        dst_ref=far_bias,
        send_sem=b_sem.at[0],
        recv_sem=b_sem.at[1],
        device_id=far_id,
        device_id_type=MESH,
    )
    b_copy.start()
    x_local[1].start()
    x_remote[1].start()
    for copy in load_a(1, 0) + load_f(0, 0) + load_f(1, 0):
        copy.start()

    n = BLOB // 4
    third = n // 3
    moves = []
    for g, (layer, e, which) in enumerate(GROUPS):

        def at(quarter, start, size):
            row = pl.ds(pl.multiple_of(quarter * n + start, 16), size)
            return far.at[layer * 2 + e, which, row]

        def source(quarter, size):
            row = pl.ds(pl.multiple_of(quarter * n, 16), size)
            return (blob_a, w_in, w_down)[which][e].at[layer, row]

        def move(src, dst, k, device):
            return remote(src, dst, (y_send, y_recv), (g, k), device)

        made = (
            move(source(q, n), at(q, 0, n), 0, far_id),
            move(source(q ^ 3, third), at(q ^ 3, 0, third), 1, far_id),
            move(at(q, 0, n), at(q, 0, n), 2, x_id),
            move(at(q, 0, n), at(q, 0, n), 3, z_id),
            move(at(q ^ 2, third, third), at(q ^ 2, third, third), 4, x_id),
            move(at(q ^ 1, 2 * third, third), at(q ^ 1, 2 * third, third), 5, z_id),
        )
        got = made[:2] + (
            move(at(q ^ 1, 0, n), at(q ^ 1, 0, n), 2, x_id),
            move(at(q ^ 2, 0, n), at(q ^ 2, 0, n), 3, z_id),
            move(at(q ^ 3, third, third), at(q ^ 3, third, third), 4, x_id),
            move(at(q ^ 3, 2 * third, third), at(q ^ 3, 2 * third, third), 5, z_id),
        )
        moves.append((made, got))

    for g in range(len(GROUPS) + T_DELAY):
        if g < len(GROUPS):
            moves[g][0][0].start()
        if g >= T_DELAY:
            moves[g - T_DELAY][0][1].start()

    def stage(k, g):
        made, got = moves[g]
        if k == 1:
            got[0].wait_recv()
            made[2].start()
            made[3].start()
        elif k == 2:
            got[2].wait_recv()
            got[3].wait_recv()
            made[4].start()
            made[5].start()
        else:
            got[1].wait_recv()
            got[4].wait_recv()
            got[5].wait_recv()
            layer, e, which = GROUPS[g]
            if e == 0:
                copy = pltpu.make_async_copy(
                    far.at[2 * layer, which], far_out.at[layer, which], save_sem.at[9 + 3 * layer + which]
                )
                copy.start()
                far_copies.append(copy)

    far_copies = []

    def save(name, layer, src, k):
        return pltpu.make_async_copy(src, saves[name].at[layer], save_sem.at[k])

    pending = {}

    def start_save(name, layer, src):
        k = list(saves).index(name)
        copy = save(name, layer, src, k)
        copy.start()
        pending[name] = copy

    def end_save(*names):
        for name in names:
            if name in pending:
                pending.pop(name).wait()

    def block(i):
        return pl.ds(pl.multiple_of(i * SEQ, SEQ), SEQ)

    def part(e, k):
        return remote(send.at[e], recv.at[e, k % 2], (p_send.at[e], p_recv.at[e]), k, core_id)

    sent = {}

    def send_part(e, k):
        sent[e] = part(e, k)
        sent[e].start()

    width = proj_st.shape[2] // 3
    heads = width // HEAD

    def attn_part(e, s, w, x_low, i, layer):
        b = (bias, far_bias)[s]
        r = block(i)
        proj = (mm_nt(x_low, w[: 3 * width, :]) + b[e * 4 + layer : e * 4 + layer + 1, : 3 * width]).astype(BF)
        visible = lax.broadcasted_iota(jnp.int32, (SEQ, 1), 0) < lengths[e][half * nc + i]
        mixed = []
        for h in range(heads):
            queries = proj[:, h * HEAD : (h + 1) * HEAD]
            keys = proj[:, width + h * HEAD : width + (h + 1) * HEAD]
            values = proj[:, 2 * width + h * HEAD : 2 * width + (h + 1) * HEAD]
            scores = jnp.where(visible, mm_nt(keys, queries) * SCALE, FILL)
            ex = jnp.exp(scores - jnp.max(scores, axis=0, keepdims=True))
            probs = (ex * (1.0 / jnp.sum(ex, axis=0, keepdims=True))).astype(BF)
            if e == 0:
                probs_st[s, i, h] = probs
            mixed.append(mm_tn(probs, values).astype(BF))
        mixed = jnp.concatenate(mixed, axis=1)
        if e == 0:
            proj_st[s, r, :] = proj
            mixed_st[s, r, :] = mixed
        return mm(mixed, w[3 * width : 4 * width, :])

    def ffn_part(e, s, w, x_low, i, layer):
        b = (bias, far_bias)[s]
        r = block(i)
        u = mm(x_low, w[0]) + b[e * 4 + 2 + layer : e * 4 + 3 + layer, :]
        portion = 0.5 + 0.5 * lax.erf(u * (0.5**0.5))
        active = (u * portion).astype(BF)
        if e == 0:
            active_st[s, r, :] = active
            slope_st[s, r, :] = (
                portion + u * (jnp.exp(-0.5 * u * u) * ((2 * math.pi) ** -0.5))
            ).astype(BF)
        return mm(active, w[1])

    def crops(body, hooks):
        def step(i, _):
            body(i)
            for c in range(nc - 1):
                due = [h[1:] for h in hooks if h[0] == c]
                if due:

                    @pl.when(i == c)
                    def _():
                        for k, g in due:
                            stage(k, g)

            return 0

        lax.fori_loop(0, nc, step, 0)
        for c, k, g in hooks:
            if c >= nc - 1:
                stage(k, g)

    def joined(e, k, r):
        return base[e, r, :] + (send[e, r, :].astype(F32) + recv[e, k % 2, r, :].astype(F32))

    def attn_own(e, layer, hooks):
        for copy in load_a(e, layer):
            copy.wait()
        if layer == 0:
            x_local[e].wait()
            x_remote[e].wait_recv()
        else:
            part(e, 2 * layer - 1).wait_recv()
        if e == 0:
            end_save("v1", "normed", "proj", "probs", "mixed")

        def body(i):
            r = block(i)
            if layer == 0:
                x_low = low[e, r, :]
                x = x_low.astype(F32)
            else:
                v = joined(e, 2 * layer - 1, r)
                if e == 0:
                    v_st[r, :] = v
                x = norm(v, gains[e][layer - 1, 1:2, :], shifts[e][layer - 1, 3:4, :])[2]
                x_low = x.astype(BF)
                low[e, r, :] = x_low
            base[e, r, :] = x + shifts[e][layer, 0:1, :]
            acc[e, r, :] = attn_part(e, 0, own_a.at[e], x_low, i, layer)

        crops(body, hooks)
        if layer + 1 < LAYERS:
            for copy in load_a(e, layer + 1):
                copy.start()
        if e == 0:
            start_save("hidden", layer, low.at[e])
            if layer > 0:
                start_save("v2", layer - 1, v_st)

    def attn_far(e, layer, hooks):
        if e in sent:
            sent[e].wait_send()

        def body(i):
            r = block(i)
            total = acc[e, r, :] + attn_part(e, 1, far.at[2 * layer + e, 0], low[e, r, :], i, layer)
            send[e, r, :] = total.astype(BF)

        crops(body, hooks)
        send_part(e, 2 * layer)
        if e == 0:
            start_save("proj", layer, proj_st)
            start_save("probs", layer, probs_st)
            start_save("mixed", layer, mixed_st)

    def ffn_own(e, layer, hooks):
        for copy in load_f(e, layer):
            copy.wait()
        part(e, 2 * layer).wait_recv()
        if e == 0:
            end_save("hidden", "v2", "active", "slope")

        def body(i):
            r = block(i)
            v = joined(e, 2 * layer, r)
            if e == 0:
                v_st[r, :] = v
            x = norm(v, gains[e][layer, 0:1, :], shifts[e][layer, 1:2, :])[2]
            x_low = x.astype(BF)
            low[e, r, :] = x_low
            base[e, r, :] = x + shifts[e][layer, 2:3, :]
            acc[e, r, :] = ffn_part(e, 0, own_f.at[e], x_low, i, layer)

        crops(body, hooks)
        if layer + 1 < LAYERS:
            for copy in load_f(e, layer + 1):
                copy.start()
        if e == 0:
            start_save("normed", layer, low.at[e])
            start_save("v1", layer, v_st)

    def ffn_far(e, layer, hooks):
        sent[e].wait_send()

        def body(i):
            r = block(i)
            total = acc[e, r, :] + ffn_part(
                e, 1, far.at[2 * layer + e, pl.ds(1, 2)], low[e, r, :], i, layer
            )
            send[e, r, :] = total.astype(BF)

        crops(body, hooks)
        send_part(e, 2 * layer + 1)
        if e == 0:
            start_save("active", layer, active_st)
            start_save("slope", layer, slope_st)

    def pool(e):
        part(e, 2 * LAYERS - 1).wait_recv()
        if e == 0:
            end_save("v1")

        def body(i):
            r = block(i)
            v = joined(e, 2 * LAYERS - 1, r)
            if e == 0:
                v_st[r, :] = v
            x = norm(v, gains[e][LAYERS - 1, 1:2, :], shifts[e][LAYERS - 1, 3:4, :])[2]
            visible = lax.broadcasted_iota(jnp.int32, (SEQ, 1), 0) < lengths[e][half * nc + i]
            sums[e, pl.ds(i, 1), :] = rows(jnp.where(visible, x, 0.0))

        crops(body, ())
        if e == 0:
            start_save("v2", LAYERS - 1, v_st)

    steps = {"AO": attn_own, "AF": attn_far, "FO": ffn_own, "FF": ffn_far}
    first_far = True
    for entry in PLAN:
        if len(entry) == 2:
            stage(*entry)
        else:
            if entry[0] == "AF" and first_far:
                b_copy.wait_recv()
                first_far = False
            steps[entry[0]](*entry[1:])
    pool(0)
    pool(1)
    contrast(dp_size, nc, d, half, bit_ids, count, lengths, sums, pair_out, grad_out, held, units, c_send, c_recv, remote)
    end_save(*saves)
    for copy in far_copies:
        copy.wait()
    for e in range(2):
        sent[e].wait_send()
        x_remote[e].wait_send()
    b_copy.wait_send()
    for made, _ in moves:
        for copy in made:
            copy.wait_send()


def greet(partners):
    barrier = pltpu.get_barrier_semaphore()
    for p in partners:
        pl.semaphore_signal(barrier, inc=1, device_id=p, device_id_type=MESH)
    pl.semaphore_wait(barrier, len(partners))


def contrast(
    dp_size, nc, d, half, bit_ids, count, lengths, sums, pair_out, grad_out, held, units, send, recv, remote
):
    dp_bits = dp_size.bit_length() - 1
    low = jnp.int32(0)
    for k in range(dp_bits):
        low = low + (((d >> (dp_bits - 1 - k)) & 1) << k)
    me = low + half * dp_size
    row = lax.broadcasted_iota(jnp.int32, (nc, 1), 0)

    def unit(e):
        length = jnp.zeros((nc, 1), jnp.int32)
        for r in range(nc):
            length = jnp.where(row == r, lengths[e][half * nc + r], length)
        inverse = 1.0 / length.astype(F32)
        pooled = sums[e, 0:nc, :] * inverse
        rate = lax.rsqrt(jnp.sum(pooled * pooled, axis=1, keepdims=True) + EPS)
        return pooled * rate, rate, inverse

    unit_q, rate_q, inv_q = unit(0)
    unit_k, _, _ = unit(1)
    units[half] = jnp.zeros((8, D), F32)
    units[half, 0:nc, :] = unit_q
    last = len(bit_ids)

    def swap_units(at):
        return remote(units.at[at], units.at[at], (send, recv), last, bit_ids[-1])

    swap_units(half).start()
    pieces = D // 128

    def piece(s):
        return s % 8, slice(128 * (s // 8), 128 * (s // 8) + 128)

    held[me] = jnp.zeros(held.shape[1:], F32)
    for r in range(nc):
        for c in range(pieces):
            at, lanes = piece(r * pieces + c)
            held[me, at : at + 1, lanes] = unit_k[r : r + 1, 128 * c : 128 * c + 128]
    flag_at, flag_lanes = piece(nc * pieces)
    lane = lax.broadcasted_iota(jnp.int32, (1, 128), 1)
    held[me, flag_at : flag_at + 1, flag_lanes] = jnp.where(
        (lane < nc) & (half * nc + lane < count[0]), 1.0, 0.0
    )
    for s, p in enumerate(bit_ids):
        mine = pl.ds((me >> s) << s, 1 << s)
        theirs = pl.ds(((me >> s) ^ 1) << s, 1 << s)
        remote(held.at[mine], held.at[mine], (send, recv), s, p).start()
        remote(held.at[theirs], held.at[theirs], (send, recv), s, p).wait_recv()
    swap_units(1 - half).wait_recv()
    for s, p in enumerate(bit_ids):
        mine = pl.ds((me >> s) << s, 1 << s)
        remote(held.at[mine], held.at[mine], (send, recv), s, p).wait_send()
    swap_units(half).wait_send()
    chips = held.shape[0]

    def gather(s):
        at, lanes = piece(s)
        return held[:, at, lanes]

    def exact(a, b, dims):
        return lax.dot_general(
            a, b, (dims, ((), ())), precision=lax.Precision.HIGHEST, preferred_element_type=F32
        )

    here = units[...].reshape(16, D)
    flags = gather(nc * pieces)
    row = lax.broadcasted_iota(jnp.int32, (16, 1), 0)
    chip = row // 8
    place = row % 8
    column = lax.broadcasted_iota(jnp.int32, (16, chips), 1)
    wide_lane = lax.broadcasted_iota(jnp.int32, (16, 128), 1)
    keys, logits, masked, own = [], [], [], []
    for r in range(nc):
        keys.append(jnp.concatenate([gather(r * pieces + c) for c in range(pieces)], axis=1))
        live = exact(jnp.where(wide_lane == r, 1.0, 0.0), flags, ((1,), (1,))) > 0.5
        logits.append(exact(here, keys[r], ((1,), (1,))) / TEMPER)
        masked.append(jnp.where(live, logits[r], FILL))
        own.append((column == low + chip * dp_size) & (place == r))

    def over_rows(parts, op, fold):
        return functools.reduce(op, [fold(v, axis=1, keepdims=True) for v in parts])

    highest = over_rows(masked, jnp.maximum, jnp.max)
    exps = [jnp.exp(v - highest) for v in masked]
    total = over_rows(exps, jnp.add, jnp.sum)
    live_here = (place < nc) & (chip * nc + place < count[0])
    own_logit = over_rows([jnp.where(o, v, 0.0) for o, v in zip(own, logits)], jnp.add, jnp.sum)
    value = jnp.where(live_here, highest + jnp.log(total) - own_logit, 0.0)
    pair_out[0:nc, :] = value[0:nc]
    pair_out[nc : 2 * nc, :] = value[8 : 8 + nc]
    g_unit = None
    for r in range(nc):
        weighting = jnp.where(live_here, exps[r] / total - own[r].astype(F32), 0.0) * (SEQ / TEMPER)
        term = exact(weighting, keys[r], ((1,), (0,)))
        g_unit = term if g_unit is None else g_unit + term
    g_unit = jnp.where(half == 0, g_unit[0:nc], g_unit[8 : 8 + nc])
    g_pooled = rate_q * (g_unit - unit_q * jnp.sum(unit_q * g_unit, axis=1, keepdims=True))
    grad_out[...] = g_pooled * inv_q


ROWS = D // 8
VEC_ROWS = 16
CODE_TOP = 32000.0
FIRST_SLOT = (0, 8, 12, 14)
BLOBS = (
    (1, 0, 0, 384, 'yxwz'),
    (1, 0, 384, 384, 'xwyz'),
    (1, 1, 0, 384, 'xyzw'),
    (1, 1, 384, 384, 'ywzx'),
    (1, 2, 0, 384, 'xyzw'),
    (1, 2, 384, 384, 'yzwx'),
    (0, 0, 0, 384, 'xyzw'),
    (0, 0, 384, 384, 'zxyw'),
    (0, 1, 0, 384, 'ywxz'),
    (0, 1, 384, 384, 'xyzw'),
    (0, 2, 0, 384, 'yzxw'),
    (0, 2, 384, 384, 'xyzw'),
)
BACK_PLAN = (
    ('FL', 1, ()),
    ('GD', 1, ()),
    ('FB', 1, ()),
    ('GI', 1, ()),
    ('AB', 1, ((0, 3, 0), (0, 2, 0))),
    ('AW', 1, ((0, 0, 0), (1, 1, 0))),
    ('FL', 0, ((1, 3, 1), (1, 2, 1))),
    ('GD', 0, ((1, 0, 1),)),
    ('FB', 0, ((1, 3, 2), (2, 5, 0), (2, 1, 1), (2, 2, 2))),
    ('GI', 0, ((1, 4, 0),)),
    ('AB', 0, ((0, 0, 2), (0, 5, 1), (1, 2, 3), (2, 1, 2), (2, 3, 3), (2, 8, 0), (2, 9, 0))),
    ('AW', 0, ((0, 4, 1), (1, -1, 0))),
    ("END", 0, ((0, 3), (9, 1), (1, 3), (7, 0), (6, 0), (5, 2), (4, 2), (9, 2), (8, 1), (-1, 1), (4, 3), (6, 1), (9, 3), (-1, 2), (7, 1), (5, 3), (10, 0), (11, 0), (6, 2), (8, 2), (7, 2), (-1, 3), (-1, 4), (10, 1), (11, 1), (8, 3), (6, 3), (10, 2), (7, 3), (11, 2), (10, 3), (11, 3))),
)
VEC_STAGES = 5


def backward(dp_size, nc, *refs):
    refs = list(refs)

    def take(n):
        return [refs.pop(0) for _ in range(n)]

    meta, g_sum = take(2)
    names = ("hidden", "proj", "probs", "mixed", "v1", "normed", "active", "slope", "v2")
    saves = dict(zip(names, take(9)))
    blob_a, w_in, w_down, far, gains = take(5)
    query_out, grads_out, vec_out = take(3)
    wf, wa, v_in, sl, act, nm, pj, pr, mx, low, base, part, got_part = take(13)
    temp, kept8, code8, kept4, code4, got, scale8, scale4, got_scale, bounds = take(10)
    vec, vec_got = take(2)
    load_sem, out_sem, p_send, p_recv, r_send, r_recv, s_send, s_recv, v_send, v_recv = take(10)

    d = lax.axis_index("dp")
    t = lax.axis_index("tensor")
    core = t & 1
    dp_bits = dp_size.bit_length() - 1
    spare = dp_bits - 3
    m = d >> spare
    share = query_out.shape[0]
    width = mx.shape[2]
    heads = width // HEAD
    far_id, core_id = (d, t ^ 2), (d, t ^ 1)
    bit_ids = [(d ^ (1 << k), t) for k in range(dp_bits)]
    top_ids = bit_ids[spare:]
    everyone = [far_id] + bit_ids + [core_id]
    greet(everyone)

    def remote(src, dst, send, recv, device):
        return pltpu.make_async_remote_copy(
            src_ref=src,
            dst_ref=dst,
            send_sem=send,
            recv_sem=recv,
            device_id=device,
            device_id_type=MESH,
        )

    def loads(name, layer):
        pairs = {
            "v1": [(saves["v1"].at[layer], v_in)],
            "v2": [(saves["v2"].at[layer], v_in)],
            "slope": [(saves["slope"].at[layer], sl)],
            "active": [(saves["active"].at[layer], act)],
            "normed": [(saves["normed"].at[layer], nm)],
            "hidden": [(saves["hidden"].at[layer], nm)],
            "proj": [(saves["proj"].at[layer], pj)],
            "probs": [(saves["probs"].at[layer], pr)],
            "mixed": [(saves["mixed"].at[layer], mx)],
            "wf": [
                (w_in.at[layer], wf.at[0, 0]),
                (w_down.at[layer], wf.at[0, 1]),
                (far.at[layer, pl.ds(1, 2)], wf.at[1]),
            ],
            "wa": [(blob_a.at[layer], wa.at[0]), (far.at[layer, 0], wa.at[1])],
        }[name]
        at = ("v1", "v2", "slope", "active", "normed", "hidden", "proj", "probs", "mixed", "wf", "wa").index(name)
        return [
            pltpu.make_async_copy(s, o, load_sem.at[at, k]) for k, (s, o) in enumerate(pairs)
        ]

    def load(layer, *which):
        for name in which:
            for copy in loads(name, layer):
                copy.start()

    def loaded(layer, *which):
        for name in which:
            for copy in loads(name, layer):
                copy.wait()

    top = LAYERS - 1
    load(top, "v2", "active", "wf", "slope", "normed", "probs", "proj", "wa", "mixed")
    vec[0] = jnp.zeros_like(vec[0])
    for tiles in (scale8, scale4, bounds):
        tiles[...] = jnp.zeros_like(tiles)

    def block(i):
        return pl.ds(pl.multiple_of(i * SEQ, SEQ), SEQ)

    def add_row(at, value):
        vec[0, pl.ds(at, 1), :] += value

    sent = []

    def exchange(k, slot):
        return remote(part, got_part.at[slot], p_send.at[k], p_recv.at[k], core_id)

    def send_part(k, slot):
        copy = exchange(k, slot)
        copy.start()
        sent.append(copy)

    def free_part():
        while sent:
            sent.pop().wait_send()

    bit_of = {"x": 0, "z": 1, "w": 2}

    def stage(blob, k):
        layer, kind, c0, cn, order = BLOBS[blob]
        device = far_id if order[k] == "y" else top_ids[bit_of[order[k]]]
        n = 8 >> k
        cols = pl.ds(c0, cn)
        codes, scales = (code8, scale8) if k == 0 else (code4, scale4)
        return (
            remote(
                codes.at[kind, pl.ds(0, n), :, cols],
                got.at[3 * layer + kind, pl.ds(FIRST_SLOT[k], n), :, cols],
                r_send.at[blob, k],
                r_recv.at[blob, k],
                device,
            ),
            remote(
                scales.at[blob],
                got_scale.at[blob, k],
                s_send.at[blob, k],
                s_recv.at[blob, k],
                device,
            ),
        ), n

    def groups(blob):
        c0, cn = BLOBS[blob][2:4]
        return [(g, slice(c0 + 128 * g, c0 + 128 * g + 128)) for g in range(cn // 128)]

    def encode(x, bound):
        return jnp.round(x * (CODE_TOP / bound)).astype(jnp.int32).astype(jnp.int16)

    def bound_row(blob, k, j, g):
        rest = BLOBS[blob][4][k + 1 :]
        if "y" not in rest:
            return g
        return 4 * ((j >> (len(rest) - 1 - rest.index("y"))) & 1) + g

    def decode(blob, k, j, g, lanes):
        layer, kind = BLOBS[blob][:2]
        code = got[3 * layer + kind, FIRST_SLOT[k] + j, :, lanes]
        bound = got_scale[blob, k, pl.ds(bound_row(blob, k, j, g), 1), :]
        return code.astype(jnp.int32).astype(F32) * (bound * (1.0 / CODE_TOP)), bound

    def place(order, s, j, flag):
        rest = order[1:]
        free = [link for link in rest if link != "y"]
        r = 0 if order[0] == "y" else flag << bit_of[order[0]]
        slot = 0
        for at, link in enumerate(rest):
            if link == "y":
                bit = s
            else:
                bit = (j >> (len(free) - 1 - free.index(link))) & 1
                r = r | (bit << bit_of[link])
            slot = slot | (bit << (2 - at))
        return r, slot

    def chunk(r, lanes):
        return temp[pl.ds(pl.multiple_of((r ^ m) * ROWS, 16), ROWS), lanes]

    def loop(n, body):
        lax.fori_loop(0, n, lambda i, _: (body(i), 0)[1], 0)

    def blobs_of(layer, kind):
        return [b for b, entry in enumerate(BLOBS) if entry[:2] == (layer, kind)]

    def largest():
        return jnp.maximum(jnp.max(jnp.abs(temp[...]), axis=0, keepdims=True), 1e-30)

    def split(blob, s, bound):
        kind, order = BLOBS[blob][1], BLOBS[blob][4]

        def keep(j):
            r, slot = place(order, s, j, 0)
            for g, lanes in groups(blob):
                kept8[kind, slot, :, lanes] = chunk(r, lanes)

        def code(j):
            r, slot = place(order, s, j, 1)
            for g, lanes in groups(blob):
                code8[kind, slot, :, lanes] = encode(chunk(r, lanes), bound[:, lanes])

        def both(j):
            code(j)
            keep(j)

        first = order[0] == "y"
        for g, lanes in groups(blob):
            if s == 1 or not first:
                at = g if first else 4 * s + g
                scale8[blob, at : at + 1, :] = bound[:, lanes]
            if s == 0 or not first:
                bounds[blob, 4 * s + g : 4 * s + g + 1, :] = bound[:, lanes]
        if first:
            loop(8, code if s == 1 else keep)
        else:
            loop(4, both)

    def start_stage(blob, k):
        for copy in stage(blob, k)[0]:
            copy.start()

    def end_stage(blob, k):
        for copy in stage(blob, k)[0]:
            copy.wait_send()

    def out_copy(blob):
        layer, kind, c0, cn, _ = BLOBS[blob]
        cols = pl.ds(c0, cn)
        return pltpu.make_async_copy(
            kept4.at[kind, 3, :, cols], grads_out.at[3 * layer + kind, :, cols], out_sem.at[1 + blob]
        )

    going_out = []

    def receive(blob, k):
        if blob < 0:
            vec_next(k)
            return
        layer, kind = BLOBS[blob][:2]
        copies, n = stage(blob, k)
        for copy in copies:
            copy.wait_recv()
        kept = kept8 if k == 0 else kept4
        half = n // 2
        if k == 0:
            for other in [b for b in going_out if BLOBS[b][1] == kind]:
                out_copy(other).wait()
                going_out.remove(other)
        else:
            end_stage(blob, k)
        if half:

            def send_on(j):
                for g, lanes in groups(blob):
                    value, bound = decode(blob, k, half + j, g, lanes)
                    bound = bound + bounds[blob, pl.ds(bound_row(blob, k, half + j, g), 1), :]
                    code4[kind, j, :, lanes] = encode(kept[kind, half + j, :, lanes] + value, bound)
                    scale4[blob, pl.ds(bound_row(blob, k + 1, j, g), 1), :] = bound

            loop(half, send_on)
            start_stage(blob, k + 1)

            def stay(j):
                for g, lanes in groups(blob):
                    value, _ = decode(blob, k, j, g, lanes)
                    kept4[kind, j, :, lanes] = kept[kind, j, :, lanes] + value

            loop(half, stay)
            bounds[blob] = bounds[blob] + got_scale[blob, k]
            if k == 0:
                end_stage(blob, 0)
        else:
            for g, lanes in groups(blob):
                kept4[kind, 3, :, lanes] = kept[kind, 0, :, lanes] + decode(blob, k, 0, g, lanes)[0]
            out_copy(blob).start()
            going_out.append(blob)

    def crops(body, hooks):
        def step(i, _):
            body(i)
            for c in range(nc - 1):
                due = [h[1:] for h in hooks if h[0] == c]
                if due:

                    @pl.when(i == c)
                    def _():
                        for blob, k in due:
                            receive(blob, k)

            return 0

        lax.fori_loop(0, nc, step, 0)

    def after(hooks, c):
        for at, blob, k in hooks:
            if at == c:
                receive(blob, k)

    def ffn_norm(layer, hooks):
        is_top = layer == top
        loaded(layer, "v2")
        if not is_top:
            exchange(2 * (top - layer) - 1, 1).wait_recv()
        at = VEC_ROWS * layer

        def body(i):
            r = block(i)
            if is_top:
                visible = lax.broadcasted_iota(jnp.int32, (SEQ, 1), 0) < meta[(t // 2) * nc + i]
                g = jnp.where(visible, g_sum[pl.ds(i, 1), :], 0.0)
            else:
                g = base[r, :] + got_part[1, r, :].astype(F32)
            gain = gains[layer, 1:2, :]
            xh, rate, _ = norm(v_in[r, :], gain, 0.0)
            gc = norm_back(g, xh, rate, gain)
            add_row(at + 1, rows(g * xh))
            add_row(at + 5, rows(g))
            add_row(at + 4, rows(gc))
            low[r, :] = gc.astype(BF)
            base[r, :] = gc

        crops(body, hooks)
        load(layer, "v1")
        after(hooks, nc - 1)

    def ffn_back(layer, hooks):
        loaded(layer, "slope", "wf")
        free_part()
        at = VEC_ROWS * layer

        def body(i):
            r = block(i)
            g_low = low[r, :]
            total = None
            for s in range(2):
                inner = (mm_nt(g_low, wf[s, 1]) * sl[s, r, :].astype(F32)).astype(BF)
                sl[s, r, :] = inner
                add_row(at + 6 + (t ^ (2 * s)), rows(inner.astype(F32)))
                term = mm_nt(inner, wf[s, 0])
                total = term if total is None else total + term
            base[r, :] += total
            part[r, :] = total.astype(BF)

        crops(body, hooks)
        send_part(2 * (top - layer), 0)
        if layer > 0:
            load(layer - 1, "wf")
        after(hooks, nc - 1)

    def ffn_grads(layer, kind, left, right, hooks):
        for s in (1, 0):
            temp[...] = mm_tn(left[...], right[s])
            bound = largest()
            for blob in blobs_of(layer, kind):
                split(blob, s, bound)
                if s == (BLOBS[blob][4][0] == "y"):
                    start_stage(blob, 0)
            if s == 1:
                after(hooks, 0)

    def outer_grads(layer, hooks):
        loaded(layer, "active")
        ffn_grads(layer, 1, low, act, hooks)
        if layer > 0:
            load(layer - 1, "active")
        after(hooks, 1)

    def inner_grads(layer, hooks):
        loaded(layer, "normed")
        ffn_grads(layer, 0, nm, sl, hooks)
        load(layer, "hidden")
        if layer > 0:
            load(layer - 1, "slope")
        after(hooks, 1)

    def attn_back(layer, hooks):
        loaded(layer, "v1", "proj", "probs", "wa")
        exchange(2 * (top - layer), 0).wait_recv()
        free_part()
        at = VEC_ROWS * layer

        def body(i):
            r = block(i)
            g = base[r, :] + got_part[0, r, :].astype(F32)
            gain = gains[layer, 0:1, :]
            xh, rate, _ = norm(v_in[r, :], gain, 0.0)
            gr = norm_back(g, xh, rate, gain)
            add_row(at, rows(g * xh))
            add_row(at + 3, rows(g))
            add_row(at + 2, rows(gr))
            g_low = gr.astype(BF)
            low[r, :] = g_low
            total = None
            for s in range(2):
                g_mixed = mm_nt(g_low, wa[s, 3 * width : 4 * width, :]).astype(BF)
                here = pj[s, r, :]
                parts = [[], [], []]
                for h in range(heads):
                    queries = here[:, h * HEAD : (h + 1) * HEAD]
                    keys = here[:, width + h * HEAD : width + (h + 1) * HEAD]
                    values = here[:, 2 * width + h * HEAD : 2 * width + (h + 1) * HEAD]
                    gm = g_mixed[:, h * HEAD : (h + 1) * HEAD]
                    p_low = pr[s, i, h]
                    p = p_low.astype(F32)
                    gp = mm_nt(values, gm)
                    gs = (p * (gp - jnp.sum(p * gp, axis=0, keepdims=True))).astype(BF)
                    parts[0].append((mm_tn(gs, keys) * SCALE).astype(BF))
                    parts[1].append((mm(gs, queries) * SCALE).astype(BF))
                    parts[2].append(mm(p_low, gm).astype(BF))
                g_proj = jnp.concatenate(parts[0] + parts[1] + parts[2], axis=1)
                pj[s, r, :] = g_proj
                vec[0, pl.ds(at + 10 + (t ^ (2 * s)), 1), 0 : 3 * width] += rows(g_proj.astype(F32))
                term = mm(g_proj, wa[s, 0 : 3 * width, :])
                total = term if total is None else total + term
            base[r, :] = gr + total
            part[r, :] = total.astype(BF)

        crops(body, hooks)
        send_part(2 * (top - layer) + 1, 1)
        if layer > 0:
            load(layer - 1, "v2", "probs", "wa")
        else:
            first = (lax.broadcasted_iota(jnp.int32, vec.shape[1:], 0) % VEC_ROWS >= 6) | (core == 0)
            vec[0] = jnp.where(first, vec[0], 0.0)
            vec_start(0)
        after(hooks, nc - 1)

    def attn_grads(layer, hooks):
        loaded(layer, "hidden", "mixed")
        for s in (1, 0):
            temp[:, 0 : 3 * width] = mm_tn(nm[...], pj[s])
            temp[:, 3 * width : 4 * width] = mm_tn(low[...], mx[s])
            bound = largest()
            for blob in blobs_of(layer, 2):
                split(blob, s, bound)
                if s == (BLOBS[blob][4][0] == "y"):
                    start_stage(blob, 0)
            if s == 0 and layer > 0:
                load(layer - 1, "proj", "mixed", "normed")
            after(hooks, 1 - s)

    def vec_copy(s):
        return remote(vec.at[0], vec_got.at[s], v_send.at[s], v_recv.at[s], everyone[s])

    def vec_start(s):
        vec_copy(s).start()

    def vec_next(s):
        vec_copy(s).wait()
        vec[0] = vec[0] + vec_got[s]
        if s + 1 < len(everyone):
            vec_start(s + 1)

    steps = {
        "FL": ffn_norm,
        "GD": outer_grads,
        "FB": ffn_back,
        "GI": inner_grads,
        "AB": attn_back,
        "AW": attn_grads,
    }
    for name, layer, hooks in BACK_PLAN:
        if name == "END":
            break
        steps[name](layer, hooks)
    exchange(2 * LAYERS - 1, 1).wait_recv()
    mine = pl.ds(pl.multiple_of(core * share, 16), share)
    v_in[0:share, :] = base[mine, :] + got_part[1, mine, :].astype(F32)
    query_copy = pltpu.make_async_copy(v_in.at[0:share], query_out, out_sem.at[0])
    query_copy.start()
    for blob, k in BACK_PLAN[-1][2]:
        receive(blob, k)
    for s in range(VEC_STAGES, len(everyone)):
        vec_next(s)
    query_copy.wait()
    for blob in going_out:
        out_copy(blob).wait()
    vec_out[...] = vec[0]
    free_part()


SMEM = pl.BlockSpec(memory_space=pltpu.SMEM)


def on_device(mesh_shape, *args):
    (
        query_input,
        key_input,
        query_length,
        key_length,
        pair_count,
    ) = args[:5]
    encoders = (args[5:13], args[13:21])
    dp_size = mesh_shape["dp"]
    dp_bits = dp_size.bit_length() - 1
    d_pos = lax.axis_index("dp")
    t_pos = lax.axis_index("tensor")
    quarter = d_pos & 3
    core = t_pos & 1
    half = t_pos // 2
    share = query_input.shape[0]
    total_rows = 2 * share
    nc = total_rows // SEQ
    width = args[5].shape[3]

    blob_a = [
        jnp.concatenate(
            [w[0].transpose(0, 2, 3, 1).reshape(LAYERS, 3 * width, D), w[2]], axis=1
        )
        for w in encoders
    ]
    big = (total_rows, D)
    heads = width // HEAD
    unit_flops = 2 * total_rows * D
    vmem = pl.BlockSpec(memory_space=pltpu.VMEM)
    hbm = pl.BlockSpec(memory_space=pl.ANY)
    hops = dp_bits + 1
    shaped = jax.ShapeDtypeStruct
    sem = pltpu.SemaphoreType.DMA
    rows_of = lambda *s: (LAYERS,) + s
    results = pl.pallas_call(
        functools.partial(forward, dp_size, nc),
        in_specs=[SMEM] * 3 + [hbm] * 8 + [vmem] * 8,
        out_specs=[hbm] * 10 + [vmem] * 2,
        out_shape=[
            shaped(rows_of(total_rows, D), BF),
            shaped(rows_of(2, total_rows, 3 * width), BF),
            shaped(rows_of(2, nc, heads, SEQ, SEQ), BF),
            shaped(rows_of(2, total_rows, width), BF),
            shaped(rows_of(total_rows, D), F32),
            shaped(rows_of(total_rows, D), BF),
            shaped(rows_of(2, total_rows, BLOB), BF),
            shaped(rows_of(2, total_rows, BLOB), BF),
            shaped(rows_of(total_rows, D), F32),
            shaped(rows_of(3, BLOB, D), BF),
            shaped((2 * nc, 1), F32),
            shaped((nc, D), F32),
        ],
        scratch_shapes=[
            pltpu.VMEM((2,) + big, BF),
            pltpu.VMEM((2,) + big, F32),
            pltpu.VMEM((2,) + big, F32),
            pltpu.VMEM((2,) + big, BF),
            pltpu.VMEM((2, 2) + big, BF),
            pltpu.VMEM((2, BLOB, D), BF),
            pltpu.VMEM((2, 2, BLOB, D), BF),
            pltpu.VMEM((2 * LAYERS, 3, BLOB, D), BF),
            pltpu.VMEM(big, F32),
            pltpu.VMEM((2, total_rows, 3 * width), BF),
            pltpu.VMEM((2, nc, heads, SEQ, SEQ), BF),
            pltpu.VMEM((2, total_rows, width), BF),
            pltpu.VMEM((2, total_rows, BLOB), BF),
            pltpu.VMEM((2, total_rows, BLOB), BF),
            pltpu.VMEM((8, D), F32),
            pltpu.VMEM((8, D), F32),
            pltpu.VMEM((2, 8, D), F32),
            pltpu.VMEM((2 * dp_size, 8, 384), F32),
            pltpu.VMEM((2, 8, D), F32),
            sem((len(GROUPS), 6)),
            sem((len(GROUPS), 6)),
            sem((2, 2 * LAYERS)),
            sem((2, 2 * LAYERS)),
            sem((2,)),
            sem((2,)),
            sem((2, 4)),
            sem((9 + 3 * LAYERS,)),
            sem((hops + 1,)),
            sem((hops + 1,)),
            sem((2,)),
        ],
        compiler_params=pltpu.CompilerParams(
            collective_id=0, has_side_effects=True, vmem_limit_bytes=62 * MIB
        ),
        cost_estimate=pl.CostEstimate(
            flops=unit_flops * 80 * BLOB // 4, bytes_accessed=100 * MIB, transcendentals=0
        ),
        name="forward",
    )(
        query_length,
        key_length,
        pair_count,
        query_input,
        key_input,
        *blob_a,
        encoders[0][3],
        encoders[1][3],
        encoders[0][5],
        encoders[1][5],
        encoders[0][6],
        encoders[1][6],
        encoders[0][7],
        encoders[1][7],
        encoders[0][1],
        encoders[1][1],
        encoders[0][4],
        encoders[1][4],
    )
    far, pair_rows, g_sum = results[9:]
    per_pair = pair_rows.reshape(2 * nc)

    n_peers = dp_bits + 2
    mat = (BLOB, D)
    blobs = 3 * LAYERS
    query_grad, grads, summed = pl.pallas_call(
        functools.partial(backward, dp_size, nc),
        in_specs=[SMEM, vmem] + [hbm] * 13 + [vmem],
        out_specs=[hbm, hbm, vmem],
        out_shape=[
            shaped((share, D), F32),
            shaped((blobs, ROWS, BLOB), F32),
            shaped((LAYERS * VEC_ROWS, D), F32),
        ],
        scratch_shapes=[
            pltpu.VMEM((2, 2) + mat, BF),
            pltpu.VMEM((2,) + mat, BF),
            pltpu.VMEM(big, F32),
            pltpu.VMEM((2, total_rows, BLOB), BF),
            pltpu.VMEM((2, total_rows, BLOB), BF),
            pltpu.VMEM(big, BF),
            pltpu.VMEM((2, total_rows, 3 * width), BF),
            pltpu.VMEM((2, nc, heads, SEQ, SEQ), BF),
            pltpu.VMEM((2, total_rows, width), BF),
            pltpu.VMEM(big, BF),
            pltpu.VMEM(big, F32),
            pltpu.VMEM(big, BF),
            pltpu.VMEM((2,) + big, BF),
            pltpu.VMEM((D, BLOB), F32),
            pltpu.VMEM((3, 8, ROWS, BLOB), F32),
            pltpu.VMEM((3, 8, ROWS, BLOB), jnp.int16),
            pltpu.VMEM((3, 4, ROWS, BLOB), F32),
            pltpu.VMEM((3, 4, ROWS, BLOB), jnp.int16),
            pltpu.VMEM((blobs, 15, ROWS, BLOB), jnp.int16),
            pltpu.VMEM((len(BLOBS), 8, 128), F32),
            pltpu.VMEM((len(BLOBS), 8, 128), F32),
            pltpu.VMEM((len(BLOBS), 4, 8, 128), F32),
            pltpu.VMEM((len(BLOBS), 8, 128), F32),
            pltpu.VMEM((1, LAYERS * VEC_ROWS, D), F32),
            pltpu.VMEM((n_peers, LAYERS * VEC_ROWS, D), F32),
            sem((11, 3)),
            sem((1 + len(BLOBS),)),
            sem((2 * LAYERS,)),
            sem((2 * LAYERS,)),
            sem((len(BLOBS), 4)),
            sem((len(BLOBS), 4)),
            sem((len(BLOBS), 4)),
            sem((len(BLOBS), 4)),
            sem((n_peers,)),
            sem((n_peers,)),
        ],
        compiler_params=pltpu.CompilerParams(
            collective_id=1, has_side_effects=True, vmem_limit_bytes=int(62.5 * MIB)
        ),
        cost_estimate=pl.CostEstimate(
            flops=unit_flops * 40 * BLOB // 2, bytes_accessed=60 * MIB, transcendentals=0
        ),
        name="backward",
    )(query_length, g_sum, *results[:9], blob_a[0], encoders[0][3], encoders[0][5], far, encoders[0][6])

    rows_left = ROWS
    for bit in reversed(range(dp_bits - 3)):
        rows_left //= 2
        pair = grads.reshape(blobs, 2, rows_left, BLOB)
        mine = (d_pos >> bit) & 1
        send = lax.dynamic_index_in_dim(pair, 1 - mine, 1, keepdims=False)
        grads = lax.dynamic_index_in_dim(pair, mine, 1, keepdims=False) + lax.ppermute(
            send, "dp", [(i, i ^ (1 << bit)) for i in range(dp_size)]
        )
    grads = grads.reshape(LAYERS, 3, D // dp_size, BLOB)
    grad_in, grad_down, attn = grads[:, 0], grads[:, 1], grads[:, 2]
    summed = summed.reshape(LAYERS, VEC_ROWS, D)
    qv = summed[:, 10:14].reshape(LAYERS, 4, 4, width)
    grad_qv_bias = jnp.stack(
        [qv[:, :, 0].reshape(LAYERS, 4 * width), qv[:, :, 2].reshape(LAYERS, 4 * width)], axis=1
    )
    return (
        per_pair,
        query_grad,
        attn[:, :, : 3 * width].reshape(LAYERS, D // dp_size, 3, width),
        attn[:, :, 3 * width :].transpose(0, 2, 1),
        grad_in,
        grad_down.transpose(0, 2, 1),
        grad_qv_bias,
        summed[:, 6:10].reshape(LAYERS, 4 * BLOB),
        summed[:, 0:2],
        summed[:, 2:6],
    )


def solution(mesh):
    split = P(("dp", "tensor"), None)
    weights = (
        P(None, None, None, "tensor"),
        P(None, None, "tensor"),
        P(None, "tensor", None),
        P(None, None, "tensor"),
        P(None, "tensor"),
        P(None, "tensor", None),
        P(),
        P(),
    )
    return jax.shard_map(
        functools.partial(on_device, dict(mesh.shape)),
        mesh=mesh,
        in_specs=(split, split, P("dp"), P("dp"), P("dp")) + weights + weights,
        out_specs=(
            P("dp"),
            split,
            P(None, "dp", None, "tensor"),
            P(None, "tensor", "dp"),
            P(None, "dp", "tensor"),
            P(None, "tensor", "dp"),
            P(),
            P(),
            P(),
            P(),
        ),
        check_vma=False,
    )
```

```python
import functools
import math

import jax
import jax.numpy as jnp
from jax import lax
from jax.experimental import pallas as pl
from jax.experimental.pallas import tpu as pltpu
from jax.sharding import PartitionSpec as P

D = 768
HEAD = 64
SEQ = 256
LAYERS = 2
BLOB = 768
EPS = 1e-06
TEMPER = 0.05
FILL = -1e30
BF = jnp.bfloat16
F32 = jnp.float32
MESH = pl.DeviceIdType.MESH
SCALE = HEAD ** (-0.5)
MIB = 2**20


def mm(a, b):
    return jnp.dot(a, b, preferred_element_type=F32)


def mm_nt(a, b):
    return lax.dot_general(a, b, (((1,), (1,)), ((), ())), preferred_element_type=F32)


def mm_tn(a, b):
    return lax.dot_general(a, b, (((0,), (0,)), ((), ())), preferred_element_type=F32)


def norm(v, gain, shift):
    center = v - jnp.mean(v, axis=-1, keepdims=True)
    rate = lax.rsqrt(jnp.mean(center * center, axis=-1, keepdims=True) + EPS)
    xhat = center * rate
    return xhat, rate, xhat * gain + shift


def norm_back(g, xhat, rate, gain):
    gx = g * gain
    return rate * (
        gx
        - jnp.mean(gx, axis=-1, keepdims=True)
        - xhat * jnp.mean(gx * xhat, axis=-1, keepdims=True)
    )


def rows(v):
    return jnp.sum(v, axis=0, keepdims=True)


PLAN = (
    ('AO', 0, 0, ()),
    ('AO', 1, 0, ((1, 1, 0),)),
    (1, 1),
    (2, 0),
    (1, 2),
    (2, 1),
    (3, 0),
    ('AF', 0, 0, ((1, 1, 3), (2, 2, 2))),
    (3, 1),
    ('AF', 1, 0, ((1, 1, 4), (2, 2, 3))),
    ('FO', 0, 0, ((2, 1, 5),)),
    ('FO', 1, 0, ((1, 2, 4),)),
    (3, 2),
    (3, 3),
    ('FF', 0, 0, ((0, 1, 6),)),
    (2, 5),
    (3, 4),
    (1, 7),
    (2, 6),
    (3, 5),
    ('FF', 1, 0, ((1, 1, 8),)),
    ('AO', 0, 1, ((0, 2, 7), (2, 1, 9))),
    ('AO', 1, 1, ((1, 2, 8),)),
    (3, 6),
    ('AF', 0, 1, ((0, 1, 10), (2, 2, 9))),
    (3, 7),
    ('AF', 1, 1, ((1, 1, 11),)),
    ('FO', 0, 1, ((0, 2, 10),)),
    ('FO', 1, 1, ((1, 2, 11),)),
    (3, 8),
    (3, 9),
    ('FF', 0, 1, ()),
    (3, 10),
    (3, 11),
    ('FF', 1, 1, ()),
)
GROUPS = (
    (0, 0, 0),
    (0, 1, 0),
    (0, 0, 1),
    (0, 0, 2),
    (0, 1, 1),
    (0, 1, 2),
    (1, 0, 0),
    (1, 1, 0),
    (1, 0, 1),
    (1, 0, 2),
    (1, 1, 1),
    (1, 1, 2),
)
T_DELAY = 2


def forward(dp_size, nc, *refs):
    refs = list(refs)

    def take(n):
        return [refs.pop(0) for _ in range(n)]

    lengths = take(2)
    (count,) = take(1)
    x_in, blob_a, w_in, w_down, gains, shifts = [take(2) for _ in range(6)]
    qv_bias, in_bias = take(2), take(2)
    saves = dict(
        zip(("hidden", "proj", "probs", "mixed", "v1", "normed", "active", "slope", "v2"), take(9))
    )
    far_out, pair_out, grad_out = take(3)
    low, base, acc, send, recv, own_a, own_f, far = take(8)
    v_st, proj_st, probs_st, mixed_st, active_st, slope_st = take(6)
    bias, far_bias, sums, held, units = take(5)
    y_send, y_recv, p_send, p_recv, x_send, x_recv, own_sem, save_sem, c_send, c_recv, b_sem = take(11)

    d = lax.axis_index("dp")
    t = lax.axis_index("tensor")
    core = t & 1
    half = t // 2
    q = d & 3
    share = x_in[0].shape[0]
    far_id, core_id, x_id, z_id = (d, t ^ 2), (d, t ^ 1), (d ^ 1, t), (d ^ 2, t)
    dp_bits = dp_size.bit_length() - 1
    bit_ids = [(d ^ (1 << k), t) for k in reversed(range(dp_bits))] + [far_id]
    greet(bit_ids + [core_id])

    def remote(src, dst, sems, at, device):
        return pltpu.make_async_remote_copy(
            src_ref=src,
            dst_ref=dst,
            send_sem=sems[0].at[at],
            recv_sem=sems[1].at[at],
            device_id=device,
            device_id_type=MESH,
        )

    mine = pl.ds(pl.multiple_of(core * share, 16), share)
    x_local = []
    x_remote = []
    for e in range(2):
        x_local.append(pltpu.make_async_copy(x_in[e], low.at[e, mine], own_sem.at[e, 2]))
        x_remote.append(remote(x_in[e], low.at[e, mine], (x_send, x_recv), e, core_id))

    def load_a(e, layer):
        return [pltpu.make_async_copy(blob_a[e].at[layer], own_a.at[e], own_sem.at[e, 0])]

    def load_f(e, layer):
        return [
            pltpu.make_async_copy(w_in[e].at[layer], own_f.at[e, 0], own_sem.at[e, 1]),
            pltpu.make_async_copy(w_down[e].at[layer], own_f.at[e, 1], own_sem.at[e, 3]),
        ]

    x_local[0].start()
    x_remote[0].start()
    for copy in load_a(0, 0):
        copy.start()
    bias[...] = jnp.zeros_like(bias)
    part_width = proj_st.shape[2] // 3
    for e in range(2):
        for layer in range(LAYERS):
            for c, at in ((0, 0), (1, 2 * part_width)):
                bias[e * 4 + layer : e * 4 + layer + 1, at : at + part_width] = qv_bias[e][layer, c : c + 1, :]
            bias[e * 4 + 2 + layer : e * 4 + 3 + layer, :] = in_bias[e][layer : layer + 1, :]
    b_copy = pltpu.make_async_remote_copy(
        src_ref=bias,
        dst_ref=far_bias,
        send_sem=b_sem.at[0],
        recv_sem=b_sem.at[1],
        device_id=far_id,
        device_id_type=MESH,
    )
    b_copy.start()
    x_local[1].start()
    x_remote[1].start()
    for copy in load_a(1, 0) + load_f(0, 0) + load_f(1, 0):
        copy.start()

    n = BLOB // 4
    third = n // 3
    moves = []
    for g, (layer, e, which) in enumerate(GROUPS):

        def at(quarter, start, size):
            row = pl.ds(pl.multiple_of(quarter * n + start, 16), size)
            return far.at[layer * 2 + e, which, row]

        def source(quarter, size):
            row = pl.ds(pl.multiple_of(quarter * n, 16), size)
            return (blob_a, w_in, w_down)[which][e].at[layer, row]

        def move(src, dst, k, device):
            return remote(src, dst, (y_send, y_recv), (g, k), device)

        made = (
            move(source(q, n), at(q, 0, n), 0, far_id),
            move(source(q ^ 3, third), at(q ^ 3, 0, third), 1, far_id),
            move(at(q, 0, n), at(q, 0, n), 2, x_id),
            move(at(q, 0, n), at(q, 0, n), 3, z_id),
            move(at(q ^ 2, third, third), at(q ^ 2, third, third), 4, x_id),
            move(at(q ^ 1, 2 * third, third), at(q ^ 1, 2 * third, third), 5, z_id),
        )
        got = made[:2] + (
            move(at(q ^ 1, 0, n), at(q ^ 1, 0, n), 2, x_id),
            move(at(q ^ 2, 0, n), at(q ^ 2, 0, n), 3, z_id),
            move(at(q ^ 3, third, third), at(q ^ 3, third, third), 4, x_id),
            move(at(q ^ 3, 2 * third, third), at(q ^ 3, 2 * third, third), 5, z_id),
        )
        moves.append((made, got))

    for g in range(len(GROUPS) + T_DELAY):
        if g < len(GROUPS):
            moves[g][0][0].start()
        if g >= T_DELAY:
            moves[g - T_DELAY][0][1].start()

    def stage(k, g):
        made, got = moves[g]
        if k == 1:
            got[0].wait_recv()
            made[2].start()
            made[3].start()
        elif k == 2:
            got[2].wait_recv()
            got[3].wait_recv()
            made[4].start()
            made[5].start()
        else:
            got[1].wait_recv()
            got[4].wait_recv()
            got[5].wait_recv()
            layer, e, which = GROUPS[g]
            if e == 0:
                copy = pltpu.make_async_copy(
                    far.at[2 * layer, which], far_out.at[layer, which], save_sem.at[9 + 3 * layer + which]
                )
                copy.start()
                far_copies.append(copy)

    far_copies = []

    def save(name, layer, src, k):
        return pltpu.make_async_copy(src, saves[name].at[layer], save_sem.at[k])

    pending = {}

    def start_save(name, layer, src):
        k = list(saves).index(name)
        copy = save(name, layer, src, k)
        copy.start()
        pending[name] = copy

    def end_save(*names):
        for name in names:
            if name in pending:
                pending.pop(name).wait()

    def block(i):
        return pl.ds(pl.multiple_of(i * SEQ, SEQ), SEQ)

    def part(e, k):
        return remote(send.at[e], recv.at[e, k % 2], (p_send.at[e], p_recv.at[e]), k, core_id)

    sent = {}

    def send_part(e, k):
        sent[e] = part(e, k)
        sent[e].start()

    width = proj_st.shape[2] // 3
    heads = width // HEAD

    def attn_part(e, s, w, x_low, i, layer):
        b = (bias, far_bias)[s]
        r = block(i)
        proj = (mm_nt(x_low, w[: 3 * width, :]) + b[e * 4 + layer : e * 4 + layer + 1, : 3 * width]).astype(BF)
        visible = lax.broadcasted_iota(jnp.int32, (SEQ, 1), 0) < lengths[e][half * nc + i]
        mixed = []
        for h in range(heads):
            queries = proj[:, h * HEAD : (h + 1) * HEAD]
            keys = proj[:, width + h * HEAD : width + (h + 1) * HEAD]
            values = proj[:, 2 * width + h * HEAD : 2 * width + (h + 1) * HEAD]
            scores = jnp.where(visible, mm_nt(keys, queries) * SCALE, FILL)
            ex = jnp.exp(scores - jnp.max(scores, axis=0, keepdims=True))
            probs = (ex * (1.0 / jnp.sum(ex, axis=0, keepdims=True))).astype(BF)
            if e == 0:
                probs_st[s, i, h] = probs
            mixed.append(mm_tn(probs, values).astype(BF))
        mixed = jnp.concatenate(mixed, axis=1)
        if e == 0:
            proj_st[s, r, :] = proj
            mixed_st[s, r, :] = mixed
        return mm(mixed, w[3 * width : 4 * width, :])

    def ffn_part(e, s, w, x_low, i, layer):
        b = (bias, far_bias)[s]
        r = block(i)
        u = mm(x_low, w[0]) + b[e * 4 + 2 + layer : e * 4 + 3 + layer, :]
        portion = 0.5 + 0.5 * lax.erf(u * (0.5**0.5))
        active = (u * portion).astype(BF)
        if e == 0:
            active_st[s, r, :] = active
            slope_st[s, r, :] = (
                portion + u * (jnp.exp(-0.5 * u * u) * ((2 * math.pi) ** -0.5))
            ).astype(BF)
        return mm(active, w[1])

    def crops(body, hooks):
        def step(i, _):
            body(i)
            for c in range(nc - 1):
                due = [h[1:] for h in hooks if h[0] == c]
                if due:

                    @pl.when(i == c)
                    def _():
                        for k, g in due:
                            stage(k, g)

            return 0

        lax.fori_loop(0, nc, step, 0)
        for c, k, g in hooks:
            if c >= nc - 1:
                stage(k, g)

    def joined(e, k, r):
        return base[e, r, :] + (send[e, r, :].astype(F32) + recv[e, k % 2, r, :].astype(F32))

    def attn_own(e, layer, hooks):
        for copy in load_a(e, layer):
            copy.wait()
        if layer == 0:
            x_local[e].wait()
            x_remote[e].wait_recv()
        else:
            part(e, 2 * layer - 1).wait_recv()
        if e == 0:
            end_save("v1", "normed", "proj", "probs", "mixed")

        def body(i):
            r = block(i)
            if layer == 0:
                x_low = low[e, r, :]
                x = x_low.astype(F32)
            else:
                v = joined(e, 2 * layer - 1, r)
                if e == 0:
                    v_st[r, :] = v
                x = norm(v, gains[e][layer - 1, 1:2, :], shifts[e][layer - 1, 3:4, :])[2]
                x_low = x.astype(BF)
                low[e, r, :] = x_low
            base[e, r, :] = x + shifts[e][layer, 0:1, :]
            acc[e, r, :] = attn_part(e, 0, own_a.at[e], x_low, i, layer)

        crops(body, hooks)
        if layer + 1 < LAYERS:
            for copy in load_a(e, layer + 1):
                copy.start()
        if e == 0:
            start_save("hidden", layer, low.at[e])
            if layer > 0:
                start_save("v2", layer - 1, v_st)

    def attn_far(e, layer, hooks):
        if e in sent:
            sent[e].wait_send()

        def body(i):
            r = block(i)
            total = acc[e, r, :] + attn_part(e, 1, far.at[2 * layer + e, 0], low[e, r, :], i, layer)
            send[e, r, :] = total.astype(BF)

        crops(body, hooks)
        send_part(e, 2 * layer)
        if e == 0:
            start_save("proj", layer, proj_st)
            start_save("probs", layer, probs_st)
            start_save("mixed", layer, mixed_st)

    def ffn_own(e, layer, hooks):
        for copy in load_f(e, layer):
            copy.wait()
        part(e, 2 * layer).wait_recv()
        if e == 0:
            end_save("hidden", "v2", "active", "slope")

        def body(i):
            r = block(i)
            v = joined(e, 2 * layer, r)
            if e == 0:
                v_st[r, :] = v
            x = norm(v, gains[e][layer, 0:1, :], shifts[e][layer, 1:2, :])[2]
            x_low = x.astype(BF)
            low[e, r, :] = x_low
            base[e, r, :] = x + shifts[e][layer, 2:3, :]
            acc[e, r, :] = ffn_part(e, 0, own_f.at[e], x_low, i, layer)

        crops(body, hooks)
        if layer + 1 < LAYERS:
            for copy in load_f(e, layer + 1):
                copy.start()
        if e == 0:
            start_save("normed", layer, low.at[e])
            start_save("v1", layer, v_st)

    def ffn_far(e, layer, hooks):
        sent[e].wait_send()

        def body(i):
            r = block(i)
            total = acc[e, r, :] + ffn_part(
                e, 1, far.at[2 * layer + e, pl.ds(1, 2)], low[e, r, :], i, layer
            )
            send[e, r, :] = total.astype(BF)

        crops(body, hooks)
        send_part(e, 2 * layer + 1)
        if e == 0:
            start_save("active", layer, active_st)
            start_save("slope", layer, slope_st)

    def pool(e):
        part(e, 2 * LAYERS - 1).wait_recv()
        if e == 0:
            end_save("v1")

        def body(i):
            r = block(i)
            v = joined(e, 2 * LAYERS - 1, r)
            if e == 0:
                v_st[r, :] = v
            x = norm(v, gains[e][LAYERS - 1, 1:2, :], shifts[e][LAYERS - 1, 3:4, :])[2]
            visible = lax.broadcasted_iota(jnp.int32, (SEQ, 1), 0) < lengths[e][half * nc + i]
            sums[e, pl.ds(i, 1), :] = rows(jnp.where(visible, x, 0.0))

        crops(body, ())
        if e == 0:
            start_save("v2", LAYERS - 1, v_st)

    steps = {"AO": attn_own, "AF": attn_far, "FO": ffn_own, "FF": ffn_far}
    first_far = True
    for entry in PLAN:
        if len(entry) == 2:
            stage(*entry)
        else:
            if entry[0] == "AF" and first_far:
                b_copy.wait_recv()
                first_far = False
            steps[entry[0]](*entry[1:])
    pool(0)
    pool(1)
    contrast(dp_size, nc, d, half, bit_ids, count, lengths, sums, pair_out, grad_out, held, units, c_send, c_recv, remote)
    end_save(*saves)
    for copy in far_copies:
        copy.wait()
    for e in range(2):
        sent[e].wait_send()
        x_remote[e].wait_send()
    b_copy.wait_send()
    for made, _ in moves:
        for copy in made:
            copy.wait_send()


def greet(partners):
    barrier = pltpu.get_barrier_semaphore()
    for p in partners:
        pl.semaphore_signal(barrier, inc=1, device_id=p, device_id_type=MESH)
    pl.semaphore_wait(barrier, len(partners))


def contrast(
    dp_size, nc, d, half, bit_ids, count, lengths, sums, pair_out, grad_out, held, units, send, recv, remote
):
    dp_bits = dp_size.bit_length() - 1
    low = jnp.int32(0)
    for k in range(dp_bits):
        low = low + (((d >> (dp_bits - 1 - k)) & 1) << k)
    me = low + half * dp_size
    row = lax.broadcasted_iota(jnp.int32, (nc, 1), 0)

    def unit(e):
        length = jnp.zeros((nc, 1), jnp.int32)
        for r in range(nc):
            length = jnp.where(row == r, lengths[e][half * nc + r], length)
        inverse = 1.0 / length.astype(F32)
        pooled = sums[e, 0:nc, :] * inverse
        rate = lax.rsqrt(jnp.sum(pooled * pooled, axis=1, keepdims=True) + EPS)
        return pooled * rate, rate, inverse

    unit_q, rate_q, inv_q = unit(0)
    unit_k, _, _ = unit(1)
    units[half] = jnp.zeros((8, D), F32)
    units[half, 0:nc, :] = unit_q
    last = len(bit_ids)

    def swap_units(at):
        return remote(units.at[at], units.at[at], (send, recv), last, bit_ids[-1])

    swap_units(half).start()
    pieces = D // 128

    def piece(s):
        return s % 8, slice(128 * (s // 8), 128 * (s // 8) + 128)

    held[me] = jnp.zeros(held.shape[1:], F32)
    for r in range(nc):
        for c in range(pieces):
            at, lanes = piece(r * pieces + c)
            held[me, at : at + 1, lanes] = unit_k[r : r + 1, 128 * c : 128 * c + 128]
    flag_at, flag_lanes = piece(nc * pieces)
    lane = lax.broadcasted_iota(jnp.int32, (1, 128), 1)
    held[me, flag_at : flag_at + 1, flag_lanes] = jnp.where(
        (lane < nc) & (half * nc + lane < count[0]), 1.0, 0.0
    )
    for s, p in enumerate(bit_ids):
        mine = pl.ds((me >> s) << s, 1 << s)
        theirs = pl.ds(((me >> s) ^ 1) << s, 1 << s)
        remote(held.at[mine], held.at[mine], (send, recv), s, p).start()
        remote(held.at[theirs], held.at[theirs], (send, recv), s, p).wait_recv()
    swap_units(1 - half).wait_recv()
    for s, p in enumerate(bit_ids):
        mine = pl.ds((me >> s) << s, 1 << s)
        remote(held.at[mine], held.at[mine], (send, recv), s, p).wait_send()
    swap_units(half).wait_send()
    chips = held.shape[0]

    def gather(s):
        at, lanes = piece(s)
        return held[:, at, lanes]

    def exact(a, b, dims):
        return lax.dot_general(
            a, b, (dims, ((), ())), precision=lax.Precision.HIGHEST, preferred_element_type=F32
        )

    here = units[...].reshape(16, D)
    flags = gather(nc * pieces)
    row = lax.broadcasted_iota(jnp.int32, (16, 1), 0)
    chip = row // 8
    place = row % 8
    column = lax.broadcasted_iota(jnp.int32, (16, chips), 1)
    wide_lane = lax.broadcasted_iota(jnp.int32, (16, 128), 1)
    keys, logits, masked, own = [], [], [], []
    for r in range(nc):
        keys.append(jnp.concatenate([gather(r * pieces + c) for c in range(pieces)], axis=1))
        live = exact(jnp.where(wide_lane == r, 1.0, 0.0), flags, ((1,), (1,))) > 0.5
        logits.append(exact(here, keys[r], ((1,), (1,))) / TEMPER)
        masked.append(jnp.where(live, logits[r], FILL))
        own.append((column == low + chip * dp_size) & (place == r))

    def over_rows(parts, op, fold):
        return functools.reduce(op, [fold(v, axis=1, keepdims=True) for v in parts])

    highest = over_rows(masked, jnp.maximum, jnp.max)
    exps = [jnp.exp(v - highest) for v in masked]
    total = over_rows(exps, jnp.add, jnp.sum)
    live_here = (place < nc) & (chip * nc + place < count[0])
    own_logit = over_rows([jnp.where(o, v, 0.0) for o, v in zip(own, logits)], jnp.add, jnp.sum)
    value = jnp.where(live_here, highest + jnp.log(total) - own_logit, 0.0)
    pair_out[0:nc, :] = value[0:nc]
    pair_out[nc : 2 * nc, :] = value[8 : 8 + nc]
    g_unit = None
    for r in range(nc):
        weighting = jnp.where(live_here, exps[r] / total - own[r].astype(F32), 0.0) * (SEQ / TEMPER)
        term = exact(weighting, keys[r], ((1,), (0,)))
        g_unit = term if g_unit is None else g_unit + term
    g_unit = jnp.where(half == 0, g_unit[0:nc], g_unit[8 : 8 + nc])
    g_pooled = rate_q * (g_unit - unit_q * jnp.sum(unit_q * g_unit, axis=1, keepdims=True))
    grad_out[...] = g_pooled * inv_q


ROWS = D // 8
VEC_ROWS = 16
CODE_TOP = 32000.0
FIRST_SLOT = (0, 8, 12, 14)
BLOBS = (
    (1, 0, 0, 384, 'ywzx'),
    (1, 0, 384, 384, 'xyzw'),
    (1, 1, 0, 384, 'yzxw'),
    (1, 1, 384, 384, 'xyzw'),
    (1, 2, 0, 384, 'xzwy'),
    (1, 2, 384, 384, 'xyzw'),
    (0, 0, 0, 384, 'yzwx'),
    (0, 0, 384, 384, 'zxyw'),
    (0, 1, 0, 384, 'yxwz'),
    (0, 1, 384, 384, 'xyzw'),
    (0, 2, 0, 384, 'yxzw'),
    (0, 2, 384, 384, 'xywz'),
)
BACK_PLAN = (
    ('FL', 1, ()),
    ('GD', 1, ()),
    ('FB', 1, ()),
    ('GI', 1, ()),
    ('AB', 1, ((0, 2, 0), (0, 3, 0))),
    ('AW', 1, ((0, 2, 1), (0, 0, 0), (1, 1, 0))),
    ('FL', 0, ((2, 3, 1),)),
    ('GD', 0, ((0, 2, 2),)),
    ('FB', 0, ((0, 1, 1), (0, 3, 2), (2, 0, 1))),
    ('GI', 0, ((0, 4, 0), (0, 2, 3), (0, 1, 2))),
    ('AB', 0, ((0, 3, 3), (0, 8, 0), (0, 0, 2), (1, 5, 0), (1, 4, 1), (2, 1, 3))),
    ('AW', 0, ()),
    ("END", 0, ((9, 0), (5, 1), (-1, 0), (8, 1), (0, 3), (6, 0), (7, 0), (5, 2), (4, 2), (8, 2), (6, 1), (9, 1), (5, 3), (8, 3), (-1, 1), (4, 3), (10, 0), (11, 0), (9, 2), (6, 2), (7, 1), (-1, 2), (11, 1), (9, 3), (10, 1), (7, 2), (6, 3), (-1, 3), (-1, 4), (10, 2), (11, 2), (7, 3), (10, 3), (11, 3))),
)
VEC_STAGES = 5


def backward(dp_size, nc, *refs):
    refs = list(refs)

    def take(n):
        return [refs.pop(0) for _ in range(n)]

    meta, g_sum = take(2)
    names = ("hidden", "proj", "probs", "mixed", "v1", "normed", "active", "slope", "v2")
    saves = dict(zip(names, take(9)))
    blob_a, w_in, w_down, far, gains = take(5)
    query_out, *grads_out, vec_out = take(5)
    wf, wa, v_in, sl, act, nm, pj, pr, mx, low, base, part, got_part = take(13)
    temp, kept8, code8, kept4, code4, got, scale8, scale4, got_scale, bounds = take(10)
    vec, vec_got = take(2)
    load_sem, out_sem, p_send, p_recv, r_send, r_recv, s_send, s_recv, v_send, v_recv = take(10)

    d = lax.axis_index("dp")
    t = lax.axis_index("tensor")
    core = t & 1
    dp_bits = dp_size.bit_length() - 1
    spare = dp_bits - 3
    m = d >> spare
    share = query_out.shape[0]
    width = mx.shape[2]
    heads = width // HEAD
    far_id, core_id = (d, t ^ 2), (d, t ^ 1)
    bit_ids = [(d ^ (1 << k), t) for k in range(dp_bits)]
    top_ids = bit_ids[spare:]
    everyone = [far_id] + bit_ids + [core_id]
    greet(everyone)

    def remote(src, dst, send, recv, device):
        return pltpu.make_async_remote_copy(
            src_ref=src,
            dst_ref=dst,
            send_sem=send,
            recv_sem=recv,
            device_id=device,
            device_id_type=MESH,
        )

    def loads(name, layer):
        pairs = {
            "v1": [(saves["v1"].at[layer], v_in)],
            "v2": [(saves["v2"].at[layer], v_in)],
            "slope": [(saves["slope"].at[layer], sl)],
            "active": [(saves["active"].at[layer], act)],
            "normed": [(saves["normed"].at[layer], nm)],
            "hidden": [(saves["hidden"].at[layer], nm)],
            "proj": [(saves["proj"].at[layer], pj)],
            "probs": [(saves["probs"].at[layer], pr)],
            "mixed": [(saves["mixed"].at[layer], mx)],
            "wf": [
                (w_in.at[layer], wf.at[0, 0]),
                (w_down.at[layer], wf.at[0, 1]),
                (far.at[layer, pl.ds(1, 2)], wf.at[1]),
            ],
            "wa": [(blob_a.at[layer], wa.at[0]), (far.at[layer, 0], wa.at[1])],
        }[name]
        at = ("v1", "v2", "slope", "active", "normed", "hidden", "proj", "probs", "mixed", "wf", "wa").index(name)
        return [
            pltpu.make_async_copy(s, o, load_sem.at[at, k]) for k, (s, o) in enumerate(pairs)
        ]

    def load(layer, *which):
        for name in which:
            for copy in loads(name, layer):
                copy.start()

    def loaded(layer, *which):
        for name in which:
            for copy in loads(name, layer):
                copy.wait()

    top = LAYERS - 1
    load(top, "v2", "active", "wf", "slope", "normed", "probs", "proj", "wa", "mixed")
    vec[0] = jnp.zeros_like(vec[0])
    for tiles in (scale8, scale4, bounds):
        tiles[...] = jnp.zeros_like(tiles)

    def block(i):
        return pl.ds(pl.multiple_of(i * SEQ, SEQ), SEQ)

    def add_row(at, value):
        vec[0, pl.ds(at, 1), :] += value

    sent = []

    def exchange(k, slot):
        return remote(part, got_part.at[slot], p_send.at[k], p_recv.at[k], core_id)

    def send_part(k, slot):
        copy = exchange(k, slot)
        copy.start()
        sent.append(copy)

    def free_part():
        while sent:
            sent.pop().wait_send()

    bit_of = {"x": 0, "z": 1, "w": 2}

    def stage(blob, k):
        layer, kind, c0, cn, order = BLOBS[blob]
        device = far_id if order[k] == "y" else top_ids[bit_of[order[k]]]
        n = 8 >> k
        cols = pl.ds(c0, cn)
        codes, scales = (code8, scale8) if k == 0 else (code4, scale4)
        return (
            remote(
                codes.at[kind, pl.ds(0, n), :, cols],
                got.at[3 * layer + kind, pl.ds(FIRST_SLOT[k], n), :, cols],
                r_send.at[blob, k],
                r_recv.at[blob, k],
                device,
            ),
            remote(
                scales.at[blob],
                got_scale.at[blob, k],
                s_send.at[blob, k],
                s_recv.at[blob, k],
                device,
            ),
        ), n

    def groups(blob):
        c0, cn = BLOBS[blob][2:4]
        return [(g, slice(c0 + 128 * g, c0 + 128 * g + 128)) for g in range(cn // 128)]

    def encode(x, bound):
        return jnp.round(x * (CODE_TOP / bound)).astype(jnp.int32).astype(jnp.int16)

    def bound_row(blob, k, j, g):
        rest = BLOBS[blob][4][k + 1 :]
        if "y" not in rest:
            return g
        return 4 * ((j >> (len(rest) - 1 - rest.index("y"))) & 1) + g

    def decode(blob, k, j, g, lanes):
        layer, kind = BLOBS[blob][:2]
        code = got[3 * layer + kind, FIRST_SLOT[k] + j, :, lanes]
        bound = got_scale[blob, k, pl.ds(bound_row(blob, k, j, g), 1), :]
        return code.astype(jnp.int32).astype(F32) * (bound * (1.0 / CODE_TOP)), bound

    def place(order, s, j, flag):
        rest = order[1:]
        free = [link for link in rest if link != "y"]
        r = 0 if order[0] == "y" else flag << bit_of[order[0]]
        slot = 0
        for at, link in enumerate(rest):
            if link == "y":
                bit = s
            else:
                bit = (j >> (len(free) - 1 - free.index(link))) & 1
                r = r | (bit << bit_of[link])
            slot = slot | (bit << (2 - at))
        return r, slot

    def chunk(r, lanes):
        return temp[pl.ds(pl.multiple_of((r ^ m) * ROWS, 16), ROWS), lanes]

    def loop(n, body):
        lax.fori_loop(0, n, lambda i, _: (body(i), 0)[1], 0)

    def blobs_of(layer, kind):
        return [b for b, entry in enumerate(BLOBS) if entry[:2] == (layer, kind)]

    def largest():
        return jnp.maximum(jnp.max(jnp.abs(temp[...]), axis=0, keepdims=True), 1e-30)

    def split(blob, s, bound):
        kind, order = BLOBS[blob][1], BLOBS[blob][4]

        def keep(j):
            r, slot = place(order, s, j, 0)
            for g, lanes in groups(blob):
                kept8[kind, slot, :, lanes] = chunk(r, lanes)

        def code(j):
            r, slot = place(order, s, j, 1)
            for g, lanes in groups(blob):
                code8[kind, slot, :, lanes] = encode(chunk(r, lanes), bound[:, lanes])

        def both(j):
            code(j)
            keep(j)

        first = order[0] == "y"
        for g, lanes in groups(blob):
            if s == 1 or not first:
                at = g if first else 4 * s + g
                scale8[blob, at : at + 1, :] = bound[:, lanes]
            if s == 0 or not first:
                bounds[blob, 4 * s + g : 4 * s + g + 1, :] = bound[:, lanes]
        if first:
            loop(8, code if s == 1 else keep)
        else:
            loop(4, both)

    def start_stage(blob, k):
        for copy in stage(blob, k)[0]:
            copy.start()

    def end_stage(blob, k):
        for copy in stage(blob, k)[0]:
            copy.wait_send()

    def out_copy(blob):
        layer, kind, c0, cn, _ = BLOBS[blob]
        cols = pl.ds(c0, cn)
        return pltpu.make_async_copy(
            kept4.at[kind, 3, :, cols], grads_out[kind].at[layer, :, cols], out_sem.at[1 + blob]
        )

    going_out = []

    def receive(blob, k):
        if blob < 0:
            vec_next(k)
            return
        layer, kind = BLOBS[blob][:2]
        copies, n = stage(blob, k)
        for copy in copies:
            copy.wait_recv()
        kept = kept8 if k == 0 else kept4
        half = n // 2
        if k == 0:
            for other in [b for b in going_out if BLOBS[b][1] == kind]:
                out_copy(other).wait()
                going_out.remove(other)
        else:
            end_stage(blob, k)
        if half:

            def send_on(j):
                for g, lanes in groups(blob):
                    value, bound = decode(blob, k, half + j, g, lanes)
                    bound = bound + bounds[blob, pl.ds(bound_row(blob, k, half + j, g), 1), :]
                    code4[kind, j, :, lanes] = encode(kept[kind, half + j, :, lanes] + value, bound)
                    scale4[blob, pl.ds(bound_row(blob, k + 1, j, g), 1), :] = bound

            loop(half, send_on)
            start_stage(blob, k + 1)

            def stay(j):
                for g, lanes in groups(blob):
                    value, _ = decode(blob, k, j, g, lanes)
                    kept4[kind, j, :, lanes] = kept[kind, j, :, lanes] + value

            loop(half, stay)
            bounds[blob] = bounds[blob] + got_scale[blob, k]
            if k == 0:
                end_stage(blob, 0)
        else:
            for g, lanes in groups(blob):
                kept4[kind, 3, :, lanes] = kept[kind, 0, :, lanes] + decode(blob, k, 0, g, lanes)[0]
            out_copy(blob).start()
            going_out.append(blob)

    def crops(body, hooks):
        def step(i, _):
            body(i)
            for c in range(nc - 1):
                due = [h[1:] for h in hooks if h[0] == c]
                if due:

                    @pl.when(i == c)
                    def _():
                        for blob, k in due:
                            receive(blob, k)

            return 0

        lax.fori_loop(0, nc, step, 0)

    def after(hooks, c):
        for at, blob, k in hooks:
            if at == c:
                receive(blob, k)

    def ffn_norm(layer, hooks):
        is_top = layer == top
        loaded(layer, "v2")
        if not is_top:
            exchange(2 * (top - layer) - 1, 1).wait_recv()
        at = VEC_ROWS * layer

        def body(i):
            r = block(i)
            if is_top:
                visible = lax.broadcasted_iota(jnp.int32, (SEQ, 1), 0) < meta[(t // 2) * nc + i]
                g = jnp.where(visible, g_sum[pl.ds(i, 1), :], 0.0)
            else:
                g = base[r, :] + got_part[1, r, :].astype(F32)
            gain = gains[layer, 1:2, :]
            xh, rate, _ = norm(v_in[r, :], gain, 0.0)
            gc = norm_back(g, xh, rate, gain)
            add_row(at + 1, rows(g * xh))
            add_row(at + 5, rows(g))
            add_row(at + 4, rows(gc))
            low[r, :] = gc.astype(BF)
            base[r, :] = gc

        crops(body, hooks)
        load(layer, "v1")
        after(hooks, nc - 1)

    def ffn_back(layer, hooks):
        loaded(layer, "slope", "wf")
        free_part()
        at = VEC_ROWS * layer

        def body(i):
            r = block(i)
            g_low = low[r, :]
            total = None
            for s in range(2):
                inner = (mm_nt(g_low, wf[s, 1]) * sl[s, r, :].astype(F32)).astype(BF)
                sl[s, r, :] = inner
                add_row(at + 6 + (t ^ (2 * s)), rows(inner.astype(F32)))
                term = mm_nt(inner, wf[s, 0])
                total = term if total is None else total + term
            base[r, :] += total
            part[r, :] = total.astype(BF)

        crops(body, hooks)
        send_part(2 * (top - layer), 0)
        if layer > 0:
            load(layer - 1, "wf")
        after(hooks, nc - 1)

    def ffn_grads(layer, kind, left, right, hooks):
        for s in (1, 0):
            temp[...] = mm_tn(left[...], right[s])
            bound = largest()
            for blob in blobs_of(layer, kind):
                split(blob, s, bound)
                if s == (BLOBS[blob][4][0] == "y"):
                    start_stage(blob, 0)
            if s == 1:
                after(hooks, 0)

    def outer_grads(layer, hooks):
        loaded(layer, "active")
        ffn_grads(layer, 1, low, act, hooks)
        if layer > 0:
            load(layer - 1, "active")
        after(hooks, 1)

    def inner_grads(layer, hooks):
        loaded(layer, "normed")
        ffn_grads(layer, 0, nm, sl, hooks)
        load(layer, "hidden")
        if layer > 0:
            load(layer - 1, "slope")
        after(hooks, 1)

    def attn_back(layer, hooks):
        loaded(layer, "v1", "proj", "probs", "wa")
        exchange(2 * (top - layer), 0).wait_recv()
        free_part()
        at = VEC_ROWS * layer

        def body(i):
            r = block(i)
            g = base[r, :] + got_part[0, r, :].astype(F32)
            gain = gains[layer, 0:1, :]
            xh, rate, _ = norm(v_in[r, :], gain, 0.0)
            gr = norm_back(g, xh, rate, gain)
            add_row(at, rows(g * xh))
            add_row(at + 3, rows(g))
            add_row(at + 2, rows(gr))
            g_low = gr.astype(BF)
            low[r, :] = g_low
            total = None
            for s in range(2):
                g_mixed = mm_nt(g_low, wa[s, 3 * width : 4 * width, :]).astype(BF)
                here = pj[s, r, :]
                parts = [[], [], []]
                for h in range(heads):
                    queries = here[:, h * HEAD : (h + 1) * HEAD]
                    keys = here[:, width + h * HEAD : width + (h + 1) * HEAD]
                    values = here[:, 2 * width + h * HEAD : 2 * width + (h + 1) * HEAD]
                    gm = g_mixed[:, h * HEAD : (h + 1) * HEAD]
                    p_low = pr[s, i, h]
                    p = p_low.astype(F32)
                    gp = mm_nt(values, gm)
                    gs = (p * (gp - jnp.sum(p * gp, axis=0, keepdims=True))).astype(BF)
                    parts[0].append((mm_tn(gs, keys) * SCALE).astype(BF))
                    parts[1].append((mm(gs, queries) * SCALE).astype(BF))
                    parts[2].append(mm(p_low, gm).astype(BF))
                g_proj = jnp.concatenate(parts[0] + parts[1] + parts[2], axis=1)
                pj[s, r, :] = g_proj
                vec[0, pl.ds(at + 10 + (t ^ (2 * s)), 1), 0 : 3 * width] += rows(g_proj.astype(F32))
                term = mm(g_proj, wa[s, 0 : 3 * width, :])
                total = term if total is None else total + term
            base[r, :] = gr + total
            part[r, :] = total.astype(BF)

        crops(body, hooks)
        send_part(2 * (top - layer) + 1, 1)
        if layer > 0:
            load(layer - 1, "v2", "probs", "wa")
        else:
            first = (lax.broadcasted_iota(jnp.int32, vec.shape[1:], 0) % VEC_ROWS >= 6) | (core == 0)
            vec[0] = jnp.where(first, vec[0], 0.0)
            vec_start(0)
        after(hooks, nc - 1)

    def attn_grads(layer, hooks):
        loaded(layer, "hidden", "mixed")
        for s in (1, 0):
            temp[:, 0 : 3 * width] = mm_tn(nm[...], pj[s])
            temp[:, 3 * width : 4 * width] = mm_tn(low[...], mx[s])
            bound = largest()
            for blob in blobs_of(layer, 2):
                split(blob, s, bound)
                if s == (BLOBS[blob][4][0] == "y"):
                    start_stage(blob, 0)
            if s == 0 and layer > 0:
                load(layer - 1, "proj", "mixed", "normed")
            after(hooks, 1 - s)

    def vec_copy(s):
        return remote(vec.at[0], vec_got.at[s], v_send.at[s], v_recv.at[s], everyone[s])

    def vec_start(s):
        vec_copy(s).start()

    def vec_next(s):
        vec_copy(s).wait()
        vec[0] = vec[0] + vec_got[s]
        if s + 1 < len(everyone):
            vec_start(s + 1)

    steps = {
        "FL": ffn_norm,
        "GD": outer_grads,
        "FB": ffn_back,
        "GI": inner_grads,
        "AB": attn_back,
        "AW": attn_grads,
    }
    for name, layer, hooks in BACK_PLAN:
        if name == "END":
            break
        steps[name](layer, hooks)
    exchange(2 * LAYERS - 1, 1).wait_recv()
    mine = pl.ds(pl.multiple_of(core * share, 16), share)
    v_in[0:share, :] = base[mine, :] + got_part[1, mine, :].astype(F32)
    query_copy = pltpu.make_async_copy(v_in.at[0:share], query_out, out_sem.at[0])
    query_copy.start()
    for blob, k in BACK_PLAN[-1][2]:
        receive(blob, k)
    for s in range(VEC_STAGES, len(everyone)):
        vec_next(s)
    query_copy.wait()
    for blob in going_out:
        out_copy(blob).wait()
    vec_out[...] = vec[0]
    free_part()


SMEM = pl.BlockSpec(memory_space=pltpu.SMEM)


def on_device(mesh_shape, *args):
    (
        query_input,
        key_input,
        query_length,
        key_length,
        pair_count,
    ) = args[:5]
    encoders = (args[5:13], args[13:21])
    dp_size = mesh_shape["dp"]
    dp_bits = dp_size.bit_length() - 1
    d_pos = lax.axis_index("dp")
    t_pos = lax.axis_index("tensor")
    quarter = d_pos & 3
    core = t_pos & 1
    half = t_pos // 2
    share = query_input.shape[0]
    total_rows = 2 * share
    nc = total_rows // SEQ
    width = args[5].shape[3]

    blob_a = [
        jnp.concatenate(
            [w[0].transpose(0, 2, 3, 1).reshape(LAYERS, 3 * width, D), w[2]], axis=1
        )
        for w in encoders
    ]
    big = (total_rows, D)
    heads = width // HEAD
    unit_flops = 2 * total_rows * D
    vmem = pl.BlockSpec(memory_space=pltpu.VMEM)
    hbm = pl.BlockSpec(memory_space=pl.ANY)
    hops = dp_bits + 1
    shaped = jax.ShapeDtypeStruct
    sem = pltpu.SemaphoreType.DMA
    rows_of = lambda *s: (LAYERS,) + s
    results = pl.pallas_call(
        functools.partial(forward, dp_size, nc),
        in_specs=[SMEM] * 3 + [hbm] * 8 + [vmem] * 8,
        out_specs=[hbm] * 10 + [vmem] * 2,
        out_shape=[
            shaped(rows_of(total_rows, D), BF),
            shaped(rows_of(2, total_rows, 3 * width), BF),
            shaped(rows_of(2, nc, heads, SEQ, SEQ), BF),
            shaped(rows_of(2, total_rows, width), BF),
            shaped(rows_of(total_rows, D), F32),
            shaped(rows_of(total_rows, D), BF),
            shaped(rows_of(2, total_rows, BLOB), BF),
            shaped(rows_of(2, total_rows, BLOB), BF),
            shaped(rows_of(total_rows, D), F32),
            shaped(rows_of(3, BLOB, D), BF),
            shaped((2 * nc, 1), F32),
            shaped((nc, D), F32),
        ],
        scratch_shapes=[
            pltpu.VMEM((2,) + big, BF),
            pltpu.VMEM((2,) + big, F32),
            pltpu.VMEM((2,) + big, F32),
            pltpu.VMEM((2,) + big, BF),
            pltpu.VMEM((2, 2) + big, BF),
            pltpu.VMEM((2, BLOB, D), BF),
            pltpu.VMEM((2, 2, BLOB, D), BF),
            pltpu.VMEM((2 * LAYERS, 3, BLOB, D), BF),
            pltpu.VMEM(big, F32),
            pltpu.VMEM((2, total_rows, 3 * width), BF),
            pltpu.VMEM((2, nc, heads, SEQ, SEQ), BF),
            pltpu.VMEM((2, total_rows, width), BF),
            pltpu.VMEM((2, total_rows, BLOB), BF),
            pltpu.VMEM((2, total_rows, BLOB), BF),
            pltpu.VMEM((8, D), F32),
            pltpu.VMEM((8, D), F32),
            pltpu.VMEM((2, 8, D), F32),
            pltpu.VMEM((2 * dp_size, 8, 384), F32),
            pltpu.VMEM((2, 8, D), F32),
            sem((len(GROUPS), 6)),
            sem((len(GROUPS), 6)),
            sem((2, 2 * LAYERS)),
            sem((2, 2 * LAYERS)),
            sem((2,)),
            sem((2,)),
            sem((2, 4)),
            sem((9 + 3 * LAYERS,)),
            sem((hops + 1,)),
            sem((hops + 1,)),
            sem((2,)),
        ],
        compiler_params=pltpu.CompilerParams(
            collective_id=0, has_side_effects=True, vmem_limit_bytes=62 * MIB
        ),
        cost_estimate=pl.CostEstimate(
            flops=unit_flops * 80 * BLOB // 4, bytes_accessed=100 * MIB, transcendentals=0
        ),
        name="forward",
    )(
        query_length,
        key_length,
        pair_count,
        query_input,
        key_input,
        *blob_a,
        encoders[0][3],
        encoders[1][3],
        encoders[0][5],
        encoders[1][5],
        encoders[0][6],
        encoders[1][6],
        encoders[0][7],
        encoders[1][7],
        encoders[0][1],
        encoders[1][1],
        encoders[0][4],
        encoders[1][4],
    )
    far, pair_rows, g_sum = results[9:]
    per_pair = pair_rows.reshape(2 * nc)

    n_peers = dp_bits + 2
    mat = (BLOB, D)
    blobs = 3 * LAYERS
    query_grad, *grads, summed = pl.pallas_call(
        functools.partial(backward, dp_size, nc),
        in_specs=[SMEM, vmem] + [hbm] * 13 + [vmem],
        out_specs=[hbm] * 4 + [vmem],
        out_shape=[
            shaped((share, D), F32),
            *[shaped((LAYERS, ROWS, BLOB), F32)] * 3,
            shaped((LAYERS * VEC_ROWS, D), F32),
        ],
        scratch_shapes=[
            pltpu.VMEM((2, 2) + mat, BF),
            pltpu.VMEM((2,) + mat, BF),
            pltpu.VMEM(big, F32),
            pltpu.VMEM((2, total_rows, BLOB), BF),
            pltpu.VMEM((2, total_rows, BLOB), BF),
            pltpu.VMEM(big, BF),
            pltpu.VMEM((2, total_rows, 3 * width), BF),
            pltpu.VMEM((2, nc, heads, SEQ, SEQ), BF),
            pltpu.VMEM((2, total_rows, width), BF),
            pltpu.VMEM(big, BF),
            pltpu.VMEM(big, F32),
            pltpu.VMEM(big, BF),
            pltpu.VMEM((2,) + big, BF),
            pltpu.VMEM((D, BLOB), F32),
            pltpu.VMEM((3, 8, ROWS, BLOB), F32),
            pltpu.VMEM((3, 8, ROWS, BLOB), jnp.int16),
            pltpu.VMEM((3, 4, ROWS, BLOB), F32),
            pltpu.VMEM((3, 4, ROWS, BLOB), jnp.int16),
            pltpu.VMEM((blobs, 15, ROWS, BLOB), jnp.int16),
            pltpu.VMEM((len(BLOBS), 8, 128), F32),
            pltpu.VMEM((len(BLOBS), 8, 128), F32),
            pltpu.VMEM((len(BLOBS), 4, 8, 128), F32),
            pltpu.VMEM((len(BLOBS), 8, 128), F32),
            pltpu.VMEM((1, LAYERS * VEC_ROWS, D), F32),
            pltpu.VMEM((n_peers, LAYERS * VEC_ROWS, D), F32),
            sem((11, 3)),
            sem((1 + len(BLOBS),)),
            sem((2 * LAYERS,)),
            sem((2 * LAYERS,)),
            sem((len(BLOBS), 4)),
            sem((len(BLOBS), 4)),
            sem((len(BLOBS), 4)),
            sem((len(BLOBS), 4)),
            sem((n_peers,)),
            sem((n_peers,)),
        ],
        compiler_params=pltpu.CompilerParams(
            collective_id=1, has_side_effects=True, vmem_limit_bytes=int(62.5 * MIB)
        ),
        cost_estimate=pl.CostEstimate(
            flops=unit_flops * 40 * BLOB // 2, bytes_accessed=60 * MIB, transcendentals=0
        ),
        name="backward",
    )(query_length, g_sum, *results[:9], blob_a[0], encoders[0][3], encoders[0][5], far, encoders[0][6])

    rows_left = ROWS
    for bit in reversed(range(dp_bits - 3)):
        rows_left //= 2
        pairs = [g.reshape(LAYERS, 2, rows_left, BLOB) for g in grads]
        mine = (d_pos >> bit) & 1
        grads = [
            lax.dynamic_index_in_dim(pair, mine, 1, keepdims=False)
            + lax.ppermute(
                lax.dynamic_index_in_dim(pair, 1 - mine, 1, keepdims=False),
                "dp",
                [(i, i ^ (1 << bit)) for i in range(dp_size)],
            )
            for pair in pairs
        ]
    grad_in, grad_down, attn = grads
    summed = summed.reshape(LAYERS, VEC_ROWS, D)
    qv = summed[:, 10:14].reshape(LAYERS, 4, 4, width)
    grad_qv_bias = jnp.stack(
        [qv[:, :, 0].reshape(LAYERS, 4 * width), qv[:, :, 2].reshape(LAYERS, 4 * width)], axis=1
    )
    return (
        per_pair,
        query_grad,
        attn[:, :, : 3 * width].reshape(LAYERS, D // dp_size, 3, width),
        attn[:, :, 3 * width :].transpose(0, 2, 1),
        grad_in,
        grad_down.transpose(0, 2, 1),
        grad_qv_bias,
        summed[:, 6:10].reshape(LAYERS, 4 * BLOB),
        summed[:, 0:2],
        summed[:, 2:6],
    )


def solution(mesh):
    split = P(("dp", "tensor"), None)
    weights = (
        P(None, None, None, "tensor"),
        P(None, None, "tensor"),
        P(None, "tensor", None),
        P(None, None, "tensor"),
        P(None, "tensor"),
        P(None, "tensor", None),
        P(),
        P(),
    )
    return jax.shard_map(
        functools.partial(on_device, dict(mesh.shape)),
        mesh=mesh,
        in_specs=(split, split, P("dp"), P("dp"), P("dp")) + weights + weights,
        out_specs=(
            P("dp"),
            split,
            P(None, "dp", None, "tensor"),
            P(None, "tensor", "dp"),
            P(None, "dp", "tensor"),
            P(None, "tensor", "dp"),
            P(),
            P(),
            P(),
            P(),
        ),
        check_vma=False,
    )
```
